128 devices in a mesh: dp: 16 (over x_hi, z, core), seq: 8 (over y, x_lo).
Axes of the slice: x: 4 (x_hi: 2, x_lo: 2; x = x_hi * 2 + x_lo), y: 4, z: 4, core: 2. Of those that a mesh axis runs over, the one named last changes fastest.
Arguments:
- tokens: bfloat16 [16, 1024, 1024], P('dp', 'seq'), may hold values from -8 to 8
- memory: bfloat16 [16, 1024, 1024], P('dp', 'seq'), may hold values from -6 to 6
- cotangent: bfloat16 [16, 1024, 1024], P('dp', 'seq'), may hold values from -6 to 6
- offsets: int32 [16, 16], P('dp'), may hold values from 0 to 1023, as said below
- memory_ids: int32 [16, 1024], P('dp'), may hold values from 0 to 15, as said below
- pair_map: int32 [16, 16], P('dp'), may hold values from 0 to 15, as said below
- self_qkv: bfloat16 [1024, 3072], replicated, may hold values from -0.1875 to 0.1875
- self_out: bfloat16 [1024, 1024], replicated, may hold values from -1 to 1
- cross_query: bfloat16 [1024, 1024], replicated, may hold values from -0.1875 to 0.1875
- cross_kv: bfloat16 [1024, 2048], replicated, may hold values from -0.1875 to 0.1875
- cross_out: bfloat16 [1024, 1024], replicated, may hold values from -1 to 1
- expand_weight: bfloat16 [1024, 4096], replicated, may hold values from -0.1875 to 0.1875
- expand_bias: float32 [4096], replicated, may hold values from -1.75 to 1.75
- reduce_weight: bfloat16 [4096, 1024], replicated, may hold values from -0.09375 to 0.09375
- norm_gains: float32 [3, 1024], replicated, may hold values from 0.25 to 1.75
- bias_rows: float32 [10, 1024], replicated, may hold values from -1.75 to 1.75
Outputs:
- output: bfloat16 [16, 1024, 1024], P('dp', 'seq')
- grad_tokens: float32 [16, 1024, 1024], P('dp', 'seq')
- grad_memory: float32 [16, 1024, 1024], P('dp', 'seq')
- grad_self_qkv: float32 [1024, 3072], P('dp')
- grad_self_out: float32 [1024, 1024], P('dp')
- grad_cross_query: float32 [1024, 1024], P('dp')
- grad_cross_kv: float32 [1024, 2048], P('dp')
- grad_cross_out: float32 [1024, 1024], P('dp')
- grad_expand_weight: float32 [1024, 4096], P('dp')
- grad_expand_bias: float32 [4096], P('dp')
- grad_reduce_weight: float32 [4096, 1024], P('dp')
- grad_norm_gains: float32 [3, 1024], P(None, 'dp')
- grad_bias_rows: float32 [10, 1024], P(None, 'dp')
The draws below stay inside these ranges and needn't reach their ends.
Inputs may be any that keep to these rules, and one draw needn't show every extreme that they name: In each row the offsets start at 0 and rise strictly; target segment s covers the positions from offsets[s] up to the next offset minus one, the last up to 1023. `memory_ids`: along each row the ids never fall, and every id from 0 to 15 appears. `pair_map`: each row is a permutation of 0 to 15.
All inputs are finite; a program needn't handle non-finite values.
Results may differ from the reference program's by a relative error of at most 0.025.
Values may be sent and summed in bfloat16 or wider, within the bound.
A program may use at most 192 MiB of HBM per device.

```python
import jax
import jax.numpy as jnp
from jax import lax

D = 1024
HEADS = 16
HEAD_DIM = 64
FF = 4096
ROWS = 1
ROW_LEN = 1024
MEM_LEN = 1024
NSEG = 16
BATCH = 16
TOK_DEV = 128
MEM_DEV = 128


def row_starts(base_key, length, block_len, is_long, long_index):
    loose_key, head_key, tail_key = jax.random.split(base_key, 3)
    loose_cuts = jnp.sort(jax.random.permutation(loose_key, length - 1)[:NSEG - 1] + 1).astype(jnp.int32)
    places = jnp.arange(block_len - 1, dtype=jnp.int32)
    head_cuts = (jax.random.permutation(head_key, block_len - 1) + 1).astype(jnp.int32)
    tail_rest = (jax.random.permutation(tail_key, block_len - 2) + (length - block_len + 1)).astype(jnp.int32)
    tail_cuts = jnp.concatenate([jnp.full((1,), length - 1, jnp.int32), tail_rest])
    pooled = jnp.concatenate([jnp.where(places < long_index, head_cuts, length + 1), jnp.where(places < NSEG - 1 - long_index, tail_cuts, length + 1)])
    packed = jnp.sort(pooled)[:NSEG - 1].astype(jnp.int32)
    cut_points = jnp.where(is_long, packed, loose_cuts).astype(jnp.int32)
    return jnp.concatenate([jnp.zeros((1,), jnp.int32), cut_points])


def segment_plan(base_key):
    pair_key, pick_key, target_key, memory_key = jax.random.split(base_key, 4)
    pairing = jax.vmap(lambda one_key: jax.random.permutation(one_key, NSEG))(jax.random.split(pair_key, BATCH)).astype(jnp.int32)
    chosen = jax.random.randint(pick_key, (BATCH // ROWS,), 0, ROWS).astype(jnp.int32)
    row_index = jnp.arange(BATCH, dtype=jnp.int32)
    spanning = row_index % ROWS == chosen[row_index // ROWS]
    target_starts = jax.vmap(lambda one_key, is_long: row_starts(one_key, ROW_LEN, TOK_DEV, is_long, 0))(jax.random.split(target_key, BATCH), spanning)
    memory_starts = jax.vmap(lambda one_key, is_long, long_index: row_starts(one_key, MEM_LEN, MEM_DEV, is_long, long_index))(jax.random.split(memory_key, BATCH), spanning, pairing[:, 0])
    return (pairing, target_starts, memory_starts)


def draw_offsets(key, part):
    planned = segment_plan(key)
    return planned[1]


def draw_memory_ids(key, part):
    planned = segment_plan(key)
    places = jnp.arange(MEM_LEN, dtype=jnp.int32)
    memory_segs = jnp.sum((planned[2][:, None, :] <= places[None, :, None]).astype(jnp.int32), -1) - 1
    return memory_segs.astype(jnp.int32)


def draw_pair_map(key, part):
    planned = segment_plan(key)
    return planned[0]


def strengthened(array, key, source, target, parts, factor):
    owner, partner = [(jnp.arange(array.shape[position]) // (array.shape[position] // parts)).reshape([-1 if axis == position else 1 for axis in range(array.ndim)]) for position in (source, target)]
    chosen = jax.random.permutation(key, parts)[partner]
    strong = (owner == chosen) | (owner == (partner + parts // 2) % parts)
    return jnp.where(strong, factor * array, array)


def level_of(stream_key, dims, cuts, smallest, largest):
    factor_of, own = 1.0, jax.random.fold_in(stream_key, 6)
    for axis_at, parts in cuts:
        draws = jnp.exp(jax.random.uniform(jax.random.fold_in(own, axis_at), (parts,), jnp.float32, smallest / len(cuts), largest / len(cuts)))
        factor_of = factor_of * jnp.repeat(draws, dims[axis_at] // parts).reshape([-1 if axis == axis_at else 1 for axis in range(len(dims))])
    return factor_of


def centred(own_key, dims, width, limit, pieces=(), kind=jnp.bfloat16):
    drawn = width * jax.random.normal(own_key, dims, jnp.float32)
    if pieces:
        drawn = drawn * level_of(own_key, dims, pieces, -0.22, 0.18)
    return jnp.clip(drawn, -limit, limit).astype(kind)


def bell_draw_with(rng, shape, scale, reach, shards, heavy, kind=jnp.bfloat16):
    entries = scale * jax.random.normal(rng, shape, jnp.float32)
    if shards:
        entries = entries * level_of(rng, shape, shards, -0.22, 0.18)
    return jnp.clip(strengthened(entries, jax.random.fold_in(rng, 3), *heavy), -reach, reach).astype(kind)


def setup_inputs(seed: int = 0) -> dict:
    key_of = jax.random.split(jax.random.key(seed), 17)
    tokens = bell_draw_with(key_of[0], (BATCH, ROW_LEN, D), 1.0, 8.0, ((0, 16), (1, 8)), (0, 2, 16, 2.0))
    memory = centred(key_of[1], (BATCH, MEM_LEN, D), 1.0, 6.0, ((0, 16), (1, 8)))
    cotangent = centred(key_of[2], (BATCH, ROW_LEN, D), 1.0, 6.0, ((0, 16), (1, 8)))
    offsets = draw_offsets(jax.random.fold_in(key_of[16], 71), 0)
    memory_ids = draw_memory_ids(jax.random.fold_in(key_of[16], 71), 0)
    pair_map = draw_pair_map(jax.random.fold_in(key_of[16], 71), 0)
    self_qkv = centred(key_of[6], (D, 3 * D), D ** -0.5, 0.1875)
    self_out = centred(key_of[7], (D, D), (D // 32) ** -0.5, 1.0)
    cross_query = centred(key_of[8], (D, D), D ** -0.5, 0.1875)
    cross_kv = centred(key_of[9], (D, 2 * D), D ** -0.5, 0.1875)
    cross_out = centred(key_of[10], (D, D), (D // 32) ** -0.5, 1.0)
    expand_weight = centred(key_of[11], (D, FF), D ** -0.5, 0.1875)
    expand_bias = centred(key_of[12], (FF,), 0.3, 1.75, (), jnp.float32)
    reduce_weight = centred(key_of[13], (FF, D), FF ** -0.5, 0.09375)
    norm_gains = jnp.clip(1.0 + 0.15 * jax.random.normal(key_of[14], (3, D), jnp.float32), 0.25, 1.75)
    bias_rows = centred(key_of[15], (10, D), 0.3, 1.75, (), jnp.float32)
    return dict(tokens=tokens, memory=memory, cotangent=cotangent, offsets=offsets, memory_ids=memory_ids, pair_map=pair_map, self_qkv=self_qkv, self_out=self_out, cross_query=cross_query, cross_kv=cross_kv, cross_out=cross_out, expand_weight=expand_weight, expand_bias=expand_bias, reduce_weight=reduce_weight, norm_gains=norm_gains, bias_rows=bias_rows)


@jax.custom_vjp
def low(v):
    return lax.optimization_barrier(v.astype(jnp.bfloat16)).astype(jnp.float32)

@jax.custom_vjp
def low_back(v):
    return v

def low_keep(v):
    return (low(v), None)

def low_pass(kept, grad):
    return (grad,)

def back_keep(v):
    return (v, None)

def back_low(kept, grad):
    return (low(grad),)
low.defvjp(low_keep, low_pass)
low_back.defvjp(back_keep, back_low)
NEG_FILL = -1e+30
EPS = 1e-05
HIGH = lax.Precision.HIGHEST

def matmul(left_side, right_side):
    return jnp.dot(left_side, right_side, precision=HIGH)

def layer_norm(values, gain_row, shift_row):
    average = lax.optimization_barrier(jnp.mean(values, -1, keepdims=True))
    centered = values - average
    variance = lax.optimization_barrier(jnp.mean(centered * centered, -1, keepdims=True))
    return centered * lax.rsqrt(variance + EPS) * gain_row + shift_row

def attend(queries, key_rows, value_rows, allowed):
    length = queries.shape[0]
    query_heads = queries.reshape(length, HEADS, HEAD_DIM)
    key_heads = key_rows.reshape(key_rows.shape[0], HEADS, HEAD_DIM)
    value_heads = value_rows.reshape(value_rows.shape[0], HEADS, HEAD_DIM)
    scores = low_back(jnp.einsum('qhd,khd->hqk', query_heads, key_heads, precision=HIGH))
    masked = jnp.where(allowed[None], scores, NEG_FILL)
    row_max = lax.optimization_barrier(jnp.max(masked, -1, keepdims=True))
    exponent = jnp.exp(masked - row_max)
    weights_row = low(exponent / lax.optimization_barrier(jnp.sum(exponent, -1, keepdims=True)))
    mixture = jnp.einsum('hqk,khd->qhd', weights_row, value_heads, precision=HIGH)
    return mixture.reshape(length, HEADS * HEAD_DIM)

def decoder_layer(params, inputs, memory_row, self_allowed, cross_allowed):
    self_qkv, self_out, cross_query, cross_kv, cross_out, expand_weight, expand_bias, reduce_weight, norm_gains, bias_rows = params
    feature = inputs.shape[1]
    query_scale = HEAD_DIM ** (-0.5)
    normed = low(layer_norm(inputs, norm_gains[0], bias_rows[0]))
    joined_proj = matmul(normed, self_qkv)
    queries = low_back(low((joined_proj[:, :feature] + bias_rows[3]) * query_scale))
    key_rows = low_back(low(joined_proj[:, feature:2 * feature]))
    value_rows = low_back(low(joined_proj[:, 2 * feature:] + bias_rows[4]))
    mixture = low_back(low(jax.checkpoint(attend)(queries, key_rows, value_rows, self_allowed)))
    after_self = inputs + low_back(matmul(mixture, self_out) + bias_rows[5])
    normed = low(layer_norm(after_self, norm_gains[1], bias_rows[1]))
    queries = low_back(low((matmul(normed, cross_query) + bias_rows[6]) * query_scale))
    memory_proj = matmul(memory_row, cross_kv)
    key_rows = low_back(low(memory_proj[:, :feature]))
    value_rows = low_back(low(memory_proj[:, feature:] + bias_rows[7]))
    mixture = low_back(low(jax.checkpoint(attend)(queries, key_rows, value_rows, cross_allowed)))
    after_cross = after_self + low_back(matmul(mixture, cross_out) + bias_rows[8])
    normed = low(layer_norm(after_cross, norm_gains[2], bias_rows[2]))
    hidden = low_back(matmul(normed, expand_weight) + expand_bias)
    active = low(jax.nn.gelu(hidden))
    return after_cross + low_back(matmul(active, reduce_weight) + bias_rows[9])

def row_masks(offsets_row, memory_ids_row, pairing_row):
    places = jnp.arange(ROW_LEN, dtype=jnp.int32)
    target_segs = lax.optimization_barrier(jnp.sum((offsets_row[None, :] <= places[:, None]).astype(jnp.int32), -1)) - 1
    self_allowed = (target_segs[:, None] == target_segs[None, :]) & (places[None, :] <= places[:, None])
    pair_ids = jnp.arange(NSEG, dtype=jnp.int32)
    mapped = lax.optimization_barrier(jnp.sum(jnp.where(target_segs[:, None] == pair_ids[None, :], pairing_row[None, :], 0), -1))
    cross_allowed = memory_ids_row[None, :] == mapped[:, None]
    return (self_allowed, cross_allowed)

def reference(tokens, memory, cotangent, offsets, memory_ids, pair_map, self_qkv, self_out, cross_query, cross_kv, cross_out, expand_weight, expand_bias, reduce_weight, norm_gains, bias_rows):
    params = tuple((weight.astype(jnp.float32) for weight in (self_qkv, self_out, cross_query, cross_kv, cross_out, expand_weight, expand_bias, reduce_weight, norm_gains, bias_rows)))

    def one_row(totals, row_data):
        inputs, memory_row, cot_row, offsets_row, ids_row, pairing_row = row_data
        self_allowed, cross_allowed = row_masks(offsets_row, ids_row, pairing_row)

        def forward(weights, inputs_f, memory_f):
            return decoder_layer(weights, inputs_f, memory_f, self_allowed, cross_allowed)
        result, pullback = jax.vjp(forward, params, inputs.astype(jnp.float32), memory_row.astype(jnp.float32))
        param_grads, grad_in, grad_mem = pullback(cot_row.astype(jnp.float32))
        totals = tuple((total + part for total, part in zip(totals, param_grads)))
        return (totals, (result.astype(jnp.bfloat16), grad_in, grad_mem))
    zero_sums = tuple((jnp.zeros_like(weight) for weight in params))
    totals, (outputs, grad_in, grad_mem) = lax.scan(one_row, zero_sums, (tokens, memory, cotangent, offsets, memory_ids, pair_map))
    return (outputs, grad_in, grad_mem, totals[0], totals[1], totals[2], totals[3], totals[4], totals[5], totals[6], totals[7], totals[8], totals[9])
```

```python
import functools
import math

import jax
import jax.numpy as jnp
from jax import lax
from jax.experimental import pallas as pl
from jax.experimental.pallas import tpu as pltpu
from jax.sharding import PartitionSpec as P

HEADS = 16
HEAD_DIM = 64
WIDTH = 1024
TOK = 128
ROW = 1024
FF = 4096
SEQ = 8
DP = 16
PAIR = 128
NEG_FILL = -1e30
EPS = 1e-05
SCALE = HEAD_DIM ** (-0.5)
LOW = jnp.bfloat16
F32 = jnp.float32
MESH = pl.DeviceIdType.MESH
MIB = 2**20


def dot(left, right):
    return lax.dot_general(left, right, (((1,), (0,)), ((), ())), preferred_element_type=F32)


def dot_nt(left, right):
    return lax.dot_general(left, right, (((1,), (1,)), ((), ())), preferred_element_type=F32)


def dot_tn(left, right):
    return lax.dot_general(left, right, (((0,), (0,)), ((), ())), preferred_element_type=F32)


def norm_unit(values):
    average = jnp.mean(values, -1, keepdims=True)
    centered = values - average
    inverse = lax.rsqrt(jnp.mean(centered * centered, -1, keepdims=True) + EPS)
    return centered * inverse, inverse


def norm_back(incoming, unit, inverse, gain_row):
    scaled = incoming * gain_row
    return inverse * (
        scaled
        - jnp.mean(scaled, -1, keepdims=True)
        - unit * jnp.mean(scaled * unit, -1, keepdims=True)
    )


def column_sum(values):
    return jnp.sum(values, 0, keepdims=True)


def spec_any():
    return pl.BlockSpec(memory_space=pl.ANY)


def spec_vmem():
    return pl.BlockSpec(memory_space=pltpu.VMEM)


def spec_smem():
    return pl.BlockSpec(memory_space=pltpu.SMEM)


def local_call(kernel, outs, specs, scratch, name, flops, moved, vmem=48):
    return pl.pallas_call(
        kernel,
        out_shape=outs,
        in_specs=specs,
        out_specs=jax.tree.map(lambda _: spec_vmem(), outs),
        scratch_shapes=scratch,
        compiler_params=pltpu.CompilerParams(vmem_limit_bytes=vmem * MIB),
        cost_estimate=pl.CostEstimate(flops=flops, bytes_accessed=moved, transcendentals=0),
        name=name,
    )


def shaped(shape, kind=LOW):
    return jax.ShapeDtypeStruct(shape, kind)


def project_kernel(
    tok_ref, mem_ref, gain_ref, bias_ref, qkv_hbm, ckv_hbm, heads_ref, mem_heads_ref, n1_ref,
    qkv_ref, ckv_ref, sems,
):
    copies = []
    for step in range(4):
        for part in range(3):
            cols = pl.ds(part * WIDTH + step * 256, 256)
            copies.append(
                pltpu.make_async_copy(
                    qkv_hbm.at[:, cols], qkv_ref.at[:, cols], sems.at[step * 3 + part]
                )
            )
    for step in range(4):
        for part in range(2):
            cols = pl.ds(part * WIDTH + step * 256, 256)
            copies.append(
                pltpu.make_async_copy(
                    ckv_hbm.at[:, cols], ckv_ref.at[:, cols], sems.at[12 + step * 2 + part]
                )
            )
    for one in copies:
        one.start()
    unit, _ = norm_unit(tok_ref[...].astype(F32))
    n1 = (unit * gain_ref[0:1, :] + bias_ref[0:1, :]).astype(LOW)
    n1_ref[...] = n1
    for step in range(4):
        for part in range(3):
            copies[step * 3 + part].wait()
            cols = slice(part * WIDTH + step * 256, part * WIDTH + step * 256 + 256)
            own = slice(step * 256, step * 256 + 256)
            value = dot(n1, qkv_ref[:, cols])
            if part == 0:
                value = (value + bias_ref[3:4, own]) * SCALE
            elif part == 2:
                value = value + bias_ref[4:5, own]
            low = value.astype(LOW)
            heads_ref[2 * step, :, part * PAIR : part * PAIR + PAIR] = low[:, :PAIR]
            heads_ref[2 * step + 1, :, part * PAIR : part * PAIR + PAIR] = low[:, PAIR:]
    mem = mem_ref[...]
    for step in range(4):
        for part in range(2):
            copies[12 + step * 2 + part].wait()
            cols = slice(part * WIDTH + step * 256, part * WIDTH + step * 256 + 256)
            own = slice(step * 256, step * 256 + 256)
            value = dot(mem, ckv_ref[:, cols])
            if part == 1:
                value = value + bias_ref[7:8, own]
            low = value.astype(LOW)
            mem_heads_ref[2 * step, :, part * PAIR : part * PAIR + PAIR] = low[:, :PAIR]
            mem_heads_ref[2 * step + 1, :, part * PAIR : part * PAIR + PAIR] = low[:, PAIR:]


def head_lanes(rows):
    return lax.broadcasted_iota(jnp.int32, (rows, PAIR), 1) < HEAD_DIM


def pick_head(values, lanes, head):
    zero = jnp.zeros_like(values)
    return jnp.where(lanes, values, zero) if head == 0 else jnp.where(lanes, zero, values)


def attend_tile(query, key_t, value, allowed, exp_ref, rows, width):
    lanes = head_lanes(query.shape[0])
    mixed, inverses = [], []
    for head in range(2):
        scores = dot(pick_head(query, lanes, head), key_t)
        scores = jnp.where(allowed, scores, NEG_FILL)
        top = jnp.max(scores, -1, keepdims=True)
        exponent = jnp.exp(scores - top)
        inverse = 1.0 / jnp.sum(exponent, -1, keepdims=True)
        low = exponent.astype(LOW)
        exp_ref[head, rows, 0:width] = low
        mixed.append(dot(low, value))
        inverses.append(inverse)
    inverse = jnp.where(lanes, inverses[0], inverses[1])
    return jnp.where(lanes, mixed[0], mixed[1]) * inverse, inverse


def self_attend_kernel(heads_ref, offsets_ref, out_ref, exp_ref, inv_ref):
    key_t = heads_ref[:, PAIR : 2 * PAIR].T
    tile = 256
    for step in range(ROW // tile):
        rows = slice(step * tile, step * tile + tile)
        width = (step + 1) * tile
        places = lax.broadcasted_iota(jnp.int32, (tile, 1), 0) + step * tile
        begin = jnp.zeros((tile, 1), jnp.int32)
        for seg in range(1, 16):
            offset = offsets_ref[0, seg]
            begin = jnp.where(places >= offset, offset, begin)
        keys = lax.broadcasted_iota(jnp.int32, (tile, width), 1)
        allowed = (keys <= places) & (keys >= begin)
        mixture, inverse = attend_tile(
            heads_ref[rows, 0:PAIR], key_t[:, 0:width], heads_ref[0:width, 2 * PAIR : 3 * PAIR],
            allowed, exp_ref, rows, width,
        )
        out_ref[rows, :] = mixture.astype(LOW)
        inv_ref[rows, :] = inverse


def cross_attend_kernel(query_ref, kv_ref, ids_ref, offsets_ref, pair_ref, out_ref, exp_ref, inv_ref):
    key_t = kv_ref[:, 0:PAIR].T
    tile = 256
    ids = ids_ref[...]
    for step in range(ROW // tile):
        rows = slice(step * tile, step * tile + tile)
        places = lax.broadcasted_iota(jnp.int32, (tile, 1), 0) + step * tile
        reads = jnp.zeros((tile, 1), jnp.int32) + pair_ref[0, 0]
        for seg in range(1, 16):
            reads = jnp.where(places >= offsets_ref[0, seg], pair_ref[0, seg], reads)
        allowed = ids == reads
        mixture, inverse = attend_tile(
            query_ref[rows, :], key_t, kv_ref[:, PAIR : 2 * PAIR], allowed, exp_ref, rows, ROW
        )
        out_ref[rows, :] = mixture.astype(LOW)
        inv_ref[rows, :] = inverse


def attend_back(
    query, key_rows, value_rows, grad_ref, mix_ref, inv_ref, exp_ref, out_ref, dkt_ref, dvt_ref,
    causal,
):
    tile = 256
    scaled = (grad_ref[...].astype(F32) * inv_ref[...]).astype(LOW)
    lanes = head_lanes(ROW)
    product = scaled.astype(F32) * mix_ref[...].astype(F32)
    inner = [jnp.sum(pick_head(product, lanes, head), -1, keepdims=True) for head in range(2)]
    value_t = value_rows.T
    query_t = query.T
    scaled_t = scaled.T
    dkt_ref[...] = jnp.zeros_like(dkt_ref)
    dvt_ref[...] = jnp.zeros_like(dvt_ref)
    tile_lanes = head_lanes(tile)
    for step in range(ROW // tile):
        rows = slice(step * tile, step * tile + tile)
        width = (step + 1) * tile if causal else ROW
        parts = []
        for head in range(2):
            own = slice(head * HEAD_DIM, head * HEAD_DIM + HEAD_DIM)
            exponent = exp_ref[head, rows, 0:width]
            grad_p = dot(pick_head(scaled[rows, :], tile_lanes, head), value_t[:, 0:width])
            grad_s = (exponent.astype(F32) * (grad_p - inner[head][rows, :])).astype(LOW)
            parts.append(dot(grad_s, key_rows[0:width, :]))
            dkt_ref[own, 0:width] += dot(query_t[own, rows], grad_s)
            dvt_ref[own, 0:width] += dot(scaled_t[own, rows], exponent)
        grad_q = jnp.where(tile_lanes, parts[0], parts[1]).astype(LOW) * SCALE
        out_ref[rows, 0:PAIR] = grad_q.astype(LOW)
    out_ref[:, PAIR : 2 * PAIR] = dkt_ref[...].T.astype(LOW)
    out_ref[:, 2 * PAIR : 3 * PAIR] = dvt_ref[...].T.astype(LOW)


def cross_back_kernel(
    query_ref, kv_ref, grad_ref, mix_ref, inv_ref, exp_ref, full_ref, out_ref, weight_ref,
    dkt_ref, dvt_ref,
):
    attend_back(
        query_ref[...], kv_ref[:, 0:PAIR], kv_ref[:, PAIR : 2 * PAIR], grad_ref, mix_ref, inv_ref,
        exp_ref, out_ref, dkt_ref, dvt_ref, False,
    )
    full = full_ref[...]
    weight_ref[:, 0:PAIR] = dot(dkt_ref[...].astype(LOW), full).T.astype(LOW)
    weight_ref[:, PAIR : 2 * PAIR] = dot(dvt_ref[...].astype(LOW), full).T.astype(LOW)


def self_back_kernel(
    heads_ref, grad_ref, mix_ref, inv_ref, exp_ref, full_ref, out_ref, weight_ref, dkt_ref, dvt_ref
):
    attend_back(
        heads_ref[:, 0:PAIR], heads_ref[:, PAIR : 2 * PAIR], heads_ref[:, 2 * PAIR : 3 * PAIR],
        grad_ref, mix_ref, inv_ref, exp_ref, out_ref, dkt_ref, dvt_ref, True,
    )
    full = full_ref[...]
    weight_ref[:, 0:PAIR] = dot(out_ref[:, 0:PAIR].T, full).T.astype(LOW)
    weight_ref[:, PAIR : 2 * PAIR] = dot(dkt_ref[...].astype(LOW), full).T.astype(LOW)
    weight_ref[:, 2 * PAIR : 3 * PAIR] = dot(dvt_ref[...].astype(LOW), full).T.astype(LOW)


def join_heads(blocks_ref, whole_ref, start=0):
    for block in range(SEQ):
        whole_ref[:, block * PAIR : block * PAIR + PAIR] = blocks_ref[
            block, :, start : start + PAIR
        ]


def split_heads(values, blocks_ref):
    for block in range(SEQ):
        blocks_ref[block, :, :] = values[:, block * PAIR : block * PAIR + PAIR]


def middle_kernel(
    mix_ref, tok_ref, gain_ref, bias_ref, out_hbm, query_hbm, x1_ref, n2_ref, o1_ref, cq_ref,
    out_w, query_w, sems,
):
    first = pltpu.make_async_copy(out_hbm, out_w, sems.at[0])
    second = pltpu.make_async_copy(query_hbm, query_w, sems.at[1])
    first.start()
    second.start()
    join_heads(mix_ref, o1_ref)
    first.wait()
    x1 = tok_ref[...].astype(F32) + dot(o1_ref[...], out_w[...]) + bias_ref[5:6, :]
    x1_ref[...] = x1
    unit, _ = norm_unit(x1)
    n2 = (unit * gain_ref[1:2, :] + bias_ref[1:2, :]).astype(LOW)
    n2_ref[...] = n2
    second.wait()
    cq = ((dot(n2, query_w[...]) + bias_ref[6:7, :]) * SCALE).astype(LOW)
    split_heads(cq, cq_ref)


FF_CHUNK = 512


def feed_kernel(
    mix_ref, x1_ref, cot_ref, gain_ref, bias_ref, ebias_ref, out_hbm, expand_hbm, reduce_hbm,
    output_ref, o2_ref, n3_ref, act_ref, dfe_ref, dx2_ref, dc_ref, do2_ref, vec_ref,
    out_w, expand_w, reduce_w, acc_ref, dn3_ref, sems,
):
    chunks = FF // FF_CHUNK
    first = pltpu.make_async_copy(out_hbm, out_w, sems.at[0])
    first.start()

    def chunk_copies(step):
        span = pl.ds(pl.multiple_of(step * FF_CHUNK, FF_CHUNK), FF_CHUNK)
        return (
            pltpu.make_async_copy(
                expand_hbm.at[:, span], expand_w.at[:, span], sems.at[1 + step]
            ),
            pltpu.make_async_copy(
                reduce_hbm.at[span, :], reduce_w.at[span, :], sems.at[1 + chunks + step]
            ),
        )

    for step in range(chunks):
        for one in chunk_copies(step):
            one.start()
    join_heads(mix_ref, o2_ref)
    first.wait()
    x2 = x1_ref[...] + dot(o2_ref[...], out_w[...]) + bias_ref[8:9, :]
    unit, inverse = norm_unit(x2)
    n3_ref[...] = (unit * gain_ref[2:3, :] + bias_ref[2:3, :]).astype(LOW)
    acc_ref[...] = x2 + bias_ref[9:10, :]
    dn3_ref[...] = jnp.zeros_like(dn3_ref)
    root = math.sqrt(2.0 / math.pi)

    def body(step, carry):
        for one in chunk_copies(step):
            one.wait()
        span = pl.ds(pl.multiple_of(step * FF_CHUNK, FF_CHUNK), FF_CHUNK)
        hidden = dot(n3_ref[...], expand_w[:, span]) + ebias_ref[:, span]
        square = hidden * hidden
        curve = jnp.tanh(root * hidden * (1.0 + 0.044715 * square))
        half = 0.5 * (1.0 + curve)
        act = (hidden * half).astype(LOW)
        act_ref[:, span] = act
        slope = half + 0.5 * hidden * (1.0 - curve * curve) * (
            root * (1.0 + 3.0 * 0.044715 * square)
        )
        acc_ref[...] += dot(act, reduce_w[span, :])
        grad_act = dot_nt(cot_ref[...], reduce_w[span, :])
        grad_hidden = (slope * grad_act).astype(LOW)
        dfe_ref[:, span] = grad_hidden
        dn3_ref[...] += dot_nt(grad_hidden, expand_w[:, span])
        return carry

    lax.fori_loop(0, chunks, body, 0)
    output_ref[...] = acc_ref[...].astype(LOW)
    dn3 = dn3_ref[...]
    grad = cot_ref[...].astype(F32)
    dx2 = grad + norm_back(dn3, unit, inverse, gain_ref[2:3, :])
    dx2_ref[...] = dx2
    dc = dx2.astype(LOW)
    dc_ref[...] = dc
    split_heads(dot_nt(dc, out_w[...]).astype(LOW), do2_ref)
    for row in range(4):
        vec_ref[row : row + 1, :] = column_sum(
            dfe_ref[:, row * WIDTH : row * WIDTH + WIDTH].astype(F32)
        )
    vec_ref[4:5, :] = column_sum(dn3 * unit)
    vec_ref[5:6, :] = column_sum(dn3)
    vec_ref[6:7, :] = column_sum(dc.astype(F32))
    vec_ref[7:8, :] = column_sum(grad)


def middle_back_kernel(
    sums_ref, x1_ref, dx2_ref, gain_ref, ckv_hbm, query_hbm, out_hbm,
    gmem_ref, e2_ref, dx1_ref, da_ref, do1_ref, vec_ref,
    dkv_ref, ckv_w, query_w, out_w, sems,
):
    copies = [
        pltpu.make_async_copy(query_hbm, query_w, sems.at[0]),
        pltpu.make_async_copy(out_hbm, out_w, sems.at[1]),
        pltpu.make_async_copy(ckv_hbm, ckv_w, sems.at[2]),
    ]
    for one in copies:
        one.start()
    join_heads(sums_ref, e2_ref)
    for part in range(2):
        for block in range(SEQ):
            at = part * WIDTH + block * PAIR
            dkv_ref[:, at : at + PAIR] = sums_ref[block, :, (part + 1) * PAIR : (part + 2) * PAIR]
    unit, inverse = norm_unit(x1_ref[...])
    copies[0].wait()
    dn2 = dot_nt(e2_ref[...], query_w[...])
    dx1 = dx2_ref[...] + norm_back(dn2, unit, inverse, gain_ref[1:2, :])
    dx1_ref[...] = dx1
    da = dx1.astype(LOW)
    da_ref[...] = da
    copies[1].wait()
    split_heads(dot_nt(da, out_w[...]).astype(LOW), do1_ref)
    copies[2].wait()
    gmem_ref[...] = dot_nt(dkv_ref[...], ckv_w[...])
    vec_ref[0:1, :] = column_sum(dn2 * unit)
    vec_ref[1:2, :] = column_sum(dn2)
    vec_ref[2:3, :] = column_sum(da.astype(F32))
    vec_ref[3:4, :] = column_sum(e2_ref[...].astype(F32))
    vec_ref[4:5, :] = column_sum(dkv_ref[:, WIDTH : 2 * WIDTH].astype(F32))


def first_back_kernel(
    sums_ref, tok_ref, dx1_ref, gain_ref, qkv_hbm, gtok_ref, vec_ref, e1_ref, qkv_w, sems
):
    copy = pltpu.make_async_copy(qkv_hbm, qkv_w, sems.at[0])
    copy.start()
    for part in range(3):
        for block in range(SEQ):
            at = part * WIDTH + block * PAIR
            e1_ref[:, at : at + PAIR] = sums_ref[block, :, part * PAIR : (part + 1) * PAIR]
    unit, inverse = norm_unit(tok_ref[...].astype(F32))
    copy.wait()
    dn1 = dot_nt(e1_ref[...], qkv_w[...])
    gtok_ref[...] = dx1_ref[...] + norm_back(dn1, unit, inverse, gain_ref[0:1, :])
    vec_ref[0:1, :] = column_sum(dn1 * unit)
    vec_ref[1:2, :] = column_sum(dn1)
    vec_ref[2:3, :] = column_sum(e1_ref[:, 0:WIDTH].astype(F32))
    vec_ref[3:4, :] = column_sum(e1_ref[:, 2 * WIDTH : 3 * WIDTH].astype(F32))


LANES = 256
HALF = 176
CHUNK = 2 * HALF
FLOWS = (
    ("yzx", 0, 64, 1),
    ("yzx", 64, 48, -1),
    ("zxy", 112, 64, 1),
    ("zxy", 176, 64, -1),
    ("xyz", 240, 64, 1),
    ("xyz", 304, 48, -1),
)


def wrap(index):
    return lax.rem(index + 8, 4)


def device_of(core, x, y, z):
    return ((x // 2) * 8 + z * 2 + core, y * 2 + lax.rem(x, 2))


def reduce_kernel(
    n3_ref, dfe_ref, act_ref, cot_ref, o1_ref, da_ref, n2_ref, e2_ref, o2_ref, dc_ref,
    out_ref,
    a_exp, b_exp, a_red, b_red, a_out, b_out, a_que, b_que, a_cro, b_cro,
    grads, land1, land2, land3, pair_send, pair_recv, pair_local, send_sems, recv_sems, last_sems,
):
    dp = lax.axis_index("dp")
    seq = lax.axis_index("seq")
    core = lax.rem(dp, 2)
    z = lax.rem(dp // 2, 4)
    y = seq // 2
    x = (dp // 8) * 2 + lax.rem(seq, 2)
    other = device_of(1 - core, x, y, z)
    place = {"x": x, "y": y, "z": z}

    def neighbour(axis, step):
        at = dict(place)
        at[axis] = wrap(at[axis] + step)
        return device_of(core, **at)

    barrier = pltpu.get_barrier_semaphore()
    pl.semaphore_signal(barrier, inc=1, device_id=other, device_id_type=MESH)
    for axis in "xyz":
        for step in (1, -1):
            pl.semaphore_signal(
                barrier, inc=1, device_id=neighbour(axis, step), device_id_type=MESH
            )
    pl.semaphore_wait(barrier, 7)

    pairs = (
        (n3_ref, dfe_ref, a_exp, b_exp),
        (act_ref, cot_ref, a_red, b_red),
        (o1_ref, da_ref, a_out, b_out),
        (n2_ref, e2_ref, a_que, b_que),
        (o2_ref, dc_ref, a_cro, b_cro),
    )
    waits = []
    for index, (left, right, left_all, right_all) in enumerate(pairs):
        half = right.shape[1] // 2
        mine = pl.ds(pl.multiple_of(core * half, 512), half)
        theirs = pl.ds(pl.multiple_of((1 - core) * half, 512), half)
        for slot, (source, here, there) in enumerate(
            ((left, left_all, left), (right, right_all, right))
        ):
            at = 2 * index + slot
            keep = source if slot == 0 else source.at[:, mine]
            give = source if slot == 0 else source.at[:, theirs]
            local = pltpu.make_async_copy(keep, here.at[pl.ds(0, TOK), :], pair_local.at[at])
            remote = pltpu.make_async_remote_copy(
                src_ref=give,
                dst_ref=here.at[pl.ds(TOK, TOK), :],
                send_sem=pair_send.at[at],
                recv_sem=pair_recv.at[at],
                device_id=other,
                device_id_type=MESH,
            )
            local.start()
            remote.start()
            waits += [local, remote]
    for one in waits:
        one.wait()

    def fill(group, carry):
        xh = group // 4
        zz = lax.rem(group, 4)

        def put(result, rows, base, offset, spread):
            for to in range(2):
                for yy in range(4):
                    for xl in range(2):
                        for sub in range(spread):
                            grads[
                                xh * 2 + xl, yy, zz,
                                to * HALF + offset + sub * rows : to * HALF
                                + offset
                                + sub * rows
                                + rows,
                                :,
                            ] = result[
                                (to * 4 + yy) * rows : (to * 4 + yy) * rows + rows,
                                (xl * spread + sub) * LANES : (xl * spread + sub) * LANES + LANES,
                            ]

        cols = pl.ds(pl.multiple_of(group * 128, 128), 128)
        put(dot_tn(a_exp[:, cols], b_exp[...]).astype(LOW), 16, 0, 0, 4)
        wide = pl.ds(pl.multiple_of(group * 512, 512), 512)
        put(dot_tn(a_red[:, wide], b_red[...]).astype(LOW), 64, 0, 64, 1)
        put(dot_tn(a_out[:, cols], b_out[...]).astype(LOW), 16, 0, 128, 1)
        put(dot_tn(a_que[:, cols], b_que[...]).astype(LOW), 16, 0, 144, 1)
        put(dot_tn(a_cro[:, cols], b_cro[...]).astype(LOW), 16, 0, 160, 1)
        return carry

    lax.fori_loop(0, 8, fill, 0)

    def view(order, stage, chunk, first, rows):
        index = {"x": slice(None), "y": slice(None), "z": slice(None)}
        for done in range(stage):
            index[order[done]] = place[order[done]]
        index[order[stage]] = chunk
        return (index["x"], index["y"], index["z"], slice(first, first + rows), slice(None))

    lands = (land1, land2, land3)
    for stage in range(3):
        for step in range(3):
            copies = []
            for flow, (order, first, rows, way) in enumerate(FLOWS):
                axis = order[stage]
                sent = wrap(place[axis] - way * (1 + step))
                at = (stage * 3 + step) * 6 + flow
                land = lands[stage].at[(step,) + (slice(None),) * (2 - stage) + (slice(first, first + rows),)]
                copy = pltpu.make_async_remote_copy(
                    src_ref=grads.at[view(order, stage, sent, first, rows)],
                    dst_ref=land,
                    send_sem=send_sems.at[at],
                    recv_sem=recv_sems.at[at],
                    device_id=neighbour(axis, way),
                    device_id_type=MESH,
                )
                copy.start()
                copies.append(copy)
            for flow, (order, first, rows, way) in enumerate(FLOWS):
                copies[flow].wait()
                got = wrap(place[order[stage]] - way * (2 + step))
                land = lands[stage][(step,) + (slice(None),) * (2 - stage) + (slice(first, first + rows),)]
                at = view(order, stage, got, first, rows)
                grads[at] = grads[at] + land

    keep = pltpu.make_async_copy(
        grads.at[x, y, z, pl.ds(pl.multiple_of(core * HALF, 16), HALF), :],
        out_ref.at[core],
        last_sems.at[0],
    )
    give = pltpu.make_async_remote_copy(
        src_ref=grads.at[x, y, z, pl.ds(pl.multiple_of((1 - core) * HALF, 16), HALF), :],
        dst_ref=out_ref.at[core],
        send_sem=last_sems.at[1],
        recv_sem=last_sems.at[2],
        device_id=other,
        device_id_type=MESH,
    )
    keep.start()
    give.start()
    keep.wait()
    give.wait()


def reduce_call(operands):
    dma = pltpu.SemaphoreType.DMA
    vmem = pltpu.VMEM
    return pl.pallas_call(
        reduce_kernel,
        out_shape=shaped((2, HALF, LANES)),
        in_specs=[spec_vmem()] * 10,
        out_specs=spec_vmem(),
        scratch_shapes=[
            vmem((2 * TOK, WIDTH), LOW), vmem((2 * TOK, 2048), LOW),
            vmem((2 * TOK, FF), LOW), vmem((2 * TOK, 512), LOW),
            vmem((2 * TOK, WIDTH), LOW), vmem((2 * TOK, 512), LOW),
            vmem((2 * TOK, WIDTH), LOW), vmem((2 * TOK, 512), LOW),
            vmem((2 * TOK, WIDTH), LOW), vmem((2 * TOK, 512), LOW),
            vmem((4, 4, 4, CHUNK, LANES), LOW),
            vmem((3, 4, 4, CHUNK, LANES), LOW),
            vmem((3, 4, CHUNK, LANES), LOW),
            vmem((3, CHUNK, LANES), LOW),
            dma((10,)), dma((10,)), dma((10,)), dma((54,)), dma((54,)), dma((3,)),
        ],
        compiler_params=pltpu.CompilerParams(
            collective_id=1, has_side_effects=True, vmem_limit_bytes=56 * MIB
        ),
        cost_estimate=pl.CostEstimate(
            flops=2 * 128 * 11 * MIB, bytes_accessed=100 * MIB, transcendentals=0
        ),
        name="reduce_weights",
    )(*operands)


def finish_kernel(
    piece_ref, qkv_ref, ckv_ref, vec_ref,
    gqkv_ref, gout_ref, gque_ref, gckv_ref, gcro_ref, gexp_ref, gred_ref, gvec_ref,
):
    for seq in range(SEQ):
        y, xl = seq // 2, seq % 2
        for col in range(2):
            for sub in range(4):
                at = col * 2048 + xl * 1024 + sub * LANES
                gexp_ref[16 * y : 16 * y + 16, at : at + LANES] = piece_ref[
                    seq, col, sub * 16 : sub * 16 + 16, :
                ].astype(F32)
            at = col * 512 + xl * LANES
            gred_ref[64 * y : 64 * y + 64, at : at + LANES] = piece_ref[
                seq, col, 64:128, :
            ].astype(F32)
            for target, start in ((gout_ref, 128), (gque_ref, 144), (gcro_ref, 160)):
                target[16 * y : 16 * y + 16, at : at + LANES] = piece_ref[
                    seq, col, start : start + 16, :
                ].astype(F32)
        for part in range(3):
            at = part * WIDTH + seq * PAIR
            gqkv_ref[:, at : at + PAIR] = qkv_ref[seq, :, part * PAIR : (part + 1) * PAIR].astype(F32)
        for part in range(2):
            at = part * WIDTH + seq * PAIR
            gckv_ref[:, at : at + PAIR] = ckv_ref[seq, :, part * PAIR : (part + 1) * PAIR].astype(F32)
    total = vec_ref[0]
    for seq in range(1, SEQ):
        total = total + vec_ref[seq]
    gvec_ref[...] = total


def swap(values, axis):
    return lax.all_to_all(values, axis, split_axis=0, concat_axis=0, tiled=True)


def spread_to_all(values):
    return swap(jnp.broadcast_to(values[None], (SEQ,) + values.shape), "seq")


def on_device(
    tokens, memory, cotangent, offsets, memory_ids, pair_map, self_qkv, self_out, cross_query,
    cross_kv, cross_out, expand_weight, expand_bias, reduce_weight, norm_gains, bias_rows,
):
    dma = pltpu.SemaphoreType.DMA
    vmem = pltpu.VMEM
    tok = tokens.reshape(TOK, WIDTH)
    mem = memory.reshape(TOK, WIDTH)
    cot = cotangent.reshape(TOK, WIDTH)
    memory_all = lax.all_gather(mem, "seq", axis=0, tiled=True)

    heads, mem_heads, n1 = local_call(
        project_kernel,
        (shaped((SEQ, TOK, 3 * PAIR)), shaped((SEQ, TOK, 2 * PAIR)), shaped((TOK, WIDTH))),
        [spec_vmem()] * 4 + [spec_any()] * 2,
        [vmem((WIDTH, 3 * WIDTH), LOW), vmem((WIDTH, 2 * WIDTH), LOW), dma((20,))],
        "project", 2 * TOK * WIDTH * 5 * WIDTH, 12 * MIB,
    )(tok, mem, norm_gains, bias_rows, self_qkv, cross_kv)
    n1_all = lax.all_gather(n1, "seq", axis=0, tiled=True)
    heads = swap(heads, "seq").reshape(ROW, 3 * PAIR)

    attend_outs = (shaped((ROW, PAIR)), shaped((2, ROW, ROW)), shaped((ROW, PAIR), F32))
    mix1, exp1, inv1 = local_call(
        self_attend_kernel, attend_outs, [spec_vmem(), spec_smem()], [],
        "self_attend", 2 * 2 * ROW * ROW * PAIR, 5 * MIB,
    )(heads, offsets)
    mix1_back = swap(mix1.reshape(SEQ, TOK, PAIR), "seq")
    mem_heads = swap(mem_heads, "seq").reshape(ROW, 2 * PAIR)

    x1, n2, o1, cq = local_call(
        middle_kernel,
        (shaped((TOK, WIDTH), F32), shaped((TOK, WIDTH)), shaped((TOK, WIDTH)),
         shaped((SEQ, TOK, PAIR))),
        [spec_vmem()] * 4 + [spec_any()] * 2,
        [vmem((WIDTH, WIDTH), LOW), vmem((WIDTH, WIDTH), LOW), dma((2,))],
        "middle", 2 * TOK * WIDTH * 2 * WIDTH, 5 * MIB,
    )(mix1_back, tok, norm_gains, bias_rows, self_out, cross_query)
    cq = swap(cq, "seq").reshape(ROW, PAIR)

    mix2, exp2, inv2 = local_call(
        cross_attend_kernel, attend_outs, [spec_vmem()] * 3 + [spec_smem()] * 2, [],
        "cross_attend", 4 * 2 * ROW * ROW * PAIR, 5 * MIB,
    )(cq, mem_heads, memory_ids, offsets, pair_map)
    mix2_back = swap(mix2.reshape(SEQ, TOK, PAIR), "seq")

    output, o2, n3, act, dfe, dx2, dc, do2, vec_a = local_call(
        feed_kernel,
        (
            shaped((TOK, WIDTH)), shaped((TOK, WIDTH)), shaped((TOK, WIDTH)), shaped((TOK, FF)),
            shaped((TOK, FF)), shaped((TOK, WIDTH), F32), shaped((TOK, WIDTH)),
            shaped((SEQ, TOK, PAIR)), shaped((8, WIDTH), F32),
        ),
        [spec_vmem()] * 6 + [spec_any()] * 3,
        [
            vmem((WIDTH, WIDTH), LOW), vmem((WIDTH, FF), LOW), vmem((FF, WIDTH), LOW),
            vmem((TOK, WIDTH), F32), vmem((TOK, WIDTH), F32), dma((1 + 2 * FF // FF_CHUNK,)),
        ],
        "feed", 2 * TOK * WIDTH * 18 * WIDTH, 22 * MIB,
    )(mix2_back, x1, cot, norm_gains, bias_rows, expand_bias.reshape(1, FF), cross_out,
      expand_weight, reduce_weight)
    do2 = swap(do2, "seq").reshape(ROW, PAIR)

    scratch_back = [vmem((PAIR, ROW), F32), vmem((PAIR, ROW), F32)]
    sums2, weight_ckv = local_call(
        cross_back_kernel,
        (shaped((ROW, 3 * PAIR)), shaped((ROW, 2 * PAIR))),
        [spec_vmem()] * 7, scratch_back,
        "cross_back", 12 * 2 * ROW * ROW * PAIR, 10 * MIB,
    )(cq, mem_heads, do2, mix2, inv2, exp2, memory_all)
    sums2 = swap(sums2.reshape(SEQ, TOK, 3 * PAIR), "seq")

    gmem, e2, dx1, da, do1, vec_b = local_call(
        middle_back_kernel,
        (
            shaped((TOK, WIDTH), F32), shaped((TOK, WIDTH)), shaped((TOK, WIDTH), F32),
            shaped((TOK, WIDTH)), shaped((SEQ, TOK, PAIR)), shaped((5, WIDTH), F32),
        ),
        [spec_vmem()] * 4 + [spec_any()] * 3,
        [
            vmem((TOK, 2 * WIDTH), LOW), vmem((WIDTH, 2 * WIDTH), LOW), vmem((WIDTH, WIDTH), LOW),
            vmem((WIDTH, WIDTH), LOW), dma((3,)),
        ],
        "middle_back", 2 * TOK * WIDTH * 4 * WIDTH, 10 * MIB,
    )(sums2, x1, dx2, norm_gains, cross_kv, cross_query, self_out)
    do1 = swap(do1, "seq").reshape(ROW, PAIR)

    sums1, weight_qkv = local_call(
        self_back_kernel,
        (shaped((ROW, 3 * PAIR)), shaped((ROW, 3 * PAIR))),
        [spec_vmem()] * 6, scratch_back,
        "self_back", 8 * 2 * ROW * ROW * PAIR, 10 * MIB,
    )(heads, do1, mix1, inv1, exp1, n1_all)
    sums1 = swap(sums1.reshape(SEQ, TOK, 3 * PAIR), "seq")

    gtok, vec_c = local_call(
        first_back_kernel,
        (shaped((TOK, WIDTH), F32), shaped((4, WIDTH), F32)),
        [spec_vmem()] * 4 + [spec_any()],
        [vmem((TOK, 3 * WIDTH), LOW), vmem((WIDTH, 3 * WIDTH), LOW), dma((1,))],
        "first_back", 2 * TOK * WIDTH * 3 * WIDTH, 8 * MIB,
    )(sums1, tok, dx1, norm_gains, self_qkv)

    piece = reduce_call((n3, dfe, act, cot, o1, da, n2, e2, o2, dc))

    def summed(values, kind):
        blocks = swap(values, "dp")
        return jnp.sum(blocks.astype(F32), 0).astype(kind)

    part_qkv = summed(weight_qkv.reshape(DP, ROW // DP, 3 * PAIR), LOW)
    part_ckv = summed(weight_ckv.reshape(DP, ROW // DP, 2 * PAIR), LOW)
    rows = jnp.concatenate(
        [
            vec_c[0:1], vec_b[0:1], vec_a[4:5],
            vec_c[1:2], vec_b[1:2], vec_a[5:6], vec_c[2:4], vec_b[2:5], vec_a[6:8],
        ]
    )
    vec = jnp.concatenate(
        [
            vec_a[0:4].reshape(DP, 2, PAIR),
            jnp.concatenate(
                [rows.reshape(13, DP, 64), jnp.zeros((1, DP, 64), F32)]
            ).transpose(1, 0, 2).reshape(DP, 7, PAIR),
        ],
        1,
    )
    part_vec = summed(vec, F32)

    gqkv, gout, gque, gckv, gcro, gexp, gred, gvec = local_call(
        finish_kernel,
        (
            shaped((64, 3 * WIDTH), F32), shaped((64, WIDTH), F32), shaped((64, WIDTH), F32),
            shaped((64, 2 * WIDTH), F32), shaped((64, WIDTH), F32), shaped((64, FF), F32),
            shaped((256, WIDTH), F32), shaped((9, PAIR), F32),
        ),
        [spec_vmem()] * 4, [], "finish", 0, 8 * MIB,
    )(spread_to_all(piece), spread_to_all(part_qkv), spread_to_all(part_ckv),
      spread_to_all(part_vec))
    tail = gvec[2:].reshape(14, 64)
    return (
        output.reshape(1, TOK, WIDTH), gtok.reshape(1, TOK, WIDTH), gmem.reshape(1, TOK, WIDTH),
        gqkv, gout, gque, gckv, gcro, gexp, gvec[0:2].reshape(256), gred, tail[0:3], tail[3:13],
    )


def solution(mesh):
    row = P("dp", "seq", None)
    split = P("dp", None)
    in_specs = (row,) * 3 + (split,) * 3 + (P(),) * 10
    out_specs = (row,) * 3 + (split,) * 6 + (P("dp"), split, P(None, "dp"), P(None, "dp"))
    return jax.shard_map(
        on_device, mesh=mesh, in_specs=in_specs, out_specs=out_specs, check_vma=False
    )
```

```python
import functools
import math

import jax
import jax.numpy as jnp
from jax import lax
from jax.experimental import pallas as pl
from jax.experimental.pallas import tpu as pltpu
from jax.sharding import PartitionSpec as P

HEADS = 16
HEAD_DIM = 64
WIDTH = 1024
TOK = 128
ROW = 1024
FF = 4096
SEQ = 8
DP = 16
PAIR = 128
NEG_FILL = -1e30
EPS = 1e-05
SCALE = HEAD_DIM ** (-0.5)
LOW = jnp.bfloat16
F32 = jnp.float32
MESH = pl.DeviceIdType.MESH
MIB = 2**20


def dot(left, right):
    return lax.dot_general(left, right, (((1,), (0,)), ((), ())), preferred_element_type=F32)


def dot_nt(left, right):
    return lax.dot_general(left, right, (((1,), (1,)), ((), ())), preferred_element_type=F32)


def dot_tn(left, right):
    return lax.dot_general(left, right, (((0,), (0,)), ((), ())), preferred_element_type=F32)


def norm_unit(values):
    average = jnp.mean(values, -1, keepdims=True)
    centered = values - average
    inverse = lax.rsqrt(jnp.mean(centered * centered, -1, keepdims=True) + EPS)
    return centered * inverse, inverse


def norm_back(incoming, unit, inverse, gain_row):
    scaled = incoming * gain_row
    return inverse * (
        scaled
        - jnp.mean(scaled, -1, keepdims=True)
        - unit * jnp.mean(scaled * unit, -1, keepdims=True)
    )


def column_sum(values):
    return jnp.sum(values, 0, keepdims=True)


def spec_any():
    return pl.BlockSpec(memory_space=pl.ANY)


def spec_vmem():
    return pl.BlockSpec(memory_space=pltpu.VMEM)


def spec_smem():
    return pl.BlockSpec(memory_space=pltpu.SMEM)


def local_call(kernel, outs, specs, scratch, name, flops, moved, vmem=48):
    return pl.pallas_call(
        kernel,
        out_shape=outs,
        in_specs=specs,
        out_specs=jax.tree.map(lambda _: spec_vmem(), outs),
        scratch_shapes=scratch,
        compiler_params=pltpu.CompilerParams(vmem_limit_bytes=vmem * MIB),
        cost_estimate=pl.CostEstimate(flops=flops, bytes_accessed=moved, transcendentals=0),
        name=name,
    )


def shaped(shape, kind=LOW):
    return jax.ShapeDtypeStruct(shape, kind)


def head_lanes(rows):
    return lax.broadcasted_iota(jnp.int32, (rows, PAIR), 1) < HEAD_DIM


def pick_head(values, lanes, head):
    zero = jnp.zeros_like(values)
    return jnp.where(lanes, values, zero) if head == 0 else jnp.where(lanes, zero, values)


def attend_tile(query, key_t, value, allowed, exp_ref, rows, width):
    lanes = head_lanes(query.shape[0])
    mixed, inverses = [], []
    for head in range(2):
        scores = dot(pick_head(query, lanes, head), key_t)
        scores = jnp.where(allowed, scores, NEG_FILL)
        top = jnp.max(scores, -1, keepdims=True)
        exponent = jnp.exp(scores - top)
        inverse = 1.0 / jnp.sum(exponent, -1, keepdims=True)
        low = exponent.astype(LOW)
        exp_ref[head, rows, 0:width] = low
        mixed.append(dot(low, value))
        inverses.append(inverse)
    inverse = jnp.where(lanes, inverses[0], inverses[1])
    return jnp.where(lanes, mixed[0], mixed[1]) * inverse, inverse


def self_allowed(offsets_ref, step, tile, width):
    places = lax.broadcasted_iota(jnp.int32, (tile, 1), 0) + step * tile
    begin = jnp.zeros((tile, 1), jnp.int32)
    for seg in range(1, 16):
        offset = offsets_ref[0, seg]
        begin = jnp.where(places >= offset, offset, begin)
    keys = lax.broadcasted_iota(jnp.int32, (tile, width), 1)
    return (keys <= places) & (keys >= begin)


def cross_allowed(ids, offsets_ref, pair_ref, step, tile):
    places = lax.broadcasted_iota(jnp.int32, (tile, 1), 0) + step * tile
    reads = jnp.zeros((tile, 1), jnp.int32) + pair_ref[0, 0]
    for seg in range(1, 16):
        reads = jnp.where(places >= offsets_ref[0, seg], pair_ref[0, seg], reads)
    return ids == reads


def aligned(index, unit):
    return pl.ds(pl.multiple_of(index * unit, unit), unit)


class Exchange:
    def __init__(self, send_sems, recv_sems, base):
        self.dp = lax.axis_index("dp")
        self.me = lax.axis_index("seq")
        self.send_sems, self.recv_sems, self.base = send_sems, recv_sems, base
        self.sent = []

    def copy(self, source, target, there, distance):
        return pltpu.make_async_remote_copy(
            src_ref=source,
            dst_ref=target,
            send_sem=self.send_sems.at[self.base + distance],
            recv_sem=self.recv_sems.at[self.base + distance],
            device_id=(self.dp, there),
            device_id_type=MESH,
        )

    def push(self, source, target, there, may_be_own):
        distance = lax.rem(there - self.me + SEQ, SEQ)
        if may_be_own:
            remote = there != self.me

            @pl.when(remote)
            def _():
                self.copy(source, target, there, distance).start()

        else:
            self.copy(source, target, there, distance).start()
        self.sent.append((source, target))

    def receive(self, place):
        for distance in range(1, SEQ):
            sender = lax.rem(self.me - distance + SEQ, SEQ)
            spot = place(sender)
            self.copy(spot, spot, sender, distance).wait_recv()

    def drain(self):
        source, target = self.sent[0]
        for distance in range(1, SEQ):
            there = lax.rem(self.me + distance, SEQ)
            self.copy(source, target, there, distance).wait_send()


def greet_row():
    dp = lax.axis_index("dp")
    me = lax.axis_index("seq")
    barrier = pltpu.get_barrier_semaphore()
    for distance in range(1, SEQ):
        pl.semaphore_signal(
            barrier, inc=1, device_id=(dp, lax.rem(me + distance, SEQ)), device_id_type=MESH
        )
    return barrier


class Gather:
    def __init__(self, block, whole, local_sem, send_sems, recv_sems, base):
        self.dp = lax.axis_index("dp")
        self.me = lax.axis_index("seq")
        self.y, self.xl = self.me // 2, lax.rem(self.me, 2)
        self.whole, self.send_sems, self.recv_sems, self.base = whole, send_sems, recv_sems, base
        self.own = pltpu.make_async_copy(block, whole.at[aligned(self.me, TOK), :], local_sem)
        self.block = block

    def part(self, y, half=None):
        y = lax.rem(y + 8, 4)
        if half is None:
            return self.whole.at[aligned(y, 2 * TOK), :]
        return self.whole.at[aligned(y * 2 + half, TOK), :]

    def copy(self, source, target, there, slot):
        return pltpu.make_async_remote_copy(
            src_ref=source,
            dst_ref=target,
            send_sem=self.send_sems.at[self.base + slot],
            recv_sem=self.recv_sems.at[self.base + slot],
            device_id=(self.dp, there),
            device_id_type=MESH,
        )

    def beside(self, step):
        return lax.rem(self.y + step + 4, 4) * 2 + self.xl

    def first(self):
        self.own.start()
        partner = self.y * 2 + 1 - self.xl
        self.copy(self.block, self.part(self.y, self.xl), partner, 0).start()

    def second(self):
        self.own.wait()
        partner = self.y * 2 + 1 - self.xl
        spot = self.part(self.y, 1 - self.xl)
        self.copy(spot, spot, partner, 0).wait_recv()
        for slot, step in ((1, 1), (2, -1)):
            self.copy(self.part(self.y), self.part(self.y), self.beside(step), slot).start()

    def third(self):
        for slot, step in ((1, 1), (2, -1)):
            spot = self.part(self.y - step)
            self.copy(spot, spot, self.beside(-step), slot).wait_recv()
            half = slot - 1
            piece = self.part(self.y - step, half)
            self.copy(piece, piece, self.beside(step), slot + 2).start()

    def finish(self):
        for slot, step in ((1, 1), (2, -1)):
            spot = self.part(self.y + 2, slot - 1)
            self.copy(spot, spot, self.beside(-step), slot + 2).wait_recv()
        partner = self.y * 2 + 1 - self.xl
        self.copy(self.block, self.part(self.y, self.xl), partner, 0).wait_send()
        for slot, step in ((1, 1), (2, -1)):
            whole = self.part(self.y)
            self.copy(whole, whole, self.beside(step), slot).wait_send()
            piece = self.part(self.y - step, slot - 1)
            self.copy(piece, piece, self.beside(step), slot + 2).wait_send()


def front_kernel(
    tok_ref, mem_ref, gain_ref, bias_ref, ids_ref, offsets_ref, pair_ref,
    qkv_hbm, ckv_hbm, out_hbm, query_hbm,
    x1_ref, n2_ref, o1_ref, o2_ref, heads_ref, memh_ref, cqh_ref, mix1_ref, mix2_ref,
    inv1_ref, inv2_ref, n1_ref, exp1_hbm, exp2_hbm,
    qkv_w, ckv_w, out_w, query_w, give_heads, give_mem, cq_ref, exp1_ref, exp2_ref,
    load_sems, keep_sems, exp_sems, send_sems, recv_sems,
):
    me = lax.axis_index("seq")
    y, xl = me // 2, lax.rem(me, 2)
    barrier = greet_row()
    order = [lax.rem(y + step, 4) for step in (1, 2, 3, 0)]
    loads = {}
    for step in range(4):
        for part in range(3):
            cols = pl.ds(pl.multiple_of(part * WIDTH + order[step] * 256, 256), 256)
            loads["qkv", step, part] = pltpu.make_async_copy(
                qkv_hbm.at[:, cols], qkv_w.at[:, cols], load_sems.at[step * 3 + part]
            )
    for step in range(4):
        for part in range(2):
            cols = pl.ds(pl.multiple_of(part * WIDTH + order[step] * 256, 256), 256)
            loads["ckv", step, part] = pltpu.make_async_copy(
                ckv_hbm.at[:, cols], ckv_w.at[:, cols], load_sems.at[12 + step * 2 + part]
            )
    loads["out"] = pltpu.make_async_copy(out_hbm, out_w, load_sems.at[20])
    loads["query"] = pltpu.make_async_copy(query_hbm, query_w, load_sems.at[21])
    for one in loads.values():
        one.start()

    give_qkv, give_kv, back1, give_q, back2 = (
        Exchange(send_sems, recv_sems, 8 * index) for index in range(5)
    )
    own_rows = aligned(me, TOK)

    unit, _ = norm_unit(tok_ref[...].astype(F32))
    n1 = (unit * gain_ref[0:1, :] + bias_ref[0:1, :]).astype(LOW)
    n1_ref[...] = n1
    mem = mem_ref[...]
    for kind, count, source, give, heads, exchange in (
        ("qkv", 3, n1, give_heads, heads_ref, give_qkv),
        ("ckv", 2, mem, give_mem, memh_ref, give_kv),
    ):
        for step in range(4):
            at = order[step]
            own = aligned(at, 256)
            for part in range(count):
                loads[kind, step, part].wait()
                cols = pl.ds(pl.multiple_of(part * WIDTH + at * 256, 256), 256)
                if kind == "qkv":
                    value = dot(source, qkv_w[:, cols])
                    if part == 0:
                        value = (value + bias_ref[3:4, own]) * SCALE
                    elif part == 2:
                        value = value + bias_ref[4:5, own]
                else:
                    value = dot(source, ckv_w[:, cols])
                    if part == 1:
                        value = value + bias_ref[7:8, own]
                low = value.astype(LOW)
                give[2 * at, :, part * PAIR : part * PAIR + PAIR] = low[:, :PAIR]
                give[2 * at + 1, :, part * PAIR : part * PAIR + PAIR] = low[:, PAIR:]
            if kind == "qkv" and step == 0:
                pl.semaphore_wait(barrier, SEQ - 1)
            there = heads.at[own_rows, :]
            if step < 3:
                exchange.push(give.at[2 * at], there, 2 * at, False)
                exchange.push(give.at[2 * at + 1], there, 2 * at + 1, False)
            else:
                partner = 2 * y + 1 - xl
                exchange.push(give.at[partner], there, partner, False)
                keep = pltpu.make_async_copy(
                    give.at[me], there, keep_sems.at[2 if kind == "qkv" else 3]
                )
                keep.start()
                loads[kind] = keep

    def attended(allowed_of, query_of, key_t, value_ref, value_at, mix_ref, inv_ref, exp_ref,
                 exp_hbm, exp_base, causal, back, target_ref, keep_sem):
        tile = 256
        for step in range(ROW // tile):
            rows = slice(step * tile, step * tile + tile)
            width = (step + 1) * tile if causal else ROW
            mixture, inverse = attend_tile(
                query_of(rows), key_t[:, 0:width], value_ref[0:width, value_at], allowed_of(step, width),
                exp_ref, rows, width,
            )
            mix_ref[rows, :] = mixture.astype(LOW)
            inv_ref[rows, :] = inverse
            for half in range(2):
                there = 2 * step + half
                back.push(
                    mix_ref.at[there * TOK : there * TOK + TOK, :],
                    target_ref.at[:, aligned(me, PAIR)], there, True,
                )
            for head in range(2):
                spot = (head, rows, slice(0, width))
                pltpu.make_async_copy(
                    exp_ref.at[spot], exp_hbm.at[spot], exp_sems.at[exp_base + step * 2 + head]
                ).start()
        keep = pltpu.make_async_copy(
            mix_ref.at[own_rows, :], target_ref.at[:, aligned(me, PAIR)], keep_sem
        )
        keep.start()
        return keep

    loads["qkv"].wait()
    give_qkv.receive(lambda sender: heads_ref.at[aligned(sender, TOK), :])
    key_t = heads_ref[:, PAIR : 2 * PAIR].T
    keep1 = attended(
        lambda step, width: self_allowed(offsets_ref, step, 256, width),
        lambda rows: heads_ref[rows, 0:PAIR], key_t, heads_ref, slice(2 * PAIR, 3 * PAIR),
        mix1_ref, inv1_ref, exp1_ref, exp1_hbm, 0, True, back1, o1_ref, keep_sems.at[4],
    )
    keep1.wait()
    loads["out"].wait()
    back1.receive(lambda sender: o1_ref.at[:, aligned(sender, PAIR)])
    x1 = tok_ref[...].astype(F32) + dot(o1_ref[...], out_w[...]) + bias_ref[5:6, :]
    x1_ref[...] = x1
    unit, _ = norm_unit(x1)
    n2 = (unit * gain_ref[1:2, :] + bias_ref[1:2, :]).astype(LOW)
    n2_ref[...] = n2
    loads["query"].wait()
    for step in range(4):
        at = order[step]
        own = aligned(at, 256)
        cq_ref[:, own] = ((dot(n2, query_w[:, own]) + bias_ref[6:7, own]) * SCALE).astype(LOW)
        for half in range(2):
            there = 2 * at + half if step < 3 else 2 * y + 1 - xl
            if step == 3 and half == 1:
                continue
            give_q.push(cq_ref.at[:, aligned(there, PAIR)], cqh_ref.at[own_rows, :], there, False)
    keep = pltpu.make_async_copy(cq_ref.at[:, aligned(me, PAIR)], cqh_ref.at[own_rows, :], keep_sems.at[5])
    keep.start()
    loads["ckv"].wait()
    give_kv.receive(lambda sender: memh_ref.at[aligned(sender, TOK), :])
    key_t = memh_ref[:, 0:PAIR].T
    keep.wait()
    give_q.receive(lambda sender: cqh_ref.at[aligned(sender, TOK), :])
    ids = ids_ref[...]
    keep2 = attended(
        lambda step, width: cross_allowed(ids, offsets_ref, pair_ref, step, 256),
        lambda rows: cqh_ref[rows, :], key_t, memh_ref, slice(PAIR, 2 * PAIR),
        mix2_ref, inv2_ref, exp2_ref, exp2_hbm, 8, False, back2, o2_ref, keep_sems.at[6],
    )
    keep2.wait()
    back2.receive(lambda sender: o2_ref.at[:, aligned(sender, PAIR)])
    for step in range(4):
        rows = slice(step * 256, step * 256 + 256)
        for head in range(2):
            spot = (head, rows, slice(0, step * 256 + 256))
            pltpu.make_async_copy(
                exp1_ref.at[spot], exp1_hbm.at[spot], exp_sems.at[step * 2 + head]
            ).wait()
            spot = (head, rows, slice(0, ROW))
            pltpu.make_async_copy(
                exp2_ref.at[spot], exp2_hbm.at[spot], exp_sems.at[8 + step * 2 + head]
            ).wait()
    for exchange in (give_qkv, give_kv, back1, give_q, back2):
        exchange.drain()


def front_call(operands):
    dma = pltpu.SemaphoreType.DMA
    vmem = pltpu.VMEM
    heads = shaped((ROW, PAIR))
    token = shaped((TOK, WIDTH))
    inverse = shaped((ROW, PAIR), F32)
    exps = shaped((2, ROW, ROW))
    return pl.pallas_call(
        front_kernel,
        out_shape=(
            shaped((TOK, WIDTH), F32), token, token, token, shaped((ROW, 3 * PAIR)),
            shaped((ROW, 2 * PAIR)), heads, heads, heads, inverse, inverse, token,
            exps, exps,
        ),
        in_specs=[spec_vmem()] * 5 + [spec_smem()] * 2 + [spec_any()] * 4,
        out_specs=(spec_vmem(),) * 12 + (spec_any(),) * 2,
        scratch_shapes=[
            vmem((WIDTH, 3 * WIDTH), LOW), vmem((WIDTH, 2 * WIDTH), LOW), vmem((WIDTH, WIDTH), LOW),
            vmem((WIDTH, WIDTH), LOW), vmem((SEQ, TOK, 3 * PAIR), LOW), vmem((SEQ, TOK, 2 * PAIR), LOW),
            vmem((TOK, WIDTH), LOW), vmem((2, ROW, ROW), LOW), vmem((2, ROW, ROW), LOW),
            dma((22,)), dma((7,)), dma((16,)), dma((40,)), dma((40,)),
        ],
        compiler_params=pltpu.CompilerParams(
            collective_id=2, has_side_effects=True, vmem_limit_bytes=56 * MIB
        ),
        cost_estimate=pl.CostEstimate(
            flops=2 * TOK * WIDTH * 7 * WIDTH, bytes_accessed=60 * MIB, transcendentals=0
        ),
        name="front",
    )(*operands)


LANES = 256


def wrap(index):
    return lax.rem(index + 8, 4)


def device_of(core, x, y, z):
    return ((x // 2) * 8 + z * 2 + core, y * 2 + lax.rem(x, 2))


class Place:
    def __init__(self):
        self.dp = lax.axis_index("dp")
        self.seq = lax.axis_index("seq")
        self.core = lax.rem(self.dp, 2)
        self.y, self.xl = self.seq // 2, lax.rem(self.seq, 2)
        self.at = {
            "x": (self.dp // 8) * 2 + self.xl,
            "y": self.y,
            "z": lax.rem(self.dp // 2, 4),
        }
        self.other = (self.dp + 1 - 2 * self.core, self.seq)

    def neighbour(self, axis, step):
        at = dict(self.at)
        at[axis] = wrap(at[axis] + step)
        return device_of(self.core, **at)


class Sum:
    def __init__(self, place, grads, lands, flows, send_sems, recv_sems, base):
        self.place, self.grads, self.lands, self.flows = place, grads, lands, flows
        self.send_sems, self.recv_sems, self.base = send_sems, recv_sems, base
        self.open_sends = []

    def view(self, order, stage, block, first, rows):
        index = {"x": slice(None), "y": slice(None), "z": slice(None)}
        for done in range(stage):
            index[order[done]] = self.place.at[order[done]]
        index[order[stage]] = block
        return (index["x"], index["y"], index["z"], slice(first, first + rows), slice(None))

    def land(self, stage, slot, first, rows):
        return (slot,) + (slice(None),) * (2 - stage) + (slice(first, first + rows), slice(None))

    def spans(self, flow):
        order, first, low, high = self.flows[flow]
        return order, (first, low), (first + low, high)

    def copy(self, stage, flow, kind):
        order, low, high = self.spans(flow)
        axis = order[stage]
        step = (2, 2, 1, -1, 1, -1)[kind]
        way = (1, -1, 1, -1, 1, -1)[kind]
        first, rows = (low, high, high, low, low, high)[kind]
        slot = (0, 0, 1, 1, 2, 2)[kind]
        at = self.base + (stage * len(self.flows) + flow) * 6 + kind
        return pltpu.make_async_remote_copy(
            src_ref=self.grads.at[
                self.view(order, stage, wrap(self.place.at[axis] + step), first, rows)
            ],
            dst_ref=self.lands[stage].at[self.land(stage, slot, first, rows)],
            send_sem=self.send_sems.at[at],
            recv_sem=self.recv_sems.at[at],
            device_id=self.place.neighbour(axis, way),
            device_id_type=MESH,
        )

    def add(self, stage, flow, step, span, slots):
        order, _, _ = self.spans(flow)
        at = self.view(order, stage, wrap(self.place.at[order[stage]] + step), *span)
        total = self.grads[at].astype(F32)
        for slot in slots:
            total = total + self.lands[stage][self.land(stage, slot, *span)].astype(F32)
        self.grads[at] = total.astype(LOW)

    def start(self, stage, flow, kind):
        copy = self.copy(stage, flow, kind)
        copy.start()
        self.open_sends.append(copy)

    def run(self):
        count = len(self.flows)
        for stage in range(3):
            for kind in range(4):
                for flow in range(count):
                    self.start(stage, flow, kind)
            yield
            for flow in range(count):
                _, low, high = self.spans(flow)
                self.copy(stage, flow, 0).wait_recv()
                self.add(stage, flow, 1, low, (0,))
                self.start(stage, flow, 4)
                self.copy(stage, flow, 1).wait_recv()
                self.add(stage, flow, -1, high, (0,))
                self.start(stage, flow, 5)
            yield
            for flow in range(count):
                _, low, high = self.spans(flow)
                for kind in (2, 3, 4, 5):
                    self.copy(stage, flow, kind).wait_recv()
                self.add(stage, flow, 0, low, (1, 2))
                self.add(stage, flow, 0, high, (1, 2))
        yield

    def drain(self):
        for copy in self.open_sends:
            copy.wait_send()
        self.open_sends = []


FF_CHUNK = 512
HALF_CHUNKS = FF // FF_CHUNK // 2
FLOWS_A = (("zxy", 0, 32, 32), ("xyz", 64, 16, 16), ("yzx", 96, 16, 16))
FLOWS_B = (("zxy", 0, 32, 32), ("xyz", 64, 32, 16), ("yzx", 112, 32, 16))
ROWS_A, ROWS_B, ROWS_C = 128, 160, 128


def back_kernel(
    gain_ref, bias_ref, ebias_ref, offsets_ref,
    o2_hbm, x1_hbm, cot_hbm, tok_hbm, mem_hbm, n1_hbm, n2_hbm, o1_hbm,
    heads_hbm, memh_hbm, cqh_hbm, mix1_hbm, mix2_hbm, inv1_hbm, inv2_hbm, exp1_hbm, exp2_hbm,
    qkv_hbm, ckv_hbm, out_hbm, query_hbm, cross_hbm, expand_hbm, reduce_hbm,
    output_ref, gtok_ref, gmem_ref, all_a, all_b, all_c, all_q, all_v, n1_all,
    ring_e, ring_r, cross_w, exp_ref, x1_ref, cot_ref, tok_ref,
    heads_ref, memh_ref, cqh_ref, mix1_ref, mix2_ref, inv1_ref, inv2_ref,
    a_exp, b_exp, a_red, b_red, a_cro, b_cro, a_ckv, b_ckv, a_que, b_que, a_out, b_out,
    spare_exp, dc_ref, acc_ref, dn_ref, expand_sums, vec_ref,
    do2_ref, do1_ref, do2h_ref, do1h_ref, sums_ref, e2_ref, dkv_ref, e1_ref, dkt_ref, dvt_ref,
    grads_a, land_a1, land_a2, land_a3, grads_b, land_b1, land_b2, land_b3,
    piece_a, piece_b, piece_c, weight_ref, weight_in, piece_q, vec_out, vec_in, piece_v,
    load_sems, ring_sems, keep_sems, pair_send, pair_recv, send_sems, recv_sems,
    dp_send, dp_recv, sum_send, sum_recv, free_sem,
):
    place = Place()
    core, y, xl, me, dp = place.core, place.y, place.xl, place.seq, place.dp
    partner = 2 * y + 1 - xl
    own_rows = aligned(me, TOK)
    order = [lax.rem(y + step, 4) for step in (1, 2, 3, 0)]
    mine = pl.ds(pl.multiple_of(core * 512, 512), 512)
    theirs = pl.ds(pl.multiple_of((1 - core) * 512, 512), 512)

    barrier = greet_row()
    for distance in range(1, DP):
        pl.semaphore_signal(
            barrier, inc=1, device_id=(lax.rem(dp + distance, DP), me), device_id_type=MESH
        )
    outer = place.neighbour("x", 2 * xl - 1)
    pl.semaphore_signal(barrier, inc=1, device_id=outer, device_id_type=MESH)

    def load(source, target, sem):
        copy = pltpu.make_async_copy(source, target, load_sems.at[sem])
        copy.start()
        return copy

    def ring_copies(step):
        half, inside = step // HALF_CHUNKS, lax.rem(step, HALF_CHUNKS)
        chunk = jnp.where(half == 0, 1 - core, core) * HALF_CHUNKS + inside
        span = aligned(chunk, FF_CHUNK)
        slot = aligned(inside, FF_CHUNK)
        return (
            pltpu.make_async_copy(expand_hbm.at[:, span], ring_e.at[:, slot], ring_sems.at[inside]),
            pltpu.make_async_copy(
                reduce_hbm.at[span, :], ring_r.at[slot, :], ring_sems.at[HALF_CHUNKS + inside]
            ),
        )

    top = slice(0, TOK)
    loads = [
        load(o2_hbm, a_cro.at[top, :], 0), load(cross_hbm, cross_w, 1), load(x1_hbm, x1_ref, 2),
        load(cot_hbm, cot_ref, 3),
    ]
    for step in range(HALF_CHUNKS):
        for one in ring_copies(step):
            one.start()
    late = [
        load(mem_hbm, a_ckv.at[top, :], 4), load(n2_hbm, a_que.at[top, :], 5),
        load(o1_hbm, a_out.at[top, :], 6), load(tok_hbm, tok_ref, 7),
    ]
    kept = [
        load(memh_hbm, memh_ref, 8), load(cqh_hbm, cqh_ref, 9), load(mix2_hbm, mix2_ref, 10),
        load(inv2_hbm, inv2_ref, 11), load(exp2_hbm, exp_ref, 12),
    ]
    kept1 = [
        load(heads_hbm, heads_ref, 13), load(mix1_hbm, mix1_ref, 14), load(inv1_hbm, inv1_ref, 15),
    ]

    pair_waits = {}

    def give(name, source, target, slot):
        copy = pltpu.make_async_remote_copy(
            src_ref=source,
            dst_ref=target,
            send_sem=pair_send.at[slot],
            recv_sem=pair_recv.at[slot],
            device_id=place.other,
            device_id_type=MESH,
        )
        copy.start()
        pair_waits[name] = copy

    low_half = slice(TOK, 2 * TOK)
    gather = Gather(n1_hbm, n1_all, keep_sems.at[0], send_sems, recv_sems, 64)

    for one in loads[:3]:
        one.wait()
    x2 = x1_ref[...] + dot(a_cro[top, :], cross_w[...]) + bias_ref[8:9, :]
    unit3, inverse3 = norm_unit(x2)
    a_exp[top, :] = (unit3 * gain_ref[2:3, :] + bias_ref[2:3, :]).astype(LOW)
    acc_ref[...] = x2 + bias_ref[9:10, :]
    dn_ref[...] = jnp.zeros_like(dn_ref)
    loads[3].wait()
    b_red[top, :] = cot_ref[:, mine]
    pl.semaphore_wait(barrier, SEQ - 1 + DP - 1 + 1)
    gather.first()
    give("a_exp", a_exp.at[top, :], a_exp.at[low_half, :], 0)
    give("b_red", cot_ref.at[:, theirs], b_red.at[low_half, :], 1)
    give("a_cro", a_cro.at[top, :], a_cro.at[low_half, :], 2)
    root = math.sqrt(2.0 / math.pi)

    def feed(half):
        def body(inside, carry):
            step = half * HALF_CHUNKS + inside
            for one in ring_copies(step):
                one.wait()
            chunk = jnp.where(half == 0, 1 - core, core) * HALF_CHUNKS + inside
            span = aligned(chunk, FF_CHUNK)
            slot = aligned(inside, FF_CHUNK)
            hidden = dot(a_exp[top, :], ring_e[:, slot]) + ebias_ref[:, span]
            square = hidden * hidden
            curve = jnp.tanh(root * hidden * (1.0 + 0.044715 * square))
            share = 0.5 * (1.0 + curve)
            act = (hidden * share).astype(LOW)
            a_red[top, span] = act
            slope = share + 0.5 * hidden * (1.0 - curve * curve) * (
                root * (1.0 + 3.0 * 0.044715 * square)
            )
            acc_ref[...] += dot(act, ring_r[slot, :])
            grad_act = dot_nt(cot_ref[...], ring_r[slot, :])
            grad_hidden = (slope * grad_act).astype(LOW)
            if half == 0:
                spare_exp[:, slot] = grad_hidden
            else:
                b_exp[top, slot] = grad_hidden
            expand_sums[chunk] = column_sum(grad_hidden.astype(F32))
            dn_ref[...] += dot_nt(grad_hidden, ring_e[:, slot])
            if half == 0:
                for one in ring_copies(step + HALF_CHUNKS):
                    one.start()
            return carry

        lax.fori_loop(0, HALF_CHUNKS, body, 0)

    feed(0)
    wide_theirs = pl.ds(pl.multiple_of((1 - core) * 2048, 2048), 2048)
    wide_mine = pl.ds(pl.multiple_of(core * 2048, 2048), 2048)
    give("b_exp", spare_exp, b_exp.at[low_half, :], 3)
    give("a_red0", a_red.at[top, wide_theirs], a_red.at[low_half, wide_theirs], 4)
    gather.second()
    feed(1)
    give("a_red1", a_red.at[top, wide_mine], a_red.at[low_half, wide_mine], 5)
    gather.third()
    later = [load(query_hbm, ring_r.at[1024:2048, :], 16), load(out_hbm, ring_r.at[0:1024, :], 17),
             load(ckv_hbm, ring_e, 18)]
    output_ref[...] = acc_ref[...].astype(LOW)
    dn3 = dn_ref[...]
    grad = cot_ref[...].astype(F32)
    dx2 = grad + norm_back(dn3, unit3, inverse3, gain_ref[2:3, :])
    acc_ref[...] = dx2
    dc_ref[...] = dx2.astype(LOW)
    b_cro[top, :] = dc_ref[:, mine]
    give("b_cro", dc_ref.at[:, theirs], b_cro.at[low_half, :], 6)

    give_do2, give_e2, give_k2, give_v2, give_do1, give_q1, give_k1, give_v1 = (
        Exchange(send_sems, recv_sems, 8 * index) for index in range(8)
    )

    def push_heads(exchange, low_ref, weight_of, values, target, keep_slot):
        for step in range(4):
            at = order[step]
            low_ref[:, aligned(at, 256)] = dot_nt(values, weight_of(aligned(at, 256))).astype(LOW)
            if step < 3:
                for half in range(2):
                    there = 2 * at + half
                    exchange.push(
                        low_ref.at[:, aligned(there, PAIR)], target.at[own_rows, :], there, False
                    )
            else:
                exchange.push(
                    low_ref.at[:, aligned(partner, PAIR)], target.at[own_rows, :], partner, False
                )
        keep = pltpu.make_async_copy(
            low_ref.at[:, aligned(me, PAIR)], target.at[own_rows, :], keep_sems.at[keep_slot]
        )
        keep.start()
        return keep

    keep_do2 = push_heads(
        give_do2, do2_ref, lambda rows: cross_w[rows, :], dc_ref[...], do2h_ref, 1
    )
    vec_ref[2:3, :] = column_sum(dn3 * unit3)
    vec_ref[5:6, :] = column_sum(dn3)
    vec_ref[11:12, :] = column_sum(dc_ref[...].astype(F32))
    vec_ref[12:13, :] = column_sum(grad)

    def put(grads, half_rows, group, result, rows, offset, spread):
        xh, zz = group // 4, lax.rem(group, 4)
        for to in range(2):
            for yy in range(4):
                for col in range(2):
                    for sub in range(spread):
                        at = to * half_rows + offset + sub * rows
                        grads[xh * 2 + col, yy, zz, at : at + rows, :] = result[
                            (to * 4 + yy) * rows : (to * 4 + yy) * rows + rows,
                            (col * spread + sub) * LANES : (col * spread + sub) * LANES + LANES,
                        ]

    def outer(left, right, group, width):
        return dot_tn(left[:, aligned(group, width)], right[...]).astype(LOW)

    def fill_a(group, carry):
        put(grads_a, 64, group, outer(a_exp, b_exp, group, 128), 16, 0, 4)
        return carry

    def fill_b(group, carry):
        put(grads_b, 80, group, outer(a_red, b_red, group, 512), 64, 0, 1)
        put(grads_b, 80, group, outer(a_cro, b_cro, group, 128), 16, 64, 1)
        return carry

    def fill_c(group, carry):
        put(grads_a, 64, group, outer(a_ckv, b_ckv, group, 128), 16, 0, 2)
        put(grads_a, 64, group, outer(a_que, b_que, group, 128), 16, 32, 1)
        put(grads_a, 64, group, outer(a_out, b_out, group, 128), 16, 48, 1)
        return carry

    lands_a = (land_a1, land_a2, land_a3)
    sum_a = Sum(place, grads_a, lands_a, FLOWS_A, sum_send, sum_recv, 0)
    sum_b = Sum(place, grads_b, (land_b1, land_b2, land_b3), FLOWS_B, sum_send, sum_recv, 54)
    sum_c = Sum(place, grads_a, lands_a, FLOWS_A, sum_send, sum_recv, 108)
    run_a, run_b, run_c = sum_a.run(), sum_b.run(), sum_c.run()

    for name in ("a_exp", "b_exp"):
        pair_waits[name].wait_recv()
    lax.fori_loop(0, 8, fill_a, 0)
    next(run_a)
    for name in ("a_red0", "a_red1", "b_red", "a_cro", "b_cro"):
        pair_waits[name].wait_recv()
    lax.fori_loop(0, 8, fill_b, 0)
    next(run_b)
    for one in late:
        one.wait()
    give("a_ckv", a_ckv.at[top, :], a_ckv.at[low_half, :], 7)
    give("a_que", a_que.at[top, :], a_que.at[low_half, :], 8)
    give("a_out", a_out.at[top, :], a_out.at[low_half, :], 9)

    def attend_back(query, key_rows, value_rows, grad_ref, mix_ref, inv_ref, causal, after_tile):
        tile = 256
        scaled = (grad_ref[...].astype(F32) * inv_ref[...]).astype(LOW)
        lanes = head_lanes(ROW)
        product = scaled.astype(F32) * mix_ref[...].astype(F32)
        inner = [jnp.sum(pick_head(product, lanes, head), -1, keepdims=True) for head in range(2)]
        value_t = value_rows.T
        query_t = query.T
        scaled_t = scaled.T
        dkt_ref[...] = jnp.zeros_like(dkt_ref)
        dvt_ref[...] = jnp.zeros_like(dvt_ref)
        tile_lanes = head_lanes(tile)
        steps = range(ROW // tile)
        for step in reversed(steps) if causal else steps:
            rows = slice(step * tile, step * tile + tile)
            width = (step + 1) * tile if causal else ROW
            parts = []
            for head in range(2):
                own = slice(head * HEAD_DIM, head * HEAD_DIM + HEAD_DIM)
                exponent = exp_ref[head, rows, 0:width]
                grad_p = dot(pick_head(scaled[rows, :], tile_lanes, head), value_t[:, 0:width])
                grad_s = (exponent.astype(F32) * (grad_p - inner[head][rows, :])).astype(LOW)
                parts.append(dot(grad_s, key_rows[0:width, :]))
                dkt_ref[own, 0:width] += dot(query_t[own, rows], grad_s)
                dvt_ref[own, 0:width] += dot(scaled_t[own, rows], exponent)
            grad_q = jnp.where(tile_lanes, parts[0], parts[1]).astype(LOW) * SCALE
            sums_ref[rows, 0:PAIR] = grad_q.astype(LOW)
            after_tile(step, rows)

    def send_part(exchange, part, there, target, column):
        exchange.push(
            sums_ref.at[there * TOK : there * TOK + TOK, part * PAIR : part * PAIR + PAIR],
            target.at[:, pl.ds(pl.multiple_of(column + me * PAIR, PAIR), PAIR)], there, True,
        )

    def keep_part(part, target, column, slot):
        copy = pltpu.make_async_copy(
            sums_ref.at[own_rows, part * PAIR : part * PAIR + PAIR],
            target.at[:, pl.ds(pl.multiple_of(column + me * PAIR, PAIR), PAIR)],
            keep_sems.at[slot],
        )
        copy.start()
        return copy

    def from_peers(target, column):
        return lambda sender: target.at[
            :, pl.ds(pl.multiple_of(column + sender * PAIR, PAIR), PAIR)
        ]

    for one in kept:
        one.wait()
    keep_do2.wait()
    give_do2.receive(lambda sender: do2h_ref.at[aligned(sender, TOK), :])

    def after_cross(step, rows):
        for half in range(2):
            send_part(give_e2, 0, 2 * step + half, e2_ref, 0)

    attend_back(
        cqh_ref[...], memh_ref[:, 0:PAIR], memh_ref[:, PAIR : 2 * PAIR], do2h_ref, mix2_ref,
        inv2_ref, False, after_cross,
    )
    keeps = [keep_part(0, e2_ref, 0, 2)]
    sums_ref[:, PAIR : 2 * PAIR] = dkt_ref[...].T.astype(LOW)
    sums_ref[:, 2 * PAIR : 3 * PAIR] = dvt_ref[...].T.astype(LOW)
    for there in range(SEQ):
        send_part(give_k2, 1, there, dkv_ref, 0)
        send_part(give_v2, 2, there, dkv_ref, WIDTH)
    keeps += [keep_part(1, dkv_ref, 0, 3), keep_part(2, dkv_ref, WIDTH, 4)]
    exp1_load = load(exp1_hbm, exp_ref, 19)
    next(run_a)

    keeps[0].wait()
    later[0].wait()
    unit2, inverse2 = norm_unit(x1_ref[...])
    give_e2.receive(from_peers(e2_ref, 0))
    dn2 = dot_nt(e2_ref[...], ring_r[1024:2048, :])
    dx1 = acc_ref[...] + norm_back(dn2, unit2, inverse2, gain_ref[1:2, :])
    acc_ref[...] = dx1
    dc_sent = pair_waits["b_cro"]
    dc_sent.wait_send()
    dc_ref[...] = dx1.astype(LOW)
    later[1].wait()
    keep_do1 = push_heads(
        give_do1, do1_ref, lambda rows: ring_r[rows, :], dc_ref[...], do1h_ref, 5
    )
    next(run_b)
    b_out[top, :] = dc_ref[:, mine]
    b_que[top, :] = e2_ref[:, mine]
    give("b_out", dc_ref.at[:, theirs], b_out.at[low_half, :], 10)
    give("b_que", e2_ref.at[:, theirs], b_que.at[low_half, :], 11)
    vec_ref[1:2, :] = column_sum(dn2 * unit2)
    vec_ref[4:5, :] = column_sum(dn2)
    vec_ref[8:9, :] = column_sum(dc_ref[...].astype(F32))
    vec_ref[9:10, :] = column_sum(e2_ref[...].astype(F32))
    next(run_a)
    keeps[1].wait()
    keeps[2].wait()
    give_k2.receive(from_peers(dkv_ref, 0))
    give_v2.receive(from_peers(dkv_ref, WIDTH))
    kv_mine = aligned(core, WIDTH)
    kv_theirs = aligned(1 - core, WIDTH)
    b_ckv[top, :] = dkv_ref[:, kv_mine]
    give("b_ckv", dkv_ref.at[:, kv_theirs], b_ckv.at[low_half, :], 12)
    later[2].wait()
    gmem_ref[...] = dot_nt(dkv_ref[...], ring_e[...])
    vec_ref[10:11, :] = column_sum(dkv_ref[:, WIDTH : 2 * WIDTH].astype(F32))
    gather.finish()
    last = [
        load(qkv_hbm.at[:, 0 : 2 * WIDTH], ring_e, 20),
        load(qkv_hbm.at[:, 2 * WIDTH : 3 * WIDTH], ring_r.at[0:1024, :], 21),
        load(n1_all, ring_r.at[1024:2048, :], 22),
    ]

    for exchange in (give_e2, give_k2, give_v2):
        exchange.drain()
    for one in kept1:
        one.wait()
    exp1_load.wait()
    keep_do1.wait()
    give_do1.receive(lambda sender: do1h_ref.at[aligned(sender, TOK), :])

    def after_self(step, rows):
        sums_ref[rows, PAIR : 2 * PAIR] = dkt_ref[:, rows].T.astype(LOW)
        sums_ref[rows, 2 * PAIR : 3 * PAIR] = dvt_ref[:, rows].T.astype(LOW)
        for half in range(2):
            for part, exchange in enumerate((give_q1, give_k1, give_v1)):
                send_part(exchange, part, 2 * step + half, e1_ref, part * WIDTH)
        if step == 3:
            next(run_a)
        elif step == 2:
            next(run_b)
        elif step == 1:
            next(run_a)

    attend_back(
        heads_ref[:, 0:PAIR], heads_ref[:, PAIR : 2 * PAIR], heads_ref[:, 2 * PAIR : 3 * PAIR],
        do1h_ref, mix1_ref, inv1_ref, True, after_self,
    )
    keeps = [keep_part(part, e1_ref, part * WIDTH, 6 + part) for part in range(3)]

    last[2].wait()
    for part in range(3):
        value = sums_ref[:, part * PAIR : part * PAIR + PAIR].T
        weight_ref[:, :, part * PAIR : part * PAIR + PAIR] = (
            dot(value, ring_r[1024:2048, :]).T.astype(LOW).reshape(DP, ROW // DP, PAIR)
        )

    def dp_copy(source, target, distance, base):
        there = lax.rem(dp + distance, DP)
        return pltpu.make_async_remote_copy(
            src_ref=source.at[there],
            dst_ref=target.at[dp],
            send_sem=dp_send.at[base + distance],
            recv_sem=dp_recv.at[base + distance],
            device_id=(there, me),
            device_id_type=MESH,
        )

    def dp_receive(target, distance, base):
        sender = lax.rem(dp - distance + DP, DP)
        return pltpu.make_async_remote_copy(
            src_ref=target.at[sender],
            dst_ref=target.at[sender],
            send_sem=dp_send.at[base + distance],
            recv_sem=dp_recv.at[base + distance],
            device_id=(sender, me),
            device_id_type=MESH,
        )

    for distance in range(1, DP):
        dp_copy(weight_ref, weight_in, distance, 0).start()
    next(run_b)
    next(run_a)

    for one in keeps:
        one.wait()
    for one in last[:2]:
        one.wait()
    unit1, inverse1 = norm_unit(tok_ref[...].astype(F32))
    give_q1.receive(from_peers(e1_ref, 0))
    give_k1.receive(from_peers(e1_ref, WIDTH))
    dn1 = dot_nt(e1_ref[:, 0 : 2 * WIDTH], ring_e[...])
    give_v1.receive(from_peers(e1_ref, 2 * WIDTH))
    dn1 = dn1 + dot_nt(e1_ref[:, 2 * WIDTH : 3 * WIDTH], ring_r[0:1024, :])
    gtok_ref[...] = acc_ref[...] + norm_back(dn1, unit1, inverse1, gain_ref[0:1, :])
    vec_ref[0:1, :] = column_sum(dn1 * unit1)
    vec_ref[3:4, :] = column_sum(dn1)
    vec_ref[6:7, :] = column_sum(e1_ref[:, 0:WIDTH].astype(F32))
    vec_ref[7:8, :] = column_sum(e1_ref[:, 2 * WIDTH : 3 * WIDTH].astype(F32))

    vec_out[...] = jnp.zeros_like(vec_out)
    for owner in range(DP):
        vec_out[owner, 0:13, 0:64] = vec_ref[0:13, owner * 64 : owner * 64 + 64]
        for half in range(2):
            at = (owner % 2) * 256 + half * PAIR
            vec_out[owner, 13 + half : 14 + half, :] = expand_sums[owner // 2, :, at : at + PAIR]
    for distance in range(1, DP):
        dp_copy(vec_out, vec_in, distance, DP).start()

    def join(grads, piece, half_rows, slot):
        block = grads.at[place.at["x"], place.at["y"], place.at["z"]]
        copy = pltpu.make_async_remote_copy(
            src_ref=block.at[aligned(1 - core, half_rows), :],
            dst_ref=piece.at[core],
            send_sem=pair_send.at[slot],
            recv_sem=pair_recv.at[slot],
            device_id=place.other,
            device_id_type=MESH,
        )
        copy.start()
        keep = pltpu.make_async_copy(
            block.at[aligned(core, half_rows), :], piece.at[core], keep_sems.at[slot]
        )
        keep.start()
        return keep, copy

    spreads = []

    def spread(piece, whole, base, slot):
        exchange = Exchange(send_sems, recv_sems, base)
        for distance in range(1, SEQ):
            exchange.push(piece, whole.at[me], lax.rem(me + distance, SEQ), False)
        keep = pltpu.make_async_copy(piece, whole.at[me], keep_sems.at[slot])
        keep.start()
        spreads.append((exchange, keep, whole))

    next(run_a)
    joined_a = join(grads_a, piece_a, 64, 13)
    for one in joined_a:
        one.wait()
    spread(piece_a, all_a, 69, 16)
    sum_a.drain()
    for axis in "xyz":
        for step in (1, -1):
            pl.semaphore_signal(
                free_sem, inc=1, device_id=place.neighbour(axis, step), device_id_type=MESH
            )
    for name in ("a_ckv", "b_ckv", "a_que", "b_que", "a_out", "b_out"):
        pair_waits[name].wait_recv()
    lax.fori_loop(0, 8, fill_c, 0)
    pl.semaphore_wait(free_sem, 6)
    next(run_c)
    next(run_b)
    next(run_b)
    next(run_c)
    next(run_b)
    joined_b = join(grads_b, piece_b, 80, 14)
    next(run_c)

    for distance in range(1, DP):
        dp_receive(weight_in, distance, 0).wait_recv()
    total = weight_ref[dp].astype(F32)
    for distance in range(1, DP):
        total = total + weight_in[lax.rem(dp + distance, DP)].astype(F32)
    piece_q[...] = total.astype(LOW)
    spread(piece_q, all_q, 77, 17)
    for distance in range(1, DP):
        dp_receive(vec_in, distance, DP).wait_recv()
    total = vec_out[dp]
    for distance in range(1, DP):
        total = total + vec_in[lax.rem(dp + distance, DP)]
    piece_v[...] = total
    spread(piece_v, all_v, 85, 18)
    for one in joined_b:
        one.wait()
    spread(piece_b, all_b, 93, 19)
    next(run_c)
    next(run_c)
    next(run_c)
    next(run_c)
    joined_c = join(grads_a, piece_c, 64, 15)
    for one in joined_c:
        one.wait()
    spread(piece_c, all_c, 101, 20)

    for exchange, keep, whole in spreads:
        keep.wait()
        exchange.receive(lambda sender, whole=whole: whole.at[sender])
        exchange.drain()
    for exchange in (give_do2, give_do1, give_q1, give_k1, give_v1):
        exchange.drain()
    for name, copy in pair_waits.items():
        if name != "b_cro":
            copy.wait_send()
    for distance in range(1, DP):
        dp_copy(weight_ref, weight_in, distance, 0).wait_send()
        dp_copy(vec_out, vec_in, distance, DP).wait_send()
    sum_b.drain()
    sum_c.drain()


def back_call(operands):
    dma = pltpu.SemaphoreType.DMA
    vmem = pltpu.VMEM
    token = vmem((TOK, WIDTH), LOW)
    token_wide = vmem((TOK, WIDTH), F32)
    heads = vmem((ROW, PAIR), LOW)
    inverse = vmem((ROW, PAIR), F32)
    both = vmem((2 * TOK, WIDTH), LOW)
    both_half = vmem((2 * TOK, 512), LOW)

    def sums(rows):
        return [
            vmem((4, 4, 4, rows, LANES), LOW), vmem((3, 4, 4, rows, LANES), LOW),
            vmem((3, 4, rows, LANES), LOW), vmem((3, rows, LANES), LOW),
        ]

    return pl.pallas_call(
        back_kernel,
        out_shape=(
            shaped((TOK, WIDTH)), shaped((TOK, WIDTH), F32), shaped((TOK, WIDTH), F32),
            shaped((SEQ, 2, 64, LANES)), shaped((SEQ, 2, 80, LANES)), shaped((SEQ, 2, 64, LANES)),
            shaped((SEQ, 64, 3 * PAIR)), shaped((SEQ, 16, PAIR), F32), shaped((ROW, WIDTH)),
        ),
        in_specs=[spec_vmem()] * 3 + [spec_smem()] + [spec_any()] * 24,
        out_specs=(spec_vmem(),) * 3 + (spec_any(),) * 6,
        scratch_shapes=[
            vmem((WIDTH, 2 * WIDTH), LOW), vmem((2 * WIDTH, WIDTH), LOW), vmem((WIDTH, WIDTH), LOW),
            vmem((2, ROW, ROW), LOW), token_wide, token, token,
            vmem((ROW, 3 * PAIR), LOW), vmem((ROW, 2 * PAIR), LOW), heads, heads, heads, inverse,
            inverse,
            both, vmem((2 * TOK, 2048), LOW), vmem((2 * TOK, FF), LOW), both_half, both, both_half,
            both, both, both, both_half, both, both_half,
            vmem((TOK, 2048), LOW), token, token_wide, token_wide,
            vmem((FF // FF_CHUNK, 1, FF_CHUNK), F32), vmem((16, WIDTH), F32),
            token, token, heads, heads, vmem((ROW, 3 * PAIR), LOW), token,
            vmem((TOK, 2 * WIDTH), LOW), vmem((TOK, 3 * WIDTH), LOW),
            vmem((PAIR, ROW), F32), vmem((PAIR, ROW), F32),
        ]
        + sums(ROWS_A) + sums(ROWS_B)
        + [
            vmem((2, 64, LANES), LOW), vmem((2, 80, LANES), LOW), vmem((2, 64, LANES), LOW),
            vmem((DP, ROW // DP, 3 * PAIR), LOW), vmem((DP, ROW // DP, 3 * PAIR), LOW),
            vmem((64, 3 * PAIR), LOW), vmem((DP, 16, PAIR), F32), vmem((DP, 16, PAIR), F32),
            vmem((16, PAIR), F32),
            dma((23,)), dma((8,)), dma((21,)), dma((16,)), dma((16,)), dma((109,)), dma((109,)),
            dma((32,)), dma((32,)), dma((162,)), dma((162,)), pltpu.SemaphoreType.REGULAR,
        ],
        compiler_params=pltpu.CompilerParams(
            collective_id=3, has_side_effects=True, vmem_limit_bytes=63 * MIB
        ),
        cost_estimate=pl.CostEstimate(
            flops=2 * TOK * WIDTH * 27 * WIDTH, bytes_accessed=100 * MIB, transcendentals=0
        ),
        name="back",
    )(*operands)


def finish_kernel(
    a_ref, b_ref, c_ref, q_ref, vec_ref,
    gqkv_ref, gout_ref, gque_ref, gckv_ref, gcro_ref, gexp_ref, gred_ref, ggain_ref, gbias_ref,
    gebias_ref,
):
    for seq in range(SEQ):
        y, xl = seq // 2, seq % 2
        rows = slice(16 * y, 16 * y + 16)
        for col in range(2):
            for sub in range(4):
                at = col * 2048 + xl * 1024 + sub * LANES
                gexp_ref[rows, at : at + LANES] = a_ref[
                    seq, col, sub * 16 : sub * 16 + 16, :
                ].astype(F32)
            for sub in range(2):
                at = col * 1024 + xl * 512 + sub * LANES
                gckv_ref[rows, at : at + LANES] = c_ref[
                    seq, col, sub * 16 : sub * 16 + 16, :
                ].astype(F32)
            at = col * 512 + xl * LANES
            own = slice(at, at + LANES)
            gred_ref[64 * y : 64 * y + 64, own] = b_ref[seq, col, 0:64, :].astype(F32)
            gcro_ref[rows, own] = b_ref[seq, col, 64:80, :].astype(F32)
            gque_ref[rows, own] = c_ref[seq, col, 32:48, :].astype(F32)
            gout_ref[rows, own] = c_ref[seq, col, 48:64, :].astype(F32)
        for part in range(3):
            at = part * WIDTH + seq * PAIR
            gqkv_ref[:, at : at + PAIR] = q_ref[seq, :, part * PAIR : (part + 1) * PAIR].astype(F32)
    total = vec_ref[0]
    for seq in range(1, SEQ):
        total = total + vec_ref[seq]
    ggain_ref[...] = total[0:3, 0:64]
    gbias_ref[...] = total[3:13, 0:64]
    gebias_ref[:, 0:PAIR] = total[13:14, :]
    gebias_ref[:, PAIR : 2 * PAIR] = total[14:15, :]


def on_device(
    tokens, memory, cotangent, offsets, memory_ids, pair_map, self_qkv, self_out, cross_query,
    cross_kv, cross_out, expand_weight, expand_bias, reduce_weight, norm_gains, bias_rows,
):
    tok = tokens.reshape(TOK, WIDTH)
    mem = memory.reshape(TOK, WIDTH)
    cot = cotangent.reshape(TOK, WIDTH)
    (
        x1, n2, o1, o2, heads, mem_heads, cq, mix1, mix2, inv1, inv2, n1, exp1, exp2,
    ) = front_call(
        (tok, mem, norm_gains, bias_rows, memory_ids, offsets, pair_map, self_qkv, cross_kv,
         self_out, cross_query)
    )
    output, gtok, gmem, all_a, all_b, all_c, all_q, all_v, _ = back_call(
        (norm_gains, bias_rows, expand_bias.reshape(1, FF), offsets,
         o2, x1, cot, tok, mem, n1, n2, o1, heads, mem_heads, cq, mix1, mix2, inv1, inv2, exp1, exp2,
         self_qkv, cross_kv, self_out, cross_query, cross_out, expand_weight, reduce_weight)
    )
    gqkv, gout, gque, gckv, gcro, gexp, gred, ggain, gbias, gebias = local_call(
        finish_kernel,
        (
            shaped((64, 3 * WIDTH), F32), shaped((64, WIDTH), F32), shaped((64, WIDTH), F32),
            shaped((64, 2 * WIDTH), F32), shaped((64, WIDTH), F32), shaped((64, FF), F32),
            shaped((256, WIDTH), F32), shaped((3, 64), F32), shaped((10, 64), F32),
            shaped((1, 256), F32),
        ),
        [spec_vmem()] * 5, [], "finish", 0, 8 * MIB,
    )(all_a, all_b, all_c, all_q, all_v)
    return (
        output.reshape(1, TOK, WIDTH), gtok.reshape(1, TOK, WIDTH), gmem.reshape(1, TOK, WIDTH),
        gqkv, gout, gque, gckv, gcro, gexp, gebias.reshape(256), gred, ggain, gbias,
    )


def solution(mesh):
    row = P("dp", "seq", None)
    split = P("dp", None)
    in_specs = (row,) * 3 + (split,) * 3 + (P(),) * 10
    out_specs = (row,) * 3 + (split,) * 6 + (P("dp"), split, P(None, "dp"), P(None, "dp"))
    return jax.shard_map(
        on_device, mesh=mesh, in_specs=in_specs, out_specs=out_specs, check_vma=False
    )
```

```python
import functools
import math

import jax
import jax.numpy as jnp
from jax import lax
from jax.experimental import pallas as pl
from jax.experimental.pallas import tpu as pltpu
from jax.sharding import PartitionSpec as P

HEADS = 16
HEAD_DIM = 64
WIDTH = 1024
TOK = 128
ROW = 1024
FF = 4096
SEQ = 8
DP = 16
PAIR = 128
NEG_FILL = -1e30
EPS = 1e-05
SCALE = HEAD_DIM ** (-0.5)
LOW = jnp.bfloat16
F32 = jnp.float32
MESH = pl.DeviceIdType.MESH
MIB = 2**20


def dot(left, right):
    return lax.dot_general(left, right, (((1,), (0,)), ((), ())), preferred_element_type=F32)


def dot_nt(left, right):
    return lax.dot_general(left, right, (((1,), (1,)), ((), ())), preferred_element_type=F32)


def dot_tn(left, right):
    return lax.dot_general(left, right, (((0,), (0,)), ((), ())), preferred_element_type=F32)


def norm_unit(values):
    average = jnp.mean(values, -1, keepdims=True)
    centered = values - average
    inverse = lax.rsqrt(jnp.mean(centered * centered, -1, keepdims=True) + EPS)
    return centered * inverse, inverse


def norm_back(incoming, unit, inverse, gain_row):
    scaled = incoming * gain_row
    return inverse * (
        scaled
        - jnp.mean(scaled, -1, keepdims=True)
        - unit * jnp.mean(scaled * unit, -1, keepdims=True)
    )


def column_sum(values):
    return jnp.sum(values, 0, keepdims=True)


def spec_any():
    return pl.BlockSpec(memory_space=pl.ANY)


def spec_vmem():
    return pl.BlockSpec(memory_space=pltpu.VMEM)


def spec_smem():
    return pl.BlockSpec(memory_space=pltpu.SMEM)


def shaped(shape, kind=LOW):
    return jax.ShapeDtypeStruct(shape, kind)


def head_lanes(rows):
    return lax.broadcasted_iota(jnp.int32, (rows, PAIR), 1) < HEAD_DIM


def pick_head(values, lanes, head):
    zero = jnp.zeros_like(values)
    return jnp.where(lanes, values, zero) if head == 0 else jnp.where(lanes, zero, values)


def attend_tile(query, key_t, value, allowed, exp_ref, rows, width):
    lanes = head_lanes(query.shape[0])
    mixed, inverses = [], []
    for head in range(2):
        scores = dot(pick_head(query, lanes, head), key_t)
        scores = jnp.where(allowed, scores, NEG_FILL)
        top = jnp.max(scores, -1, keepdims=True)
        exponent = jnp.exp(scores - top)
        inverse = 1.0 / jnp.sum(exponent, -1, keepdims=True)
        low = exponent.astype(LOW)
        exp_ref[head, rows, 0:width] = low
        mixed.append(dot(low, value))
        inverses.append(inverse)
    inverse = jnp.where(lanes, inverses[0], inverses[1])
    return jnp.where(lanes, mixed[0], mixed[1]) * inverse, inverse


def self_allowed(offsets_ref, step, tile, width):
    places = lax.broadcasted_iota(jnp.int32, (tile, 1), 0) + step * tile
    begin = jnp.zeros((tile, 1), jnp.int32)
    for seg in range(1, 16):
        offset = offsets_ref[0, seg]
        begin = jnp.where(places >= offset, offset, begin)
    keys = lax.broadcasted_iota(jnp.int32, (tile, width), 1)
    return (keys <= places) & (keys >= begin)


def cross_allowed(ids, offsets_ref, pair_ref, step, tile):
    places = lax.broadcasted_iota(jnp.int32, (tile, 1), 0) + step * tile
    reads = jnp.zeros((tile, 1), jnp.int32) + pair_ref[0, 0]
    for seg in range(1, 16):
        reads = jnp.where(places >= offsets_ref[0, seg], pair_ref[0, seg], reads)
    return ids == reads


def aligned(index, unit):
    return pl.ds(pl.multiple_of(index * unit, unit), unit)


class Exchange:
    def __init__(self, send_sems, recv_sems, base):
        self.dp = lax.axis_index("dp")
        self.me = lax.axis_index("seq")
        self.send_sems, self.recv_sems, self.base = send_sems, recv_sems, base
        self.sent = []

    def copy(self, source, target, there, distance):
        return pltpu.make_async_remote_copy(
            src_ref=source,
            dst_ref=target,
            send_sem=self.send_sems.at[self.base + distance],
            recv_sem=self.recv_sems.at[self.base + distance],
            device_id=(self.dp, there),
            device_id_type=MESH,
        )

    def push(self, source, target, there, may_be_own):
        distance = lax.rem(there - self.me + SEQ, SEQ)
        if may_be_own:
            remote = there != self.me

            @pl.when(remote)
            def _():
                self.copy(source, target, there, distance).start()

        else:
            self.copy(source, target, there, distance).start()
        self.sent.append((source, target))

    def receive(self, place):
        for distance in range(1, SEQ):
            sender = lax.rem(self.me - distance + SEQ, SEQ)
            spot = place(sender)
            self.copy(spot, spot, sender, distance).wait_recv()

    def drain(self):
        source, target = self.sent[0]
        for distance in range(1, SEQ):
            there = lax.rem(self.me + distance, SEQ)
            self.copy(source, target, there, distance).wait_send()


def greet_row():
    dp = lax.axis_index("dp")
    me = lax.axis_index("seq")
    barrier = pltpu.get_barrier_semaphore()
    for distance in range(1, SEQ):
        pl.semaphore_signal(
            barrier, inc=1, device_id=(dp, lax.rem(me + distance, SEQ)), device_id_type=MESH
        )
    return barrier


class Gather:
    def __init__(self, block, whole, local_sem, send_sems, recv_sems, base):
        self.dp = lax.axis_index("dp")
        self.me = lax.axis_index("seq")
        self.y, self.xl = self.me // 2, lax.rem(self.me, 2)
        self.whole, self.send_sems, self.recv_sems, self.base = whole, send_sems, recv_sems, base
        self.own = pltpu.make_async_copy(block, whole.at[aligned(self.me, TOK), :], local_sem)
        self.block = block

    def part(self, y, xl):
        return self.whole.at[aligned(lax.rem(y + 8, 4) * 2 + xl, TOK), :]

    def copy(self, source, target, there, slot):
        return pltpu.make_async_remote_copy(
            src_ref=source,
            dst_ref=target,
            send_sem=self.send_sems.at[self.base + slot],
            recv_sem=self.recv_sems.at[self.base + slot],
            device_id=(self.dp, there),
            device_id_type=MESH,
        )

    def beside(self, step):
        return lax.rem(self.y + step + 4, 4) * 2 + self.xl

    def send(self, slot):
        y, xl = self.y, self.xl
        if slot == 0:
            return self.copy(self.block, self.part(y, xl), y * 2 + 1 - xl, 0)
        step = 1 if slot % 2 else -1
        if slot < 3:
            return self.copy(self.block, self.part(y, xl), self.beside(step), slot)
        spot = self.part(y, 1 - xl) if slot < 5 else self.part(y - step, xl if step == 1 else 1 - xl)
        return self.copy(spot, spot, self.beside(step), slot)

    def arrive(self, slot):
        y, xl = self.y, self.xl
        if slot == 0:
            spot = self.part(y, 1 - xl)
        else:
            step = 1 if slot % 2 else -1
            if slot < 5:
                spot = self.part(y - step, xl if slot < 3 else 1 - xl)
            else:
                spot = self.part(y + 2, xl if step == 1 else 1 - xl)
        self.copy(spot, spot, self.beside(1), slot).wait_recv()

    def first(self):
        self.own.start()
        for slot in range(3):
            self.send(slot).start()

    def second(self):
        self.arrive(0)
        for slot in (3, 4):
            self.send(slot).start()

    def third(self):
        self.arrive(1)
        self.send(5).start()
        self.arrive(4)
        self.send(6).start()

    def finish(self):
        for slot in (2, 3, 5, 6):
            self.arrive(slot)
        self.own.wait()
        for slot in range(7):
            self.send(slot).wait_send()


class Column:
    def __init__(self, block, spot, local_sem, send_sems, recv_sems, base):
        self.dp, self.me = lax.axis_index("dp"), lax.axis_index("seq")
        self.z = lax.rem(self.dp // 2, 4)
        self.block, self.spot, self.local_sem = block, spot, local_sem
        self.send_sems, self.recv_sems, self.base = send_sems, recv_sems, base

    def at(self, step):
        return self.spot(lax.rem(self.z + step + 4, 4))

    def copy(self, source, target, step, slot):
        there = self.dp + 2 * (lax.rem(self.z + step + 4, 4) - self.z)
        return pltpu.make_async_remote_copy(
            src_ref=source,
            dst_ref=target,
            send_sem=self.send_sems.at[self.base + slot],
            recv_sem=self.recv_sems.at[self.base + slot],
            device_id=(there, self.me),
            device_id_type=MESH,
        )

    def own(self):
        return pltpu.make_async_copy(self.block, self.at(0), self.local_sem)

    def half(self, step, slot):
        return self.at(step).at[pl.ds(0 if slot == 2 else TOK // 2, TOK // 2), :]

    def first(self):
        if self.local_sem is not None:
            self.own().start()
        self.copy(self.block, self.at(0), 1, 0).start()
        self.copy(self.block, self.at(0), -1, 1).start()

    def second(self):
        for slot, step in ((0, 1), (1, -1)):
            self.copy(self.block, self.at(-step), step, slot).wait_recv()
            piece = self.half(-step, slot + 2)
            self.copy(piece, piece, step, slot + 2).start()

    def near(self):
        for slot, step in ((0, 1), (1, -1)):
            self.copy(self.block, self.at(-step), step, slot).wait_recv()
            self.copy(self.block, self.at(0), step, slot).wait_send()
        self.own().wait()

    def forward(self):
        for slot, step in ((0, 1), (1, -1)):
            piece = self.half(-step, slot + 2)
            self.copy(piece, piece, step, slot + 2).start()

    def far(self):
        for slot, step in ((0, 1), (1, -1)):
            piece = self.half(2, slot + 2)
            self.copy(piece, piece, step, slot + 2).wait_recv()
            piece = self.half(-step, slot + 2)
            self.copy(piece, piece, step, slot + 2).wait_send()

    def finish(self):
        self.far()
        for slot, step in ((0, 1), (1, -1)):
            self.copy(self.block, self.at(0), step, slot).wait_send()
        if self.local_sem is not None:
            self.own().wait()


def front_kernel(
    tok_ref, mem_ref, cot_ref, gain_ref, bias_ref, ids_ref, offsets_ref, pair_ref,
    qkv_hbm, ckv_hbm, out_hbm, query_hbm,
    x1_ref, n2_ref, o1_ref, o2_ref, heads_ref, memh_ref, cqh_ref, mix1_ref, mix2_ref,
    inv1_ref, inv2_ref, n1_ref, exp1_hbm, exp2_hbm, cot_all, mem_all, n2_all, o1_all,
    qkv_w, ckv_w, out_w, query_w, give_heads, give_mem, cq_ref, exp1_ref, exp2_ref,
    load_sems, keep_sems, exp_sems, send_sems, recv_sems,
):
    me = lax.axis_index("seq")
    y, xl = me // 2, lax.rem(me, 2)
    dp = lax.axis_index("dp")
    barrier = greet_row()
    for step in (1, 2, 3):
        z = lax.rem(dp // 2, 4)
        there = dp + 2 * (lax.rem(z + step, 4) - z)
        pl.semaphore_signal(barrier, inc=1, device_id=(there, me), device_id_type=MESH)
    order = [lax.rem(y + step, 4) for step in (1, 2, 3, 0)]
    loads = {}
    for step in range(4):
        for part in range(3):
            cols = pl.ds(pl.multiple_of(part * WIDTH + order[step] * 256, 256), 256)
            loads["qkv", step, part] = pltpu.make_async_copy(
                qkv_hbm.at[:, cols], qkv_w.at[:, cols], load_sems.at[step * 3 + part]
            )
    for step in range(4):
        for part in range(2):
            cols = pl.ds(pl.multiple_of(part * WIDTH + order[step] * 256, 256), 256)
            loads["ckv", step, part] = pltpu.make_async_copy(
                ckv_hbm.at[:, cols], ckv_w.at[:, cols], load_sems.at[12 + step * 2 + part]
            )
    loads["out"] = pltpu.make_async_copy(out_hbm, out_w, load_sems.at[20])
    loads["query"] = pltpu.make_async_copy(query_hbm, query_w, load_sems.at[21])
    for name, one in loads.items():
        if name[0] == "qkv":
            one.start()

    give_qkv, give_kv, back1, give_q, back2 = (
        Exchange(send_sems, recv_sems, 8 * index) for index in range(5)
    )
    own_rows = aligned(me, TOK)
    columns = [
        Column(
            block, lambda at, whole=whole: whole.at[at], keep_sems.at[7 + index],
            send_sems, recv_sems, 40 + 4 * index,
        )
        for index, (block, whole) in enumerate(
            ((cot_ref, cot_all), (mem_ref, mem_all), (o1_ref, o1_all), (n2_ref, n2_all))
        )
    ]

    unit, _ = norm_unit(tok_ref[...].astype(F32))
    n1 = (unit * gain_ref[0:1, :] + bias_ref[0:1, :]).astype(LOW)
    n1_ref[...] = n1
    mem = mem_ref[...]
    for kind, count, source, give, heads, exchange in (
        ("qkv", 3, n1, give_heads, heads_ref, give_qkv),
        ("ckv", 2, mem, give_mem, memh_ref, give_kv),
    ):
        for step in range(4):
            at = order[step]
            own = aligned(at, 256)
            for part in range(count):
                loads[kind, step, part].wait()
                cols = pl.ds(pl.multiple_of(part * WIDTH + at * 256, 256), 256)
                if kind == "qkv":
                    value = dot(source, qkv_w[:, cols])
                    if part == 0:
                        value = (value + bias_ref[3:4, own]) * SCALE
                    elif part == 2:
                        value = value + bias_ref[4:5, own]
                else:
                    value = dot(source, ckv_w[:, cols])
                    if part == 1:
                        value = value + bias_ref[7:8, own]
                low = value.astype(LOW)
                give[2 * at, :, part * PAIR : part * PAIR + PAIR] = low[:, :PAIR]
                give[2 * at + 1, :, part * PAIR : part * PAIR + PAIR] = low[:, PAIR:]
            if kind == "qkv" and step == 0:
                for name, one in loads.items():
                    if name[0] != "qkv":
                        one.start()
                pl.semaphore_wait(barrier, SEQ - 1 + 3)
                columns[0].first()
                columns[1].first()
            there = heads.at[own_rows, :]
            if step < 3:
                exchange.push(give.at[2 * at], there, 2 * at, False)
                exchange.push(give.at[2 * at + 1], there, 2 * at + 1, False)
            else:
                partner = 2 * y + 1 - xl
                exchange.push(give.at[partner], there, partner, False)
                keep = pltpu.make_async_copy(
                    give.at[me], there, keep_sems.at[2 if kind == "qkv" else 3]
                )
                keep.start()
                loads[kind] = keep

    def attended(allowed_of, query_of, key_t, value_ref, value_at, mix_ref, inv_ref, exp_ref,
                 exp_hbm, exp_base, causal, back, target_ref, keep_sem):
        tile = 256
        for step in range(ROW // tile):
            rows = slice(step * tile, step * tile + tile)
            width = (step + 1) * tile if causal else ROW
            mixture, inverse = attend_tile(
                query_of(rows), key_t[:, 0:width], value_ref[0:width, value_at], allowed_of(step, width),
                exp_ref, rows, width,
            )
            mix_ref[rows, :] = mixture.astype(LOW)
            inv_ref[rows, :] = inverse
            for half in range(2):
                there = 2 * step + half
                back.push(
                    mix_ref.at[there * TOK : there * TOK + TOK, :],
                    target_ref.at[:, aligned(me, PAIR)], there, True,
                )
            for head in range(2):
                spot = (head, rows, slice(0, width))
                pltpu.make_async_copy(
                    exp_ref.at[spot], exp_hbm.at[spot], exp_sems.at[exp_base + step * 2 + head]
                ).start()
        keep = pltpu.make_async_copy(
            mix_ref.at[own_rows, :], target_ref.at[:, aligned(me, PAIR)], keep_sem
        )
        keep.start()
        return keep

    loads["qkv"].wait()
    give_qkv.receive(lambda sender: heads_ref.at[aligned(sender, TOK), :])
    key_t = heads_ref[:, PAIR : 2 * PAIR].T
    keep1 = attended(
        lambda step, width: self_allowed(offsets_ref, step, 256, width),
        lambda rows: heads_ref[rows, 0:PAIR], key_t, heads_ref, slice(2 * PAIR, 3 * PAIR),
        mix1_ref, inv1_ref, exp1_ref, exp1_hbm, 0, True, back1, o1_ref, keep_sems.at[4],
    )
    columns[0].second()
    columns[1].second()
    keep1.wait()
    loads["out"].wait()
    back1.receive(lambda sender: o1_ref.at[:, aligned(sender, PAIR)])
    columns[2].first()
    x1 = tok_ref[...].astype(F32) + dot(o1_ref[...], out_w[...]) + bias_ref[5:6, :]
    x1_ref[...] = x1
    unit, _ = norm_unit(x1)
    n2 = (unit * gain_ref[1:2, :] + bias_ref[1:2, :]).astype(LOW)
    n2_ref[...] = n2
    columns[3].first()
    loads["query"].wait()
    for step in range(4):
        at = order[step]
        own = aligned(at, 256)
        cq_ref[:, own] = ((dot(n2, query_w[:, own]) + bias_ref[6:7, own]) * SCALE).astype(LOW)
        for half in range(2):
            there = 2 * at + half if step < 3 else 2 * y + 1 - xl
            if step == 3 and half == 1:
                continue
            give_q.push(cq_ref.at[:, aligned(there, PAIR)], cqh_ref.at[own_rows, :], there, False)
    keep = pltpu.make_async_copy(cq_ref.at[:, aligned(me, PAIR)], cqh_ref.at[own_rows, :], keep_sems.at[5])
    keep.start()
    loads["ckv"].wait()
    give_kv.receive(lambda sender: memh_ref.at[aligned(sender, TOK), :])
    key_t = memh_ref[:, 0:PAIR].T
    keep.wait()
    give_q.receive(lambda sender: cqh_ref.at[aligned(sender, TOK), :])
    ids = ids_ref[...]
    keep2 = attended(
        lambda step, width: cross_allowed(ids, offsets_ref, pair_ref, step, 256),
        lambda rows: cqh_ref[rows, :], key_t, memh_ref, slice(PAIR, 2 * PAIR),
        mix2_ref, inv2_ref, exp2_ref, exp2_hbm, 8, False, back2, o2_ref, keep_sems.at[6],
    )
    keep2.wait()
    back2.receive(lambda sender: o2_ref.at[:, aligned(sender, PAIR)])
    for step in range(4):
        rows = slice(step * 256, step * 256 + 256)
        for head in range(2):
            spot = (head, rows, slice(0, step * 256 + 256))
            pltpu.make_async_copy(
                exp1_ref.at[spot], exp1_hbm.at[spot], exp_sems.at[step * 2 + head]
            ).wait()
            spot = (head, rows, slice(0, ROW))
            pltpu.make_async_copy(
                exp2_ref.at[spot], exp2_hbm.at[spot], exp_sems.at[8 + step * 2 + head]
            ).wait()
    for exchange in (give_qkv, give_kv, back1, give_q, back2):
        exchange.drain()
    for column in columns[:2]:
        column.finish()
    for column in columns[2:]:
        column.near()


def front_call(operands):
    dma = pltpu.SemaphoreType.DMA
    vmem = pltpu.VMEM
    heads = shaped((ROW, PAIR))
    token = shaped((TOK, WIDTH))
    inverse = shaped((ROW, PAIR), F32)
    exps = shaped((2, ROW, ROW))
    four = shaped((4, TOK, WIDTH))
    return pl.pallas_call(
        front_kernel,
        out_shape=(
            shaped((TOK, WIDTH), F32), token, token, token, shaped((ROW, 3 * PAIR)),
            shaped((ROW, 2 * PAIR)), heads, heads, heads, inverse, inverse, token,
            exps, exps, four, four, four, four,
        ),
        in_specs=[spec_vmem()] * 6 + [spec_smem()] * 2 + [spec_any()] * 4,
        out_specs=(spec_vmem(),) * 12 + (spec_any(),) * 6,
        scratch_shapes=[
            vmem((WIDTH, 3 * WIDTH), LOW), vmem((WIDTH, 2 * WIDTH), LOW), vmem((WIDTH, WIDTH), LOW),
            vmem((WIDTH, WIDTH), LOW), vmem((SEQ, TOK, 3 * PAIR), LOW), vmem((SEQ, TOK, 2 * PAIR), LOW),
            vmem((TOK, WIDTH), LOW), vmem((2, ROW, ROW), LOW), vmem((2, ROW, ROW), LOW),
            dma((22,)), dma((11,)), dma((16,)), dma((56,)), dma((56,)),
        ],
        compiler_params=pltpu.CompilerParams(
            collective_id=2, has_side_effects=True, vmem_limit_bytes=56 * MIB
        ),
        cost_estimate=pl.CostEstimate(
            flops=2 * TOK * WIDTH * 7 * WIDTH, bytes_accessed=60 * MIB, transcendentals=0
        ),
        name="front",
    )(*operands)


LANES = 256


def wrap(index):
    return lax.rem(index + 8, 4)


def device_of(core, x, y, z):
    return ((x // 2) * 8 + z * 2 + core, y * 2 + lax.rem(x, 2))


class Place:
    def __init__(self):
        self.dp = lax.axis_index("dp")
        self.seq = lax.axis_index("seq")
        self.core = lax.rem(self.dp, 2)
        self.y, self.xl = self.seq // 2, lax.rem(self.seq, 2)
        self.at = {
            "x": (self.dp // 8) * 2 + self.xl,
            "y": self.y,
            "z": lax.rem(self.dp // 2, 4),
        }
        self.z = self.at["z"]
        self.other = (self.dp + 1 - 2 * self.core, self.seq)
        self.rank = lax.rem(self.dp, 8)

    def member(self, distance):
        rank = lax.rem(self.rank + distance + 8, 8)
        return (self.dp - self.rank + rank, self.seq), rank

    def neighbour(self, axis, step):
        at = dict(self.at)
        at[axis] = wrap(at[axis] + step)
        return device_of(self.core, **at)


class Sum:
    def __init__(self, place, grads, lands, flows, send_sems, recv_sems, base):
        self.place, self.grads, self.lands, self.flows = place, grads, lands, flows
        self.send_sems, self.recv_sems, self.base = send_sems, recv_sems, base
        self.open_sends = []

    def view(self, order, stage, block, first, rows):
        index = {"x": slice(None), "y": slice(None)}
        for done in range(stage):
            index[order[done]] = self.place.at[order[done]]
        index[order[stage]] = block
        return (index["x"], index["y"], slice(first, first + rows), slice(None))

    def land(self, stage, slot, first, rows):
        return (slot,) + (slice(None),) * (1 - stage) + (slice(first, first + rows), slice(None))

    def spans(self, flow):
        order, first, low, high = self.flows[flow]
        return order, (first, low), (first + low, high)

    def copy(self, stage, flow, kind):
        order, low, high = self.spans(flow)
        axis = order[stage]
        step = (2, 2, 1, -1, 1, -1)[kind]
        way = (1, -1, 1, -1, 1, -1)[kind]
        first, rows = (low, high, high, low, low, high)[kind]
        slot = (0, 0, 1, 1, 2, 2)[kind]
        at = self.base + (stage * len(self.flows) + flow) * 6 + kind
        return pltpu.make_async_remote_copy(
            src_ref=self.grads.at[
                self.view(order, stage, wrap(self.place.at[axis] + step), first, rows)
            ],
            dst_ref=self.lands[stage].at[self.land(stage, slot, first, rows)],
            send_sem=self.send_sems.at[at],
            recv_sem=self.recv_sems.at[at],
            device_id=self.place.neighbour(axis, way),
            device_id_type=MESH,
        )

    def straight(self, stage, flow, distance):
        order, (first, low), (_, high) = self.spans(flow)
        axis, rows = order[stage], low + high
        at = self.base + (stage * len(self.flows) + flow) * 6 + distance
        return pltpu.make_async_remote_copy(
            src_ref=self.grads.at[
                self.view(order, stage, wrap(self.place.at[axis] + distance), first, rows)
            ],
            dst_ref=self.lands[stage].at[self.land(stage, distance - 1, first, rows)],
            send_sem=self.send_sems.at[at],
            recv_sem=self.recv_sems.at[at],
            device_id=self.place.neighbour(axis, distance),
            device_id_type=MESH,
        )

    def add(self, stage, flow, step, span, slots):
        order, _, _ = self.spans(flow)
        at = self.view(order, stage, wrap(self.place.at[order[stage]] + step), *span)
        total = self.grads[at].astype(F32)
        for slot in slots:
            total = total + self.lands[stage][self.land(stage, slot, *span)].astype(F32)
        self.grads[at] = total.astype(LOW)

    def start(self, copy):
        copy.start()
        self.open_sends.append(copy)

    def run(self):
        flows = range(len(self.flows))
        for kind in range(4):
            for flow in flows:
                self.start(self.copy(0, flow, kind))
        yield
        for flow in flows:
            _, low, high = self.spans(flow)
            self.copy(0, flow, 0).wait_recv()
            self.add(0, flow, 1, low, (0,))
            self.start(self.copy(0, flow, 4))
            self.copy(0, flow, 1).wait_recv()
            self.add(0, flow, -1, high, (0,))
            self.start(self.copy(0, flow, 5))
        yield
        for flow in flows:
            _, low, high = self.spans(flow)
            for kind in (2, 3, 4, 5):
                self.copy(0, flow, kind).wait_recv()
            self.add(0, flow, 0, low, (1, 2))
            self.add(0, flow, 0, high, (1, 2))
            for distance in (1, 2, 3):
                self.start(self.straight(1, flow, distance))
        yield
        for flow in flows:
            _, low, high = self.spans(flow)
            for distance in (1, 2, 3):
                self.straight(1, flow, distance).wait_recv()
            self.add(1, flow, 0, (low[0], low[1] + high[1]), (0, 1, 2))
        yield

    def drain(self):
        for copy in self.open_sends:
            copy.wait_send()
        self.open_sends = []


FF_CHUNK = 512
HALF_CHUNKS = FF // FF_CHUNK // 2
FLOWS_F = (("xy", 0, 64, 64), ("yx", 128, 64, 64))
FLOWS_C = (("xy", 0, 32, 32), ("yx", 64, 32, 32))


class Eight:
    def __init__(self, place, send_sems, recv_sems, base):
        self.place, self.send_sems, self.recv_sems = place, send_sems, recv_sems
        self.base, self.last = base, None

    def copy(self, source, target, distance):
        device, _ = self.place.member(distance)
        return pltpu.make_async_remote_copy(
            src_ref=source,
            dst_ref=target,
            send_sem=self.send_sems.at[self.base + distance],
            recv_sem=self.recv_sems.at[self.base + distance],
            device_id=device,
            device_id_type=MESH,
        )

    def push(self, source_of, target):
        for distance in range(1, 8):
            _, rank = self.place.member(distance)
            self.last = (source_of(rank), target)
            self.copy(source_of(rank), target, distance).start()

    def receive(self, place_of):
        for distance in range(1, 8):
            _, rank = self.place.member(-distance)
            spot = place_of(rank)
            self.copy(spot, spot, distance).wait_recv()

    def drain(self):
        for distance in range(1, 8):
            self.copy(*self.last, distance).wait_send()


def back_kernel(
    gain_ref, bias_ref, ebias_ref,
    o2_hbm, x1_hbm, cot_hbm, tok_hbm, n1_hbm, cot4_hbm, mem4_hbm, n24_hbm, o14_hbm,
    heads_hbm, memh_hbm, cqh_hbm, mix1_hbm, mix2_hbm, inv1_hbm, inv2_hbm, exp1_hbm, exp2_hbm,
    qkv_hbm, ckv_hbm, out_hbm, query_hbm, cross_hbm, expand_hbm, reduce_hbm,
    output_ref, gtok_ref, gmem_ref, all_f, all_c, all_q, all_v,
    n1_all, ring_e, ring_r, cross_w, exp_ref, x1_ref, cot_ref, tok_ref,
    heads_ref, memh_ref, cqh_ref, mix1_ref, mix2_ref, inv1_ref, inv2_ref,
    a_n3, a_cot, a_o2, a_n2, a_o1, a_mem, act_in, dfe_in, act_out, dfe_out,
    b_dc, b_e2, b_da, b_kv,
    dc_ref, da_ref, acc_ref, dn_ref, expand_sums, vec_ref,
    do2_ref, do1_ref, do2h_ref, do1h_ref, sums_ref, e2_ref, dkv_ref, e1_ref, dkt_ref, dvt_ref,
    grads_f, land_f1, land_f2, grads_c, land_c1, land_c2,
    piece_f, piece_c, weight_ref, weight_in, weight_sum, piece_q, vec_out, vec_in, piece_v,
    load_sems, ring_sems, keep_sems, pair_send, pair_recv, send_sems, recv_sems,
    dp_send, dp_recv, sum_send, sum_recv, eight_send, eight_recv, column_send, column_recv,
):
    place = Place()
    core, y, xl, me, dp = place.core, place.y, place.xl, place.seq, place.dp
    partner = 2 * y + 1 - xl
    own_rows = aligned(me, TOK)
    order = [lax.rem(y + step, 4) for step in (1, 2, 3, 0)]

    barrier = greet_row()
    for distance in range(1, DP):
        pl.semaphore_signal(
            barrier, inc=1, device_id=(lax.rem(dp + distance, DP), me), device_id_type=MESH
        )
    outer = place.neighbour("x", 2 * xl - 1)
    pl.semaphore_signal(barrier, inc=1, device_id=outer, device_id_type=MESH)

    def load(source, target, sem):
        copy = pltpu.make_async_copy(source, target, load_sems.at[sem])
        copy.start()
        return copy

    z, rank = place.z, place.rank
    rank_rows = aligned(rank, TOK)

    def chunk_of(step):
        return lax.rem(rank + 1 + step, 8)

    def ring_copies(step, slot):
        copies = []
        for block in range(2):
            span = aligned(chunk_of(step) + 8 * block, 256)
            to = pl.ds(pl.multiple_of(slot * FF_CHUNK + block * 256, 256), 256)
            at = slot * 4 + block * 2
            copies += [
                pltpu.make_async_copy(expand_hbm.at[:, span], ring_e.at[:, to], ring_sems.at[at]),
                pltpu.make_async_copy(
                    reduce_hbm.at[span, :], ring_r.at[to, :], ring_sems.at[at + 1]
                ),
            ]
        return copies

    loads = [
        load(o2_hbm, a_o2.at[z, core], 0), load(cross_hbm, cross_w, 1), load(x1_hbm, x1_ref, 2),
        load(cot_hbm, cot_ref, 3)
    ]
    gather = Gather(n1_hbm, n1_all, keep_sems.at[0], send_sems, recv_sems, 64)
    col_n3, col_o2, col_n2, col_o1 = (
        Column(
            block, lambda at, whole=whole: whole.at[at, core], None,
            column_send, column_recv, 4 * index,
        )
        for index, (block, whole) in enumerate(
            (
                (a_n3.at[z, core], a_n3), (o2_hbm, a_o2), (a_n2.at[z, core], a_n2),
                (a_o1.at[z, core], a_o1),
            )
        )
    )
    pl.semaphore_wait(barrier, SEQ - 1 + DP - 1 + 1)
    gather.first()
    col_o2.first()
    to_core = []

    def both_cores(whole):
        slot = len(to_core)
        copy = pltpu.make_async_remote_copy(
            src_ref=whole.at[:, core],
            dst_ref=whole.at[:, core],
            send_sem=pair_send.at[slot],
            recv_sem=pair_recv.at[slot],
            device_id=place.other,
            device_id_type=MESH,
        )
        copy.start()
        arrival = pltpu.make_async_remote_copy(
            src_ref=whole.at[:, 1 - core],
            dst_ref=whole.at[:, 1 - core],
            send_sem=pair_send.at[slot],
            recv_sem=pair_recv.at[slot],
            device_id=place.other,
            device_id_type=MESH,
        )
        to_core.append((copy, arrival))

    give_act, give_dfe, give_dc, give_be2, give_kv, give_da, join_f, join_c = (
        Eight(place, eight_send, eight_recv, 8 * index) for index in range(8)
    )

    for one in loads[:3]:
        one.wait()
    for step in range(4):
        for one in ring_copies(step, step):
            one.start()
    x2 = x1_ref[...] + dot(a_o2[z, core], cross_w[...]) + bias_ref[8:9, :]
    unit3, inverse3 = norm_unit(x2)
    a_n3[z, core] = (unit3 * gain_ref[2:3, :] + bias_ref[2:3, :]).astype(LOW)
    acc_ref[...] = x2 + bias_ref[9:10, :]
    dn_ref[...] = jnp.zeros_like(dn_ref)
    loads[3].wait()
    col_n3.first()
    root = math.sqrt(2.0 / math.pi)

    def feed(step, slot, own):
        for one in ring_copies(step, slot):
            one.wait()
        chunk = chunk_of(step)
        span = aligned(slot, FF_CHUNK)
        offset = jnp.concatenate(
            [ebias_ref[:, aligned(chunk + 8 * block, 256)] for block in range(2)], 1
        )
        hidden = dot(a_n3[z, core], ring_e[:, span]) + offset
        square = hidden * hidden
        curve = jnp.tanh(root * hidden * (1.0 + 0.044715 * square))
        share = 0.5 * (1.0 + curve)
        act = (hidden * share).astype(LOW)
        slope = share + 0.5 * hidden * (1.0 - curve * curve) * (
            root * (1.0 + 3.0 * 0.044715 * square)
        )
        acc_ref[...] += dot(act, ring_r[span, :])
        grad_act = dot_nt(cot_ref[...], ring_r[span, :])
        grad_hidden = (slope * grad_act).astype(LOW)
        if own:
            act_in[rank_rows, :] = act
            dfe_in[rank_rows, :] = grad_hidden
        else:
            act_out[step] = act
            dfe_out[step] = grad_hidden
            give_act.copy(act_out.at[step], act_in.at[rank_rows, :], step + 1).start()
            give_dfe.copy(dfe_out.at[step], dfe_in.at[rank_rows, :], step + 1).start()
        expand_sums[chunk] = column_sum(grad_hidden.astype(F32))
        dn_ref[...] += dot_nt(grad_hidden, ring_e[:, span])

    gathered = [
        (source.at[at], whole.at[at, core])
        for source, whole, steps in (
            (cot4_hbm, a_cot, (0, 1, 2, 3)), (mem4_hbm, a_mem, (0, 1, 2, 3)),
            (n24_hbm, a_n2, (-1, 0, 1)), (o14_hbm, a_o1, (-1, 0, 1)),
        )
        for at in [lax.rem(z + step + 4, 4) for step in steps]
    ]
    gathered = [
        pltpu.make_async_copy(source, target, load_sems.at[24 + index])
        for index, (source, target) in enumerate(gathered)
    ]

    def feed_step(step, carry):
        feed(step, lax.rem(step, 4), False)

        @pl.when(step < 4)
        def _():
            for one in ring_copies(step + 4, step):
                one.start()

        @pl.when(step == 2)
        def _():
            gather.second()

        @pl.when(step == 4)
        def _():
            col_n3.second()

        @pl.when(step == 6)
        def _():
            col_o2.second()

        return carry

    lax.fori_loop(0, 7, feed_step, 0)
    feed(7, 3, True)
    give_act.last = (act_out.at[0], act_in.at[rank_rows, :])
    give_dfe.last = (dfe_out.at[0], dfe_in.at[rank_rows, :])
    for one in gathered:
        one.start()
    kept = [
        load(memh_hbm, memh_ref, 9), load(cqh_hbm, cqh_ref, 10), load(mix2_hbm, mix2_ref, 11),
        load(inv2_hbm, inv2_ref, 12), load(exp2_hbm, exp_ref, 13),
    ]
    later = [
        load(query_hbm, ring_r.at[1024:2048, :], 14), load(out_hbm, ring_r.at[0:1024, :], 15),
        load(ckv_hbm, ring_e, 16),
    ]
    kept1 = [
        load(heads_hbm, heads_ref, 17), load(mix1_hbm, mix1_ref, 18), load(inv1_hbm, inv1_ref, 19),
        load(tok_hbm, tok_ref, 20),
    ]
    output_ref[...] = acc_ref[...].astype(LOW)
    dn3 = dn_ref[...]
    grad = cot_ref[...].astype(F32)
    dx2 = grad + norm_back(dn3, unit3, inverse3, gain_ref[2:3, :])
    acc_ref[...] = dx2
    dc_ref[...] = dx2.astype(LOW)

    give_do2, give_e2, give_k2, give_v2, give_do1, give_q1, give_k1, give_v1 = (
        Exchange(send_sems, recv_sems, 8 * index) for index in range(8)
    )

    def push_heads(exchange, low_ref, weight_of, values, target, keep_slot):
        for step in range(4):
            at = order[step]
            low_ref[:, aligned(at, 256)] = dot_nt(values, weight_of(aligned(at, 256))).astype(LOW)
            if step < 3:
                for half in range(2):
                    there = 2 * at + half
                    exchange.push(
                        low_ref.at[:, aligned(there, PAIR)], target.at[own_rows, :], there, False
                    )
            else:
                exchange.push(
                    low_ref.at[:, aligned(partner, PAIR)], target.at[own_rows, :], partner, False
                )
        keep = pltpu.make_async_copy(
            low_ref.at[:, aligned(me, PAIR)], target.at[own_rows, :], keep_sems.at[keep_slot]
        )
        keep.start()
        return keep

    keep_do2 = push_heads(
        give_do2, do2_ref, lambda rows: cross_w[rows, :], dc_ref[...], do2h_ref, 1
    )

    def share(exchange, source, target, width):
        exchange.push(lambda to: source.at[:, aligned(to, width)], target.at[rank_rows, :])
        target[rank_rows, :] = source[:, aligned(rank, width)]

    share(give_dc, dc_ref, b_dc, PAIR)
    vec_ref[2:3, :] = column_sum(dn3 * unit3)
    vec_ref[5:6, :] = column_sum(dn3)
    vec_ref[11:12, :] = column_sum(dc_ref[...].astype(F32))
    vec_ref[12:13, :] = column_sum(grad)

    def left_of(whole, group):
        return whole[:, :, :, aligned(group, 128)].reshape(ROW, 128)

    def rows_of(group, block):
        to = lax.rem(group, 4) * 2 + block
        return pl.ds(pl.multiple_of(to * 16, 16), 16)

    def fill_f(group, carry):
        result = dot_tn(left_of(a_n3, group), dfe_in[...]).astype(LOW)
        for block in range(2):
            for yy in range(4):
                at = (block * 4 + yy) * 16
                for col in range(2):
                    grads_f[(group // 4) * 2 + col, yy, rows_of(group, block), :] = result[
                        at : at + 16, col * LANES : col * LANES + LANES
                    ]
        return carry

    def fill_reduce():
        for xh in range(2):
            result = dot_tn(
                act_in[:, xh * 256 : xh * 256 + 256], a_cot[...].reshape(ROW, WIDTH)
            ).astype(LOW)
            for yy in range(4):
                for col in range(2):
                    for sub in range(2):
                        at = (col * 2 + sub) * LANES
                        grads_f[xh * 2 + col, yy, 128 + sub * 64 : 192 + sub * 64, :] = result[
                            yy * 64 : yy * 64 + 64, at : at + LANES
                        ]

    def fill_c(group, carry):
        three = [
            dot_tn(left_of(whole, group), right[...]).astype(LOW)
            for whole, right in ((a_n2, b_e2), (a_o1, b_da), (a_o2, b_dc))
        ]
        wide = dot_tn(left_of(a_mem, group), b_kv[...]).astype(LOW)
        x_at = (group // 4) * 2
        for block in range(2):
            rows = rows_of(group, block)
            for yy in range(4):
                at = slice((block * 4 + yy) * 16, (block * 4 + yy) * 16 + 16)
                for index, one in enumerate(three):
                    grads_c[x_at, yy, rows, index * PAIR : index * PAIR + PAIR] = one[at, :]
                grads_c[x_at + 1, yy, rows, 0:256] = wide[at, :]
                grads_c[x_at + 1, yy, rows, 256:384] = jnp.zeros((16, PAIR), LOW)
        return carry

    sum_f = Sum(place, grads_f, (land_f1, land_f2), FLOWS_F, sum_send, sum_recv, 0)
    sum_c = Sum(place, grads_c, (land_c1, land_c2), FLOWS_C, sum_send, sum_recv, 24)
    run_f, run_c = sum_f.run(), sum_c.run()

    def attend_back(query, key_rows, value_rows, grad_ref, mix_ref, inv_ref, causal, after_tile):
        tile = 256
        scaled = (grad_ref[...].astype(F32) * inv_ref[...]).astype(LOW)
        lanes = head_lanes(ROW)
        product = scaled.astype(F32) * mix_ref[...].astype(F32)
        inner = [jnp.sum(pick_head(product, lanes, head), -1, keepdims=True) for head in range(2)]
        value_t = value_rows.T
        query_t = query.T
        scaled_t = scaled.T
        dkt_ref[...] = jnp.zeros_like(dkt_ref)
        dvt_ref[...] = jnp.zeros_like(dvt_ref)
        tile_lanes = head_lanes(tile)
        steps = range(ROW // tile)
        for step in reversed(steps) if causal else steps:
            rows = slice(step * tile, step * tile + tile)
            width = (step + 1) * tile if causal else ROW
            parts = []
            for head in range(2):
                own = slice(head * HEAD_DIM, head * HEAD_DIM + HEAD_DIM)
                exponent = exp_ref[head, rows, 0:width]
                grad_p = dot(pick_head(scaled[rows, :], tile_lanes, head), value_t[:, 0:width])
                grad_s = (exponent.astype(F32) * (grad_p - inner[head][rows, :])).astype(LOW)
                parts.append(dot(grad_s, key_rows[0:width, :]))
                dkt_ref[own, 0:width] += dot(query_t[own, rows], grad_s)
                dvt_ref[own, 0:width] += dot(scaled_t[own, rows], exponent)
            grad_q = jnp.where(tile_lanes, parts[0], parts[1]).astype(LOW) * SCALE
            sums_ref[rows, 0:PAIR] = grad_q.astype(LOW)
            after_tile(step, rows)

    def send_part(exchange, part, there, target, column):
        exchange.push(
            sums_ref.at[there * TOK : there * TOK + TOK, part * PAIR : part * PAIR + PAIR],
            target.at[:, pl.ds(pl.multiple_of(column + me * PAIR, PAIR), PAIR)], there, True,
        )

    def keep_part(part, target, column, slot):
        copy = pltpu.make_async_copy(
            sums_ref.at[own_rows, part * PAIR : part * PAIR + PAIR],
            target.at[:, pl.ds(pl.multiple_of(column + me * PAIR, PAIR), PAIR)],
            keep_sems.at[slot],
        )
        copy.start()
        return copy

    def from_peers(target, column):
        return lambda sender: target.at[
            :, pl.ds(pl.multiple_of(column + sender * PAIR, PAIR), PAIR)
        ]

    def join(exchange, grads, piece, keep_slot, rest):
        block = grads.at[place.at["x"], place.at["y"]]
        mine = pl.ds(pl.multiple_of(rank * 16, 16), 16)
        exchange.push(
            lambda to: block.at[pl.ds(pl.multiple_of(to * 16, 16), 16), :], piece.at[mine, :]
        )
        keeps = [
            pltpu.make_async_copy(block.at[mine, :], piece.at[mine, :], keep_sems.at[keep_slot])
        ]
        if rest:
            keeps.append(
                pltpu.make_async_copy(
                    block.at[pl.ds(128, 128), :], piece.at[pl.ds(128, 128), :],
                    keep_sems.at[keep_slot + 1],
                )
            )
        for one in keeps:
            one.start()
        return keeps

    def joined(exchange, piece, keeps):
        for one in keeps:
            one.wait()
        exchange.receive(lambda to: piece.at[pl.ds(pl.multiple_of(to * 16, 16), 16), :])

    spreads = []

    def spread(piece, whole, base, slot):
        exchange = Exchange(send_sems, recv_sems, base)
        for distance in range(1, SEQ):
            exchange.push(piece, whole.at[me], lax.rem(me + distance, SEQ), False)
        keep = pltpu.make_async_copy(piece, whole.at[me], keep_sems.at[slot])
        keep.start()
        spreads.append((exchange, keep, whole))

    for one in kept:
        one.wait()
    keep_do2.wait()
    give_do2.receive(lambda sender: do2h_ref.at[aligned(sender, TOK), :])

    def after_cross(step, rows):
        for half in range(2):
            send_part(give_e2, 0, 2 * step + half, e2_ref, 0)

    attend_back(
        cqh_ref[...], memh_ref[:, 0:PAIR], memh_ref[:, PAIR : 2 * PAIR], do2h_ref, mix2_ref,
        inv2_ref, False, after_cross,
    )
    keeps = [keep_part(0, e2_ref, 0, 2)]
    sums_ref[:, PAIR : 2 * PAIR] = dkt_ref[...].T.astype(LOW)
    sums_ref[:, 2 * PAIR : 3 * PAIR] = dvt_ref[...].T.astype(LOW)
    for there in range(SEQ):
        send_part(give_k2, 1, there, dkv_ref, 0)
        send_part(give_v2, 2, there, dkv_ref, WIDTH)
    keeps += [keep_part(1, dkv_ref, 0, 3), keep_part(2, dkv_ref, WIDTH, 4)]
    exp1_load = load(exp1_hbm, exp_ref, 21)

    keeps[0].wait()
    later[0].wait()
    unit2, inverse2 = norm_unit(x1_ref[...])
    give_e2.receive(from_peers(e2_ref, 0))
    dn2 = dot_nt(e2_ref[...], ring_r[1024:2048, :])
    dx1 = acc_ref[...] + norm_back(dn2, unit2, inverse2, gain_ref[1:2, :])
    acc_ref[...] = dx1
    da_ref[...] = dx1.astype(LOW)
    later[1].wait()
    keep_do1 = push_heads(
        give_do1, do1_ref, lambda rows: ring_r[rows, :], da_ref[...], do1h_ref, 5
    )
    gather.third()
    share(give_be2, e2_ref, b_e2, PAIR)
    share(give_da, da_ref, b_da, PAIR)
    col_n3.finish()
    both_cores(a_n3)
    for one in gathered:
        one.wait()
    both_cores(a_cot)
    both_cores(a_mem)
    col_n2.forward()
    col_o1.forward()
    vec_ref[1:2, :] = column_sum(dn2 * unit2)
    vec_ref[4:5, :] = column_sum(dn2)
    vec_ref[8:9, :] = column_sum(da_ref[...].astype(F32))
    vec_ref[9:10, :] = column_sum(e2_ref[...].astype(F32))
    keeps[1].wait()
    keeps[2].wait()
    give_k2.receive(from_peers(dkv_ref, 0))
    give_v2.receive(from_peers(dkv_ref, WIDTH))
    share(give_kv, dkv_ref, b_kv, 256)
    later[2].wait()
    gmem_ref[...] = dot_nt(dkv_ref[...], ring_e[...])
    vec_ref[10:11, :] = column_sum(dkv_ref[:, WIDTH : 2 * WIDTH].astype(F32))
    last = [
        load(qkv_hbm.at[:, 0 : 2 * WIDTH], ring_e, 22),
        load(qkv_hbm.at[:, 2 * WIDTH : 3 * WIDTH], ring_r.at[0:1024, :], 23),
    ]

    for index in (0, 1):
        to_core[index][1].wait_recv()
    give_act.receive(lambda to: act_in.at[aligned(to, TOK), :])
    give_dfe.receive(lambda to: dfe_in.at[aligned(to, TOK), :])
    lax.fori_loop(0, 8, fill_f, 0)
    fill_reduce()
    next(run_f)
    col_o2.finish()
    both_cores(a_o2)

    for exchange in (give_e2, give_k2, give_v2):
        exchange.drain()
    for one in kept1:
        one.wait()
    exp1_load.wait()
    keep_do1.wait()
    give_do1.receive(lambda sender: do1h_ref.at[aligned(sender, TOK), :])

    def after_self(step, rows):
        sums_ref[rows, PAIR : 2 * PAIR] = dkt_ref[:, rows].T.astype(LOW)
        sums_ref[rows, 2 * PAIR : 3 * PAIR] = dvt_ref[:, rows].T.astype(LOW)
        for half in range(2):
            for part, exchange in enumerate((give_q1, give_k1, give_v1)):
                send_part(exchange, part, 2 * step + half, e1_ref, part * WIDTH)

    attend_back(
        heads_ref[:, 0:PAIR], heads_ref[:, PAIR : 2 * PAIR], heads_ref[:, 2 * PAIR : 3 * PAIR],
        do1h_ref, mix1_ref, inv1_ref, True, after_self,
    )
    keeps = [keep_part(part, e1_ref, part * WIDTH, 6 + part) for part in range(3)]
    next(run_f)


    gather.finish()
    for part in range(3):
        value = sums_ref[:, part * PAIR : part * PAIR + PAIR].T
        weight_ref[:, :, :, part * PAIR : part * PAIR + PAIR] = (
            dot(value, n1_all[...]).T.astype(LOW).reshape(DP // 2, 2, ROW // DP, PAIR)
        )
    both_sums = pltpu.make_async_remote_copy(
        src_ref=weight_ref.at[:, 1 - core],
        dst_ref=weight_in.at[0],
        send_sem=pair_send.at[6],
        recv_sem=pair_recv.at[6],
        device_id=place.other,
        device_id_type=MESH,
    )
    both_sums.start()
    pair = dp // 2

    def pair_copy(source, target, distance):
        there = lax.rem(pair + distance + 8, 8)
        return pltpu.make_async_remote_copy(
            src_ref=source.at[there],
            dst_ref=target.at[1, pair],
            send_sem=dp_send.at[distance],
            recv_sem=dp_recv.at[distance],
            device_id=(there * 2 + core, me),
            device_id_type=MESH,
        )

    def pair_receive(target, distance):
        sender = lax.rem(pair - distance + 8, 8)
        return pltpu.make_async_remote_copy(
            src_ref=target.at[1, sender],
            dst_ref=target.at[1, sender],
            send_sem=dp_send.at[distance],
            recv_sem=dp_recv.at[distance],
            device_id=(sender * 2 + core, me),
            device_id_type=MESH,
        )

    def dp_copy(source, target, distance, base):
        there = lax.rem(dp + distance, DP)
        return pltpu.make_async_remote_copy(
            src_ref=source.at[there],
            dst_ref=target.at[dp],
            send_sem=dp_send.at[base + distance],
            recv_sem=dp_recv.at[base + distance],
            device_id=(there, me),
            device_id_type=MESH,
        )

    def dp_receive(target, distance, base):
        sender = lax.rem(dp - distance + DP, DP)
        return pltpu.make_async_remote_copy(
            src_ref=target.at[sender],
            dst_ref=target.at[sender],
            send_sem=dp_send.at[base + distance],
            recv_sem=dp_recv.at[base + distance],
            device_id=(sender, me),
            device_id_type=MESH,
        )

    for column, whole in ((col_n2, a_n2), (col_o1, a_o1)):
        column.far()
        both_cores(whole)
    both_sums.wait()
    weight_sum[...] = (
        weight_ref[:, core].astype(F32) + weight_in[0].astype(F32)
    ).astype(LOW)
    for distance in range(1, 8):
        pair_copy(weight_sum, weight_in, distance).start()
    next(run_f)

    for index in (2, 3, 4, 5):
        to_core[index][1].wait_recv()
    for exchange, target in ((give_dc, b_dc), (give_be2, b_e2), (give_kv, b_kv), (give_da, b_da)):
        exchange.receive(lambda to, target=target: target.at[aligned(to, TOK), :])
    lax.fori_loop(0, 8, fill_c, 0)
    next(run_c)
    next(run_f)
    keeps_f = join(join_f, grads_f, piece_f, 9, True)

    for one in keeps:
        one.wait()
    for one in last:
        one.wait()
    unit1, inverse1 = norm_unit(tok_ref[...].astype(F32))
    give_q1.receive(from_peers(e1_ref, 0))
    give_k1.receive(from_peers(e1_ref, WIDTH))
    dn1 = dot_nt(e1_ref[:, 0 : 2 * WIDTH], ring_e[...])
    give_v1.receive(from_peers(e1_ref, 2 * WIDTH))
    dn1 = dn1 + dot_nt(e1_ref[:, 2 * WIDTH : 3 * WIDTH], ring_r[0:1024, :])
    gtok_ref[...] = acc_ref[...] + norm_back(dn1, unit1, inverse1, gain_ref[0:1, :])
    vec_ref[0:1, :] = column_sum(dn1 * unit1)
    vec_ref[3:4, :] = column_sum(dn1)
    vec_ref[6:7, :] = column_sum(e1_ref[:, 0:WIDTH].astype(F32))
    vec_ref[7:8, :] = column_sum(e1_ref[:, 2 * WIDTH : 3 * WIDTH].astype(F32))

    next(run_c)

    vec_out[...] = jnp.zeros_like(vec_out)
    for owner in range(DP):
        vec_out[owner, 0:13, 0:64] = vec_ref[0:13, owner * 64 : owner * 64 + 64]
        for half in range(2):
            at = (owner // 8) * 256 + half * PAIR
            vec_out[owner, 13 + half : 14 + half, :] = expand_sums[owner % 8, :, at : at + PAIR]
    for distance in range(1, DP):
        dp_copy(vec_out, vec_in, distance, DP).start()

    next(run_c)
    joined(join_f, piece_f, keeps_f)
    spread(piece_f, all_f, 78, 13)
    for distance in range(1, 8):
        pair_receive(weight_in, distance).wait_recv()
    total = weight_sum[pair].astype(F32)
    for distance in range(1, 8):
        total = total + weight_in[1, lax.rem(pair + distance, 8)].astype(F32)
    piece_q[...] = total.astype(LOW)
    spread(piece_q, all_q, 70, 12)
    next(run_c)
    keeps_c = join(join_c, grads_c, piece_c, 11, False)
    for distance in range(1, DP):
        dp_receive(vec_in, distance, DP).wait_recv()
    total = vec_out[dp]
    for distance in range(1, DP):
        total = total + vec_in[lax.rem(dp + distance, DP)]
    piece_v[...] = total
    spread(piece_v, all_v, 86, 14)
    joined(join_c, piece_c, keeps_c)
    spread(piece_c, all_c, 94, 15)

    for exchange, keep, whole in spreads:
        keep.wait()
        exchange.receive(lambda sender, whole=whole: whole.at[sender])
        exchange.drain()
    for exchange in (give_do2, give_do1, give_q1, give_k1, give_v1):
        exchange.drain()
    for copy, _ in to_core:
        copy.wait_send()
    for exchange in (give_act, give_dfe, give_dc, give_be2, give_kv, give_da, join_f, join_c):
        exchange.drain()
    for distance in range(1, DP):
        dp_copy(vec_out, vec_in, distance, DP).wait_send()
    for distance in range(1, 8):
        pair_copy(weight_sum, weight_in, distance).wait_send()
    sum_f.drain()
    sum_c.drain()


def back_call(operands):
    dma = pltpu.SemaphoreType.DMA
    vmem = pltpu.VMEM
    token = vmem((TOK, WIDTH), LOW)
    token_wide = vmem((TOK, WIDTH), F32)
    heads = vmem((ROW, PAIR), LOW)
    inverse = vmem((ROW, PAIR), F32)
    eight = vmem((4, 2, TOK, WIDTH), LOW)
    column = vmem((ROW, PAIR), LOW)
    chunk = vmem((ROW, FF_CHUNK), LOW)
    chunks = vmem((7, TOK, FF_CHUNK), LOW)

    def sums(rows, lanes):
        return [
            vmem((4, 4, rows, lanes), LOW), vmem((3, 4, rows, lanes), LOW),
            vmem((3, rows, lanes), LOW),
        ]

    return pl.pallas_call(
        back_kernel,
        out_shape=(
            shaped((TOK, WIDTH)), shaped((TOK, WIDTH), F32), shaped((TOK, WIDTH), F32),
            shaped((SEQ, 256, LANES)), shaped((SEQ, 128, 384)),
            shaped((SEQ, 64, 3 * PAIR)), shaped((SEQ, 16, PAIR), F32),
        ),
        in_specs=[spec_vmem()] * 3 + [spec_any()] * 25,
        out_specs=(spec_vmem(),) * 3 + (spec_any(),) * 4,
        scratch_shapes=[
            vmem((ROW, WIDTH), LOW),
            vmem((WIDTH, 2 * WIDTH), LOW), vmem((2 * WIDTH, WIDTH), LOW), vmem((WIDTH, WIDTH), LOW),
            vmem((2, ROW, ROW), LOW), token_wide, token, token,
            vmem((ROW, 3 * PAIR), LOW), vmem((ROW, 2 * PAIR), LOW), heads, heads, heads, inverse,
            inverse,
            eight, eight, eight, eight, eight, eight, chunk, chunk, chunks, chunks,
            column, column, column, vmem((ROW, 256), LOW),
            token, token, token_wide, token_wide,
            vmem((FF // FF_CHUNK, 1, FF_CHUNK), F32), vmem((16, WIDTH), F32),
            token, token, heads, heads, vmem((ROW, 3 * PAIR), LOW), token,
            vmem((TOK, 2 * WIDTH), LOW), vmem((TOK, 3 * WIDTH), LOW),
            vmem((PAIR, ROW), F32), vmem((PAIR, ROW), F32),
        ]
        + sums(256, LANES) + sums(128, 384)
        + [
            vmem((256, LANES), LOW), vmem((128, 384), LOW),
            vmem((8, 2, 64, 3 * PAIR), LOW), vmem((2, 8, 64, 3 * PAIR), LOW),
            vmem((8, 64, 3 * PAIR), LOW),
            vmem((64, 3 * PAIR), LOW), vmem((DP, 16, PAIR), F32), vmem((DP, 16, PAIR), F32),
            vmem((16, PAIR), F32),
            dma((38,)), dma((16,)), dma((16,)), dma((7,)), dma((7,)), dma((102,)), dma((102,)),
            dma((32,)), dma((32,)), dma((48,)), dma((48,)), dma((64,)), dma((64,)), dma((16,)),
            dma((16,)),
        ],
        compiler_params=pltpu.CompilerParams(
            collective_id=3, has_side_effects=True, vmem_limit_bytes=63 * MIB
        ),
        cost_estimate=pl.CostEstimate(
            flops=2 * TOK * WIDTH * 27 * WIDTH, bytes_accessed=100 * MIB, transcendentals=0
        ),
        name="back",
    )(*operands)


def finish_kernel(
    f_hbm, c_hbm, q_hbm, vec_hbm, output_hbm, gtok_hbm, gmem_hbm,
    gqkv_ref, gout_ref, gque_ref, gckv_ref, gcro_ref, gexp_ref, gred_ref, ggain_ref, gbias_ref,
    gebias_ref, to_output, to_gtok, to_gmem,
    f_ref, c_ref, q_ref, vec_ref, sems,
):
    copies = [
        pltpu.make_async_copy(source, target, sems.at[index])
        for index, (source, target) in enumerate(
            (
                (f_hbm, f_ref), (c_hbm, c_ref), (q_hbm, q_ref), (vec_hbm, vec_ref),
                (output_hbm, to_output), (gtok_hbm, to_gtok), (gmem_hbm, to_gmem),
            )
        )
    ]
    for one in copies:
        one.start()
    for one in copies[:4]:
        one.wait()
    for seq in range(SEQ):
        y, xl = seq // 2, seq % 2
        rows = slice(16 * y, 16 * y + 16)
        for owner in range(8):
            own = slice(owner * 16, owner * 16 + 16)
            at = (owner + 8 * xl) * 256
            gexp_ref[rows, at : at + 256] = f_ref[seq, own, :].astype(F32)
            if xl == 0:
                for index, target in enumerate((gque_ref, gout_ref, gcro_ref)):
                    target[rows, owner * PAIR : owner * PAIR + PAIR] = c_ref[
                        seq, own, index * PAIR : index * PAIR + PAIR
                    ].astype(F32)
            else:
                gckv_ref[rows, owner * 256 : owner * 256 + 256] = c_ref[seq, own, 0:256].astype(F32)
        for sub in range(2):
            at = xl * 512 + sub * LANES
            gred_ref[64 * y : 64 * y + 64, at : at + LANES] = f_ref[
                seq, 128 + sub * 64 : 192 + sub * 64, :
            ].astype(F32)
        for part in range(3):
            at = part * WIDTH + seq * PAIR
            gqkv_ref[:, at : at + PAIR] = q_ref[seq, :, part * PAIR : (part + 1) * PAIR].astype(F32)
    total = vec_ref[0]
    for seq in range(1, SEQ):
        total = total + vec_ref[seq]
    ggain_ref[...] = total[0:3, 0:64]
    gbias_ref[...] = total[3:13, 0:64]
    gebias_ref[:, 0:PAIR] = total[13:14, :]
    gebias_ref[:, PAIR : 2 * PAIR] = total[14:15, :]
    for one in copies[4:]:
        one.wait()


def finish_call(operands):
    vmem = pltpu.VMEM
    return pl.pallas_call(
        finish_kernel,
        out_shape=(
            shaped((64, 3 * WIDTH), F32), shaped((64, WIDTH), F32), shaped((64, WIDTH), F32),
            shaped((64, 2 * WIDTH), F32), shaped((64, WIDTH), F32), shaped((64, FF), F32),
            shaped((256, WIDTH), F32), shaped((3, 64), F32), shaped((10, 64), F32),
            shaped((1, 256), F32), shaped((TOK, WIDTH)), shaped((TOK, WIDTH), F32),
            shaped((TOK, WIDTH), F32),
        ),
        in_specs=[spec_any()] * 7,
        out_specs=(spec_vmem(),) * 13,
        scratch_shapes=[
            vmem((SEQ, 256, LANES), LOW), vmem((SEQ, 128, 384), LOW), vmem((SEQ, 64, 3 * PAIR), LOW),
            vmem((SEQ, 16, PAIR), F32), pltpu.SemaphoreType.DMA((8,)),
        ],
        compiler_params=pltpu.CompilerParams(vmem_limit_bytes=63 * MIB),
        cost_estimate=pl.CostEstimate(flops=0, bytes_accessed=10 * MIB, transcendentals=0),
        name="finish",
    )(*operands)


def on_device(
    tokens, memory, cotangent, offsets, memory_ids, pair_map, self_qkv, self_out, cross_query,
    cross_kv, cross_out, expand_weight, expand_bias, reduce_weight, norm_gains, bias_rows,
):
    tok = tokens.reshape(TOK, WIDTH)
    mem = memory.reshape(TOK, WIDTH)
    cot = cotangent.reshape(TOK, WIDTH)
    (
        x1, _, _, o2, heads, mem_heads, cq, mix1, mix2, inv1, inv2, n1, exp1, exp2, cot4, mem4, n24, o14,
    ) = front_call(
        (tok, mem, cot, norm_gains, bias_rows, memory_ids, offsets, pair_map, self_qkv, cross_kv,
         self_out, cross_query)
    )
    output, gtok, gmem, all_f, all_c, all_q, all_v = back_call(
        (norm_gains, bias_rows, expand_bias.reshape(1, FF),
         o2, x1, cot, tok, n1, cot4, mem4, n24, o14, heads, mem_heads, cq, mix1, mix2, inv1, inv2,
         exp1, exp2, self_qkv, cross_kv, self_out, cross_query, cross_out, expand_weight,
         reduce_weight)
    )
    (
        gqkv, gout, gque, gckv, gcro, gexp, gred, ggain, gbias, gebias, output, gtok, gmem,
    ) = finish_call((all_f, all_c, all_q, all_v, output, gtok, gmem))
    return (
        output.reshape(1, TOK, WIDTH), gtok.reshape(1, TOK, WIDTH), gmem.reshape(1, TOK, WIDTH),
        gqkv, gout, gque, gckv, gcro, gexp, gebias.reshape(256), gred, ggain, gbias,
    )


def solution(mesh):
    row = P("dp", "seq", None)
    split = P("dp", None)
    in_specs = (row,) * 3 + (split,) * 3 + (P(),) * 10
    out_specs = (row,) * 3 + (split,) * 6 + (P("dp"), split, P(None, "dp"), P(None, "dp"))
    return jax.shard_map(
        on_device, mesh=mesh, in_specs=in_specs, out_specs=out_specs, check_vma=False
    )
```

```python
import functools
import math

import jax
import jax.numpy as jnp
from jax import lax
from jax.experimental import pallas as pl
from jax.experimental.pallas import tpu as pltpu
from jax.sharding import PartitionSpec as P

HEADS = 16
HEAD_DIM = 64
WIDTH = 1024
TOK = 128
ROW = 1024
FF = 4096
SEQ = 8
DP = 16
PAIR = 128
NEG_FILL = -1e30
EPS = 1e-05
SCALE = HEAD_DIM ** (-0.5)
LOW = jnp.bfloat16
F32 = jnp.float32
MESH = pl.DeviceIdType.MESH
MIB = 2**20


def dot(left, right):
    return lax.dot_general(left, right, (((1,), (0,)), ((), ())), preferred_element_type=F32)


def dot_nt(left, right):
    return lax.dot_general(left, right, (((1,), (1,)), ((), ())), preferred_element_type=F32)


def dot_tn(left, right):
    return lax.dot_general(left, right, (((0,), (0,)), ((), ())), preferred_element_type=F32)


def norm_unit(values):
    average = jnp.mean(values, -1, keepdims=True)
    centered = values - average
    inverse = lax.rsqrt(jnp.mean(centered * centered, -1, keepdims=True) + EPS)
    return centered * inverse, inverse


def norm_back(incoming, unit, inverse, gain_row):
    scaled = incoming * gain_row
    return inverse * (
        scaled
        - jnp.mean(scaled, -1, keepdims=True)
        - unit * jnp.mean(scaled * unit, -1, keepdims=True)
    )


def column_sum(values):
    return jnp.sum(values, 0, keepdims=True)


def spec_any():
    return pl.BlockSpec(memory_space=pl.ANY)


def spec_vmem():
    return pl.BlockSpec(memory_space=pltpu.VMEM)


def spec_smem():
    return pl.BlockSpec(memory_space=pltpu.SMEM)


def shaped(shape, kind=LOW):
    return jax.ShapeDtypeStruct(shape, kind)


def head_lanes(rows):
    return lax.broadcasted_iota(jnp.int32, (rows, PAIR), 1) < HEAD_DIM


def pick_head(values, lanes, head):
    zero = jnp.zeros_like(values)
    return jnp.where(lanes, values, zero) if head == 0 else jnp.where(lanes, zero, values)


def attend_tile(query, key_t, value, allowed, exp_ref, rows, width):
    lanes = head_lanes(query.shape[0])
    mixed, inverses = [], []
    for head in range(2):
        scores = dot(pick_head(query, lanes, head), key_t)
        scores = jnp.where(allowed, scores, NEG_FILL)
        top = jnp.max(scores, -1, keepdims=True)
        exponent = jnp.exp(scores - top)
        inverse = 1.0 / jnp.sum(exponent, -1, keepdims=True)
        low = exponent.astype(LOW)
        exp_ref[head, rows, 0:width] = low
        mixed.append(dot(low, value))
        inverses.append(inverse)
    inverse = jnp.where(lanes, inverses[0], inverses[1])
    return jnp.where(lanes, mixed[0], mixed[1]) * inverse, inverse


def self_allowed(offsets_ref, step, tile, width):
    places = lax.broadcasted_iota(jnp.int32, (tile, 1), 0) + step * tile
    begin = jnp.zeros((tile, 1), jnp.int32)
    for seg in range(1, 16):
        offset = offsets_ref[0, seg]
        begin = jnp.where(places >= offset, offset, begin)
    keys = lax.broadcasted_iota(jnp.int32, (tile, width), 1)
    return (keys <= places) & (keys >= begin)


def cross_allowed(ids, offsets_ref, pair_ref, step, tile):
    places = lax.broadcasted_iota(jnp.int32, (tile, 1), 0) + step * tile
    reads = jnp.zeros((tile, 1), jnp.int32) + pair_ref[0, 0]
    for seg in range(1, 16):
        reads = jnp.where(places >= offsets_ref[0, seg], pair_ref[0, seg], reads)
    return ids == reads


def aligned(index, unit):
    return pl.ds(pl.multiple_of(index * unit, unit), unit)


class Exchange:
    def __init__(self, send_sems, recv_sems, base):
        self.dp = lax.axis_index("dp")
        self.me = lax.axis_index("seq")
        self.send_sems, self.recv_sems, self.base = send_sems, recv_sems, base
        self.sent = []

    def copy(self, source, target, there, distance):
        return pltpu.make_async_remote_copy(
            src_ref=source,
            dst_ref=target,
            send_sem=self.send_sems.at[self.base + distance],
            recv_sem=self.recv_sems.at[self.base + distance],
            device_id=(self.dp, there),
            device_id_type=MESH,
        )

    def push(self, source, target, there, may_be_own):
        distance = lax.rem(there - self.me + SEQ, SEQ)
        if may_be_own:
            remote = there != self.me

            @pl.when(remote)
            def _():
                self.copy(source, target, there, distance).start()

        else:
            self.copy(source, target, there, distance).start()
        self.sent.append((source, target))

    def receive(self, place):
        for distance in range(1, SEQ):
            sender = lax.rem(self.me - distance + SEQ, SEQ)
            spot = place(sender)
            self.copy(spot, spot, sender, distance).wait_recv()

    def drain(self):
        source, target = self.sent[0]
        for distance in range(1, SEQ):
            there = lax.rem(self.me + distance, SEQ)
            self.copy(source, target, there, distance).wait_send()


def greet_row():
    dp = lax.axis_index("dp")
    me = lax.axis_index("seq")
    barrier = pltpu.get_barrier_semaphore()
    for distance in range(1, SEQ):
        pl.semaphore_signal(
            barrier, inc=1, device_id=(dp, lax.rem(me + distance, SEQ)), device_id_type=MESH
        )
    return barrier


class Gather:
    def __init__(self, block, spot, local_sem, send_sems, recv_sems, base):
        self.dp = lax.axis_index("dp")
        self.me = lax.axis_index("seq")
        self.y, self.xl = self.me // 2, lax.rem(self.me, 2)
        self.spot, self.send_sems, self.recv_sems, self.base = spot, send_sems, recv_sems, base
        self.own = pltpu.make_async_copy(block, spot(self.me), local_sem)
        self.block = block

    def part(self, y, xl):
        return self.spot(lax.rem(y + 8, 4) * 2 + xl)

    def copy(self, source, target, there, slot):
        return pltpu.make_async_remote_copy(
            src_ref=source,
            dst_ref=target,
            send_sem=self.send_sems.at[self.base + slot],
            recv_sem=self.recv_sems.at[self.base + slot],
            device_id=(self.dp, there),
            device_id_type=MESH,
        )

    def beside(self, step):
        return lax.rem(self.y + step + 4, 4) * 2 + self.xl

    def send(self, slot):
        y, xl = self.y, self.xl
        if slot == 0:
            return self.copy(self.block, self.part(y, xl), y * 2 + 1 - xl, 0)
        step = 1 if slot % 2 else -1
        if slot < 3:
            return self.copy(self.block, self.part(y, xl), self.beside(step), slot)
        spot = self.part(y, 1 - xl) if slot < 5 else self.part(y - step, xl if step == 1 else 1 - xl)
        return self.copy(spot, spot, self.beside(step), slot)

    def arrive(self, slot):
        y, xl = self.y, self.xl
        if slot == 0:
            spot = self.part(y, 1 - xl)
        else:
            step = 1 if slot % 2 else -1
            if slot < 5:
                spot = self.part(y - step, xl if slot < 3 else 1 - xl)
            else:
                spot = self.part(y + 2, xl if step == 1 else 1 - xl)
        self.copy(spot, spot, self.beside(1), slot).wait_recv()

    def first(self):
        self.own.start()
        for slot in range(3):
            self.send(slot).start()

    def second(self):
        self.arrive(0)
        for slot in (3, 4):
            self.send(slot).start()

    def third(self):
        self.arrive(1)
        self.send(5).start()
        self.arrive(4)
        self.send(6).start()

    def finish(self):
        for slot in (2, 3, 5, 6):
            self.arrive(slot)
        self.own.wait()
        for slot in range(7):
            self.send(slot).wait_send()


class Column:
    def __init__(self, block, spot, local_sem, send_sems, recv_sems, base):
        self.dp, self.me = lax.axis_index("dp"), lax.axis_index("seq")
        self.z = lax.rem(self.dp // 2, 4)
        self.block, self.spot, self.local_sem = block, spot, local_sem
        self.send_sems, self.recv_sems, self.base = send_sems, recv_sems, base

    def at(self, step):
        return self.spot(lax.rem(self.z + step + 4, 4))

    def copy(self, source, target, step, slot):
        there = self.dp + 2 * (lax.rem(self.z + step + 4, 4) - self.z)
        return pltpu.make_async_remote_copy(
            src_ref=source,
            dst_ref=target,
            send_sem=self.send_sems.at[self.base + slot],
            recv_sem=self.recv_sems.at[self.base + slot],
            device_id=(there, self.me),
            device_id_type=MESH,
        )

    def own(self):
        return pltpu.make_async_copy(self.block, self.at(0), self.local_sem)

    def half(self, step, slot):
        return self.at(step).at[pl.ds(0 if slot == 2 else TOK // 2, TOK // 2), :]

    def first(self):
        if self.local_sem is not None:
            self.own().start()
        self.copy(self.block, self.at(0), 1, 0).start()
        self.copy(self.block, self.at(0), -1, 1).start()

    def second(self):
        for slot, step in ((0, 1), (1, -1)):
            self.copy(self.block, self.at(-step), step, slot).wait_recv()
            piece = self.half(-step, slot + 2)
            self.copy(piece, piece, step, slot + 2).start()

    def near(self):
        for slot, step in ((0, 1), (1, -1)):
            self.copy(self.block, self.at(-step), step, slot).wait_recv()
            self.copy(self.block, self.at(0), step, slot).wait_send()
        self.own().wait()

    def sent_near(self):
        for slot, step in ((0, 1), (1, -1)):
            self.copy(self.block, self.at(0), step, slot).wait_send()

    def forward(self):
        for slot, step in ((0, 1), (1, -1)):
            piece = self.half(-step, slot + 2)
            self.copy(piece, piece, step, slot + 2).start()

    def far(self):
        for slot, step in ((0, 1), (1, -1)):
            piece = self.half(2, slot + 2)
            self.copy(piece, piece, step, slot + 2).wait_recv()
            piece = self.half(-step, slot + 2)
            self.copy(piece, piece, step, slot + 2).wait_send()

    def finish(self):
        self.far()
        for slot, step in ((0, 1), (1, -1)):
            self.copy(self.block, self.at(0), step, slot).wait_send()
        if self.local_sem is not None:
            self.own().wait()


def front_kernel(
    tok_ref, mem_ref, cot_ref, gain_ref, bias_ref, ids_ref, offsets_ref, pair_ref,
    qkv_hbm, ckv_hbm, out_hbm, query_hbm,
    x1_ref, n2_ref, o1_ref, o2_ref, heads_ref, memh_ref, cqh_ref, mix1_ref, mix2_ref,
    inv1_ref, inv2_ref, n1_ref, exp1_hbm, exp2_hbm, cot_all, mem_all, n2_all, o1_all,
    qkv_w, ckv_w, out_w, query_w, give_heads, give_mem, cq_ref, exp1_ref, exp2_ref,
    load_sems, keep_sems, exp_sems, send_sems, recv_sems,
):
    me = lax.axis_index("seq")
    y, xl = me // 2, lax.rem(me, 2)
    dp = lax.axis_index("dp")
    barrier = greet_row()
    for step in (1, 2, 3):
        z = lax.rem(dp // 2, 4)
        there = dp + 2 * (lax.rem(z + step, 4) - z)
        pl.semaphore_signal(barrier, inc=1, device_id=(there, me), device_id_type=MESH)
    order = [lax.rem(y + step, 4) for step in (1, 2, 3, 0)]
    loads = {}
    for step in range(4):
        for part in range(3):
            cols = pl.ds(pl.multiple_of(part * WIDTH + order[step] * 256, 256), 256)
            loads["qkv", step, part] = pltpu.make_async_copy(
                qkv_hbm.at[:, cols], qkv_w.at[:, cols], load_sems.at[step * 3 + part]
            )
    for step in range(4):
        for part in range(2):
            cols = pl.ds(pl.multiple_of(part * WIDTH + order[step] * 256, 256), 256)
            loads["ckv", step, part] = pltpu.make_async_copy(
                ckv_hbm.at[:, cols], ckv_w.at[:, cols], load_sems.at[12 + step * 2 + part]
            )
    loads["out"] = pltpu.make_async_copy(out_hbm, out_w, load_sems.at[20])
    loads["query"] = pltpu.make_async_copy(query_hbm, query_w, load_sems.at[21])
    for name, one in loads.items():
        if name[0] == "qkv":
            one.start()

    give_qkv, give_kv, back1, give_q, back2 = (
        Exchange(send_sems, recv_sems, 8 * index) for index in range(5)
    )
    own_rows = aligned(me, TOK)
    columns = [
        Column(
            block, lambda at, whole=whole: whole.at[at], keep_sems.at[7 + index],
            send_sems, recv_sems, 40 + 4 * index,
        )
        for index, (block, whole) in enumerate(
            ((cot_ref, cot_all), (mem_ref, mem_all), (o1_ref, o1_all), (n2_ref, n2_all))
        )
    ]

    unit, _ = norm_unit(tok_ref[...].astype(F32))
    n1 = (unit * gain_ref[0:1, :] + bias_ref[0:1, :]).astype(LOW)
    n1_ref[...] = n1
    mem = mem_ref[...]
    for kind, count, source, give, heads, exchange in (
        ("qkv", 3, n1, give_heads, heads_ref, give_qkv),
        ("ckv", 2, mem, give_mem, memh_ref, give_kv),
    ):
        for step in range(4):
            at = order[step]
            own = aligned(at, 256)
            for part in range(count):
                loads[kind, step, part].wait()
                cols = pl.ds(pl.multiple_of(part * WIDTH + at * 256, 256), 256)
                if kind == "qkv":
                    value = dot(source, qkv_w[:, cols])
                    if part == 0:
                        value = (value + bias_ref[3:4, own]) * SCALE
                    elif part == 2:
                        value = value + bias_ref[4:5, own]
                else:
                    value = dot(source, ckv_w[:, cols])
                    if part == 1:
                        value = value + bias_ref[7:8, own]
                low = value.astype(LOW)
                give[2 * at, :, part * PAIR : part * PAIR + PAIR] = low[:, :PAIR]
                give[2 * at + 1, :, part * PAIR : part * PAIR + PAIR] = low[:, PAIR:]
            if kind == "qkv" and step == 0:
                for name, one in loads.items():
                    if name[0] != "qkv":
                        one.start()
                pl.semaphore_wait(barrier, SEQ - 1 + 3)
                columns[0].first()
                columns[1].first()
            there = heads.at[own_rows, :]
            if step < 3:
                exchange.push(give.at[2 * at], there, 2 * at, False)
                exchange.push(give.at[2 * at + 1], there, 2 * at + 1, False)
            else:
                partner = 2 * y + 1 - xl
                exchange.push(give.at[partner], there, partner, False)
                keep = pltpu.make_async_copy(
                    give.at[me], there, keep_sems.at[2 if kind == "qkv" else 3]
                )
                keep.start()
                loads[kind] = keep

    def attended(allowed_of, query_of, key_t, value_ref, value_at, mix_ref, inv_ref, exp_ref,
                 exp_hbm, exp_base, causal, back, target_ref, keep_sem):
        tile = 256
        for step in range(ROW // tile):
            rows = slice(step * tile, step * tile + tile)
            width = (step + 1) * tile if causal else ROW
            mixture, inverse = attend_tile(
                query_of(rows), key_t[:, 0:width], value_ref[0:width, value_at], allowed_of(step, width),
                exp_ref, rows, width,
            )
            mix_ref[rows, :] = mixture.astype(LOW)
            inv_ref[rows, :] = inverse
            for half in range(2):
                there = 2 * step + half
                back.push(
                    mix_ref.at[there * TOK : there * TOK + TOK, :],
                    target_ref.at[:, aligned(me, PAIR)], there, True,
                )
            for head in range(2):
                spot = (head, rows, slice(0, width))
                pltpu.make_async_copy(
                    exp_ref.at[spot], exp_hbm.at[spot], exp_sems.at[exp_base + step * 2 + head]
                ).start()
        keep = pltpu.make_async_copy(
            mix_ref.at[own_rows, :], target_ref.at[:, aligned(me, PAIR)], keep_sem
        )
        keep.start()
        return keep

    loads["qkv"].wait()
    give_qkv.receive(lambda sender: heads_ref.at[aligned(sender, TOK), :])
    key_t = heads_ref[:, PAIR : 2 * PAIR].T
    keep1 = attended(
        lambda step, width: self_allowed(offsets_ref, step, 256, width),
        lambda rows: heads_ref[rows, 0:PAIR], key_t, heads_ref, slice(2 * PAIR, 3 * PAIR),
        mix1_ref, inv1_ref, exp1_ref, exp1_hbm, 0, True, back1, o1_ref, keep_sems.at[4],
    )
    columns[0].second()
    columns[1].second()
    keep1.wait()
    loads["out"].wait()
    back1.receive(lambda sender: o1_ref.at[:, aligned(sender, PAIR)])
    columns[2].first()
    x1 = tok_ref[...].astype(F32) + dot(o1_ref[...], out_w[...]) + bias_ref[5:6, :]
    x1_ref[...] = x1
    unit, _ = norm_unit(x1)
    n2 = (unit * gain_ref[1:2, :] + bias_ref[1:2, :]).astype(LOW)
    n2_ref[...] = n2
    columns[3].first()
    loads["query"].wait()
    for step in range(4):
        at = order[step]
        own = aligned(at, 256)
        cq_ref[:, own] = ((dot(n2, query_w[:, own]) + bias_ref[6:7, own]) * SCALE).astype(LOW)
        for half in range(2):
            there = 2 * at + half if step < 3 else 2 * y + 1 - xl
            if step == 3 and half == 1:
                continue
            give_q.push(cq_ref.at[:, aligned(there, PAIR)], cqh_ref.at[own_rows, :], there, False)
    keep = pltpu.make_async_copy(cq_ref.at[:, aligned(me, PAIR)], cqh_ref.at[own_rows, :], keep_sems.at[5])
    keep.start()
    loads["ckv"].wait()
    give_kv.receive(lambda sender: memh_ref.at[aligned(sender, TOK), :])
    key_t = memh_ref[:, 0:PAIR].T
    keep.wait()
    give_q.receive(lambda sender: cqh_ref.at[aligned(sender, TOK), :])
    ids = ids_ref[...]
    keep2 = attended(
        lambda step, width: cross_allowed(ids, offsets_ref, pair_ref, step, 256),
        lambda rows: cqh_ref[rows, :], key_t, memh_ref, slice(PAIR, 2 * PAIR),
        mix2_ref, inv2_ref, exp2_ref, exp2_hbm, 8, False, back2, o2_ref, keep_sems.at[6],
    )
    keep2.wait()
    back2.receive(lambda sender: o2_ref.at[:, aligned(sender, PAIR)])
    for step in range(4):
        rows = slice(step * 256, step * 256 + 256)
        for head in range(2):
            spot = (head, rows, slice(0, step * 256 + 256))
            pltpu.make_async_copy(
                exp1_ref.at[spot], exp1_hbm.at[spot], exp_sems.at[step * 2 + head]
            ).wait()
            spot = (head, rows, slice(0, ROW))
            pltpu.make_async_copy(
                exp2_ref.at[spot], exp2_hbm.at[spot], exp_sems.at[8 + step * 2 + head]
            ).wait()
    for exchange in (give_qkv, give_kv, back1, give_q, back2):
        exchange.drain()
    for column in columns[:2]:
        column.finish()
    for column in columns[2:]:
        column.near()


def front_call(operands):
    dma = pltpu.SemaphoreType.DMA
    vmem = pltpu.VMEM
    heads = shaped((ROW, PAIR))
    token = shaped((TOK, WIDTH))
    inverse = shaped((ROW, PAIR), F32)
    exps = shaped((2, ROW, ROW))
    four = shaped((4, TOK, WIDTH))
    return pl.pallas_call(
        front_kernel,
        out_shape=(
            shaped((TOK, WIDTH), F32), token, token, token, shaped((ROW, 3 * PAIR)),
            shaped((ROW, 2 * PAIR)), heads, heads, heads, inverse, inverse, token,
            exps, exps, four, four, four, four,
        ),
        in_specs=[spec_vmem()] * 6 + [spec_smem()] * 2 + [spec_any()] * 4,
        out_specs=(spec_vmem(),) * 12 + (spec_any(),) * 6,
        scratch_shapes=[
            vmem((WIDTH, 3 * WIDTH), LOW), vmem((WIDTH, 2 * WIDTH), LOW), vmem((WIDTH, WIDTH), LOW),
            vmem((WIDTH, WIDTH), LOW), vmem((SEQ, TOK, 3 * PAIR), LOW), vmem((SEQ, TOK, 2 * PAIR), LOW),
            vmem((TOK, WIDTH), LOW), vmem((2, ROW, ROW), LOW), vmem((2, ROW, ROW), LOW),
            dma((22,)), dma((11,)), dma((16,)), dma((56,)), dma((56,)),
        ],
        compiler_params=pltpu.CompilerParams(
            collective_id=2, has_side_effects=True, vmem_limit_bytes=56 * MIB
        ),
        cost_estimate=pl.CostEstimate(
            flops=2 * TOK * WIDTH * 7 * WIDTH, bytes_accessed=60 * MIB, transcendentals=0
        ),
        name="front",
    )(*operands)


LANES = 256


def wrap(index):
    return lax.rem(index + 8, 4)


def device_of(core, x, y, z):
    return ((x // 2) * 8 + z * 2 + core, y * 2 + lax.rem(x, 2))


class Place:
    def __init__(self):
        self.dp = lax.axis_index("dp")
        self.seq = lax.axis_index("seq")
        self.core = lax.rem(self.dp, 2)
        self.y, self.xl = self.seq // 2, lax.rem(self.seq, 2)
        self.at = {
            "x": (self.dp // 8) * 2 + self.xl,
            "y": self.y,
            "z": lax.rem(self.dp // 2, 4),
        }
        self.z = self.at["z"]
        self.other = (self.dp + 1 - 2 * self.core, self.seq)
        self.rank = lax.rem(self.dp, 8)

    def member(self, distance):
        rank = lax.rem(self.rank + distance + 8, 8)
        return (self.dp - self.rank + rank, self.seq), rank

    def neighbour(self, axis, step):
        at = dict(self.at)
        at[axis] = wrap(at[axis] + step)
        return device_of(self.core, **at)


class Sum:
    def __init__(self, place, grads, lands, flows, send_sems, recv_sems, base):
        self.place, self.grads, self.lands, self.flows = place, grads, lands, flows
        self.send_sems, self.recv_sems, self.base = send_sems, recv_sems, base
        self.open_sends = []

    def view(self, order, stage, block, first, rows):
        index = {"x": slice(None), "y": slice(None)}
        for done in range(stage):
            index[order[done]] = self.place.at[order[done]]
        index[order[stage]] = block
        return (index["x"], index["y"], slice(first, first + rows), slice(None))

    def land(self, stage, slot, first, rows):
        return (slot,) + (slice(None),) * (1 - stage) + (slice(first, first + rows), slice(None))

    def spans(self, flow):
        order, first, low, high = self.flows[flow]
        return order, (first, low), (first + low, high)

    def copy(self, stage, flow, kind):
        order, low, high = self.spans(flow)
        axis = order[stage]
        step = (2, 2, 1, -1, 1, -1)[kind]
        way = (1, -1, 1, -1, 1, -1)[kind]
        first, rows = (low, high, high, low, low, high)[kind]
        slot = (0, 0, 1, 1, 2, 2)[kind]
        at = self.base + (stage * len(self.flows) + flow) * 6 + kind
        return pltpu.make_async_remote_copy(
            src_ref=self.grads.at[
                self.view(order, stage, wrap(self.place.at[axis] + step), first, rows)
            ],
            dst_ref=self.lands[stage].at[self.land(stage, slot, first, rows)],
            send_sem=self.send_sems.at[at],
            recv_sem=self.recv_sems.at[at],
            device_id=self.place.neighbour(axis, way),
            device_id_type=MESH,
        )

    def straight(self, stage, flow, distance):
        order, (first, low), (_, high) = self.spans(flow)
        axis, rows = order[stage], low + high
        at = self.base + (stage * len(self.flows) + flow) * 6 + distance
        return pltpu.make_async_remote_copy(
            src_ref=self.grads.at[
                self.view(order, stage, wrap(self.place.at[axis] + distance), first, rows)
            ],
            dst_ref=self.lands[stage].at[self.land(stage, distance - 1, first, rows)],
            send_sem=self.send_sems.at[at],
            recv_sem=self.recv_sems.at[at],
            device_id=self.place.neighbour(axis, distance),
            device_id_type=MESH,
        )

    def add(self, stage, flow, step, span, slots):
        order, _, _ = self.spans(flow)
        at = self.view(order, stage, wrap(self.place.at[order[stage]] + step), *span)
        total = self.grads[at].astype(F32)
        for slot in slots:
            total = total + self.lands[stage][self.land(stage, slot, *span)].astype(F32)
        self.grads[at] = total.astype(LOW)

    def start(self, copy):
        copy.start()
        self.open_sends.append(copy)

    def run(self):
        flows = range(len(self.flows))
        for kind in range(4):
            for flow in flows:
                self.start(self.copy(0, flow, kind))
        yield
        for flow in flows:
            _, low, high = self.spans(flow)
            self.copy(0, flow, 0).wait_recv()
            self.add(0, flow, 1, low, (0,))
            self.start(self.copy(0, flow, 4))
            self.copy(0, flow, 1).wait_recv()
            self.add(0, flow, -1, high, (0,))
            self.start(self.copy(0, flow, 5))
        yield
        for flow in flows:
            _, low, high = self.spans(flow)
            for kind in (2, 3, 4, 5):
                self.copy(0, flow, kind).wait_recv()
            self.add(0, flow, 0, low, (1, 2))
            self.add(0, flow, 0, high, (1, 2))
            for distance in (1, 2, 3):
                self.start(self.straight(1, flow, distance))
        yield
        for flow in flows:
            _, low, high = self.spans(flow)
            for distance in (1, 2, 3):
                self.straight(1, flow, distance).wait_recv()
            self.add(1, flow, 0, (low[0], low[1] + high[1]), (0, 1, 2))
        yield

    def run_straight(self):
        flows = range(len(self.flows))
        for stage in range(2):
            for flow in flows:
                for distance in (1, 2, 3):
                    self.start(self.straight(stage, flow, distance))
            yield
            for flow in flows:
                _, low, high = self.spans(flow)
                for distance in (1, 2, 3):
                    self.straight(stage, flow, distance).wait_recv()
                self.add(stage, flow, 0, (low[0], low[1] + high[1]), (0, 1, 2))
        yield

    def drain(self):
        for copy in self.open_sends:
            copy.wait_send()
        self.open_sends = []


FF_CHUNK = 512
HALF_CHUNKS = FF // FF_CHUNK // 2
FLOWS_F = (("xy", 0, 64, 64), ("yx", 128, 64, 64))
FLOWS_C = (("xy", 0, 32, 32), ("yx", 64, 32, 32))


class Eight:
    def __init__(self, place, send_sems, recv_sems, base):
        self.place, self.send_sems, self.recv_sems = place, send_sems, recv_sems
        self.base, self.last = base, None

    def copy(self, source, target, distance):
        device, _ = self.place.member(distance)
        return pltpu.make_async_remote_copy(
            src_ref=source,
            dst_ref=target,
            send_sem=self.send_sems.at[self.base + distance],
            recv_sem=self.recv_sems.at[self.base + distance],
            device_id=device,
            device_id_type=MESH,
        )

    def push(self, source_of, target):
        for distance in range(1, 8):
            _, rank = self.place.member(distance)
            self.last = (source_of(rank), target)
            self.copy(source_of(rank), target, distance).start()

    def receive(self, place_of):
        for distance in range(1, 8):
            _, rank = self.place.member(-distance)
            spot = place_of(rank)
            self.copy(spot, spot, distance).wait_recv()

    def drain(self):
        for distance in range(1, 8):
            self.copy(*self.last, distance).wait_send()


def back_kernel(
    gain_ref, bias_ref, ebias_ref,
    o2_hbm, x1_hbm, cot_hbm, tok_hbm, n1_hbm, cot4_hbm, mem4_hbm, n24_hbm, o14_hbm,
    heads_hbm, memh_hbm, cqh_hbm, mix1_hbm, mix2_hbm, inv1_hbm, inv2_hbm, exp1_hbm, exp2_hbm,
    qkv_hbm, ckv_hbm, out_hbm, query_hbm, cross_hbm, expand_hbm, reduce_hbm,
    output_ref, gtok_ref, gmem_ref, all_f, all_c, all_q, all_v,
    n1_all, ring_e, ring_r, cross_w, exp_ref, x1_ref, cot_ref, tok_ref,
    heads_ref, memh_ref, cqh_ref, mix1_ref, mix2_ref, inv1_ref, inv2_ref,
    a_n3, a_cot, a_o2, a_n2, a_o1, a_mem, act_in, dfe_in, act_out, dfe_out,
    b_dc, b_e2, b_da, b_kv,
    dc_ref, da_ref, acc_ref, dn_ref, expand_sums, vec_ref,
    do2_ref, do1_ref, do2h_ref, do1h_ref, sums_ref, e2_ref, dkv_ref, e1_ref, dkt_ref, dvt_ref,
    grads_f, land_f1, land_f2, grads_c, land_c1, land_c2,
    piece_f, piece_c, weight_ref, weight_in, weight_sum, piece_q, vec_out, vec_in, piece_v,
    load_sems, ring_sems, keep_sems, pair_send, pair_recv, send_sems, recv_sems,
    dp_send, dp_recv, sum_send, sum_recv, eight_send, eight_recv, column_send, column_recv,
):
    place = Place()
    core, y, xl, me, dp = place.core, place.y, place.xl, place.seq, place.dp
    partner = 2 * y + 1 - xl
    own_rows = aligned(me, TOK)
    order = [lax.rem(y + step, 4) for step in (1, 2, 3, 0)]

    barrier = greet_row()
    for distance in range(1, DP):
        pl.semaphore_signal(
            barrier, inc=1, device_id=(lax.rem(dp + distance, DP), me), device_id_type=MESH
        )
    outer = place.neighbour("x", 2 * xl - 1)
    pl.semaphore_signal(barrier, inc=1, device_id=outer, device_id_type=MESH)

    def load(source, target, sem):
        copy = pltpu.make_async_copy(source, target, load_sems.at[sem])
        copy.start()
        return copy

    z, rank = place.z, place.rank
    rank_rows = aligned(rank, TOK)

    def chunk_of(step):
        return lax.rem(rank + 1 + step, 8)

    def ring_copies(step, slot):
        copies = []
        for block in range(2):
            span = aligned(chunk_of(step) + 8 * block, 256)
            to = pl.ds(pl.multiple_of(slot * FF_CHUNK + block * 256, 256), 256)
            at = slot * 4 + block * 2
            copies += [
                pltpu.make_async_copy(expand_hbm.at[:, span], ring_e.at[:, to], ring_sems.at[at]),
                pltpu.make_async_copy(
                    reduce_hbm.at[span, :], ring_r.at[to, :], ring_sems.at[at + 1]
                ),
            ]
        return copies

    loads = [
        load(o2_hbm, a_o2.at[z, core], 0), load(cross_hbm, cross_w, 1), load(x1_hbm, x1_ref, 2),
        load(cot_hbm, cot_ref, 3)
    ]
    gather = Gather(
        n1_hbm, lambda at: n1_all.at[aligned(at, TOK), :], keep_sems.at[0], send_sems, recv_sems, 64
    )
    gather_f = Gather(
        piece_f, lambda at: all_f.at[at], keep_sems.at[13], send_sems, recv_sems, 79
    )
    col_n3, col_o2, col_n2, col_o1 = (
        Column(
            block, lambda at, whole=whole: whole.at[at, core], None,
            column_send, column_recv, 4 * index,
        )
        for index, (block, whole) in enumerate(
            (
                (a_n3.at[z, core], a_n3), (o2_hbm, a_o2), (a_n2.at[z, core], a_n2),
                (a_o1.at[z, core], a_o1),
            )
        )
    )
    to_core = []

    def both_cores(whole):
        slot = len(to_core)
        copy = pltpu.make_async_remote_copy(
            src_ref=whole.at[:, core],
            dst_ref=whole.at[:, core],
            send_sem=pair_send.at[slot],
            recv_sem=pair_recv.at[slot],
            device_id=place.other,
            device_id_type=MESH,
        )
        copy.start()
        arrival = pltpu.make_async_remote_copy(
            src_ref=whole.at[:, 1 - core],
            dst_ref=whole.at[:, 1 - core],
            send_sem=pair_send.at[slot],
            recv_sem=pair_recv.at[slot],
            device_id=place.other,
            device_id_type=MESH,
        )
        to_core.append((copy, arrival))

    blocks_to_core = []

    def block_to_core(whole, step):
        slot = 7 + len(blocks_to_core)
        at = lax.rem(z + step + 4, 4)

        def copy(half):
            return pltpu.make_async_remote_copy(
                src_ref=whole.at[at, half],
                dst_ref=whole.at[at, half],
                send_sem=pair_send.at[slot],
                recv_sem=pair_recv.at[slot],
                device_id=place.other,
                device_id_type=MESH,
            )

        copy(core).start()
        blocks_to_core.append((copy(core), copy(1 - core)))

    give_act, give_dfe, give_dc, give_be2, give_kv, give_da, join_f, join_c = (
        Eight(place, eight_send, eight_recv, 8 * index) for index in range(8)
    )

    for one in loads[:3]:
        one.wait()
    for step in range(4):
        for one in ring_copies(step, step):
            one.start()
    x2 = x1_ref[...] + dot(a_o2[z, core], cross_w[...]) + bias_ref[8:9, :]
    unit3, inverse3 = norm_unit(x2)
    a_n3[z, core] = (unit3 * gain_ref[2:3, :] + bias_ref[2:3, :]).astype(LOW)
    acc_ref[...] = x2 + bias_ref[9:10, :]
    dn_ref[...] = jnp.zeros_like(dn_ref)
    loads[3].wait()
    pl.semaphore_wait(barrier, SEQ - 1 + DP - 1 + 1)
    gather.first()
    col_n3.first()
    root = math.sqrt(2.0 / math.pi)

    def feed(step, slot, own):
        for one in ring_copies(step, slot):
            one.wait()
        chunk = chunk_of(step)
        span = aligned(slot, FF_CHUNK)
        offset = jnp.concatenate(
            [ebias_ref[:, aligned(chunk + 8 * block, 256)] for block in range(2)], 1
        )
        hidden = dot(a_n3[z, core], ring_e[:, span]) + offset
        square = hidden * hidden
        curve = jnp.tanh(root * hidden * (1.0 + 0.044715 * square))
        share = 0.5 * (1.0 + curve)
        act = (hidden * share).astype(LOW)
        slope = share + 0.5 * hidden * (1.0 - curve * curve) * (
            root * (1.0 + 3.0 * 0.044715 * square)
        )
        acc_ref[...] += dot(act, ring_r[span, :])
        grad_act = dot_nt(cot_ref[...], ring_r[span, :])
        grad_hidden = (slope * grad_act).astype(LOW)
        if own:
            act_in[rank_rows, :] = act
            dfe_in[rank_rows, :] = grad_hidden
        else:
            act_out[step] = act
            dfe_out[step] = grad_hidden
            give_act.copy(act_out.at[step], act_in.at[rank_rows, :], step + 1).start()
            give_dfe.copy(dfe_out.at[step], dfe_in.at[rank_rows, :], step + 1).start()
        expand_sums[chunk] = column_sum(grad_hidden.astype(F32))
        dn_ref[...] += dot_nt(grad_hidden, ring_e[:, span])

    gathered = [
        (source.at[at], whole.at[at, core])
        for source, whole, steps in (
            (cot4_hbm, a_cot, (0, 1, 2, 3)), (mem4_hbm, a_mem, (0, 1, 2, 3)),
            (n24_hbm, a_n2, (-1, 0, 1)), (o14_hbm, a_o1, (-1, 0, 1)),
        )
        for at in [lax.rem(z + step + 4, 4) for step in steps]
    ]
    gathered = [
        pltpu.make_async_copy(source, target, load_sems.at[24 + index])
        for index, (source, target) in enumerate(gathered)
    ]

    def feed_step(step, carry):
        feed(step, lax.rem(step, 4), False)

        @pl.when(step < 4)
        def _():
            for one in ring_copies(step + 4, step):
                one.start()

        @pl.when(step == 2)
        def _():
            gather.second()

        @pl.when(step == 4)
        def _():
            col_n3.second()

        return carry

    lax.fori_loop(0, 7, feed_step, 0)
    feed(7, 3, True)
    give_act.last = (act_out.at[0], act_in.at[rank_rows, :])
    give_dfe.last = (dfe_out.at[0], dfe_in.at[rank_rows, :])
    col_o2.first()
    for one in gathered:
        one.start()
    kept = [
        load(memh_hbm, memh_ref, 9), load(cqh_hbm, cqh_ref, 10), load(mix2_hbm, mix2_ref, 11),
        load(inv2_hbm, inv2_ref, 12), load(exp2_hbm, exp_ref, 13),
    ]
    later = [
        load(query_hbm, ring_r.at[1024:2048, :], 14), load(out_hbm, ring_r.at[0:1024, :], 15),
        load(ckv_hbm, ring_e, 16),
    ]
    kept1 = [
        load(heads_hbm, heads_ref, 17), load(mix1_hbm, mix1_ref, 18), load(inv1_hbm, inv1_ref, 19),
        load(tok_hbm, tok_ref, 20),
    ]
    output_ref[...] = acc_ref[...].astype(LOW)
    dn3 = dn_ref[...]
    grad = cot_ref[...].astype(F32)
    dx2 = grad + norm_back(dn3, unit3, inverse3, gain_ref[2:3, :])
    acc_ref[...] = dx2
    dc_ref[...] = dx2.astype(LOW)

    give_do2, give_e2, give_k2, give_v2, give_do1, give_q1, give_k1, give_v1 = (
        Exchange(send_sems, recv_sems, 8 * index) for index in range(8)
    )

    def push_heads(exchange, low_ref, weight_of, values, target, keep_slot):
        for step in range(4):
            at = order[step]
            low_ref[:, aligned(at, 256)] = dot_nt(values, weight_of(aligned(at, 256))).astype(LOW)
            if step < 3:
                for half in range(2):
                    there = 2 * at + half
                    exchange.push(
                        low_ref.at[:, aligned(there, PAIR)], target.at[own_rows, :], there, False
                    )
            else:
                exchange.push(
                    low_ref.at[:, aligned(partner, PAIR)], target.at[own_rows, :], partner, False
                )
        keep = pltpu.make_async_copy(
            low_ref.at[:, aligned(me, PAIR)], target.at[own_rows, :], keep_sems.at[keep_slot]
        )
        keep.start()
        return keep

    keep_do2 = push_heads(
        give_do2, do2_ref, lambda rows: cross_w[rows, :], dc_ref[...], do2h_ref, 1
    )

    def share(exchange, source, target, width):
        exchange.push(lambda to: source.at[:, aligned(to, width)], target.at[rank_rows, :])
        target[rank_rows, :] = source[:, aligned(rank, width)]

    share(give_dc, dc_ref, b_dc, PAIR)
    vec_ref[2:3, :] = column_sum(dn3 * unit3)
    vec_ref[5:6, :] = column_sum(dn3)
    vec_ref[11:12, :] = column_sum(dc_ref[...].astype(F32))
    vec_ref[12:13, :] = column_sum(grad)

    def left_of(whole, group):
        return whole[:, :, :, aligned(group, 128)].reshape(ROW, 128)

    def rows_of(group, block):
        to = lax.rem(group, 4) * 2 + block
        return pl.ds(pl.multiple_of(to * 16, 16), 16)

    def fill_f(group, carry):
        result = dot_tn(left_of(a_n3, group), dfe_in[...]).astype(LOW)
        for block in range(2):
            for yy in range(4):
                at = (block * 4 + yy) * 16
                for col in range(2):
                    grads_f[(group // 4) * 2 + col, yy, rows_of(group, block), :] = result[
                        at : at + 16, col * LANES : col * LANES + LANES
                    ]
        return carry

    def fill_reduce():
        for xh in range(2):
            result = dot_tn(
                act_in[:, xh * 256 : xh * 256 + 256], a_cot[...].reshape(ROW, WIDTH)
            ).astype(LOW)
            for yy in range(4):
                for col in range(2):
                    for sub in range(2):
                        at = (col * 2 + sub) * LANES
                        grads_f[xh * 2 + col, yy, 128 + sub * 64 : 192 + sub * 64, :] = result[
                            yy * 64 : yy * 64 + 64, at : at + LANES
                        ]

    def fill_c():
        parts = ((a_n2, b_e2, 0, 0, PAIR), (a_o1, b_da, 0, PAIR, PAIR), (a_o2, b_dc, 0, 2 * PAIR, PAIR),
                 (a_mem, b_kv, 1, 0, 256))
        for whole, right, x_at, lane, width in parts:
            result = dot_tn(right[...], whole[...].reshape(ROW, WIDTH)).T.astype(LOW)
            for xh in range(2):
                for to in range(8):
                    for yy in range(4):
                        at = xh * 512 + to * 64 + yy * 16
                        grads_c[
                            xh * 2 + x_at, yy, to * 16 : to * 16 + 16, lane : lane + width
                        ] = result[at : at + 16, :]
        for xh in range(2):
            grads_c[xh * 2 + 1, :, :, 256:384] = jnp.zeros((4, 128, PAIR), LOW)

    sum_f = Sum(place, grads_f, (land_f1, land_f2), FLOWS_F, sum_send, sum_recv, 0)
    sum_c = Sum(place, grads_c, (land_c1, land_c2), FLOWS_C, sum_send, sum_recv, 24)
    run_f, run_c = sum_f.run(), sum_c.run_straight()

    def attend_back(query, key_rows, value_rows, grad_ref, mix_ref, inv_ref, causal, after_tile):
        tile = 256
        scaled = (grad_ref[...].astype(F32) * inv_ref[...]).astype(LOW)
        lanes = head_lanes(ROW)
        product = scaled.astype(F32) * mix_ref[...].astype(F32)
        inner = [jnp.sum(pick_head(product, lanes, head), -1, keepdims=True) for head in range(2)]
        value_t = value_rows.T
        query_t = query.T
        scaled_t = scaled.T
        dkt_ref[...] = jnp.zeros_like(dkt_ref)
        dvt_ref[...] = jnp.zeros_like(dvt_ref)
        tile_lanes = head_lanes(tile)
        steps = range(ROW // tile)
        for step in reversed(steps) if causal else steps:
            rows = slice(step * tile, step * tile + tile)
            width = (step + 1) * tile if causal else ROW
            parts = []
            for head in range(2):
                own = slice(head * HEAD_DIM, head * HEAD_DIM + HEAD_DIM)
                exponent = exp_ref[head, rows, 0:width]
                grad_p = dot(pick_head(scaled[rows, :], tile_lanes, head), value_t[:, 0:width])
                grad_s = (exponent.astype(F32) * (grad_p - inner[head][rows, :])).astype(LOW)
                parts.append(dot(grad_s, key_rows[0:width, :]))
                dkt_ref[own, 0:width] += dot(query_t[own, rows], grad_s)
                dvt_ref[own, 0:width] += dot(scaled_t[own, rows], exponent)
            grad_q = jnp.where(tile_lanes, parts[0], parts[1]).astype(LOW) * SCALE
            sums_ref[rows, 0:PAIR] = grad_q.astype(LOW)
            after_tile(step, rows)

    def send_part(exchange, part, there, target, column):
        exchange.push(
            sums_ref.at[there * TOK : there * TOK + TOK, part * PAIR : part * PAIR + PAIR],
            target.at[:, pl.ds(pl.multiple_of(column + me * PAIR, PAIR), PAIR)], there, True,
        )

    def keep_part(part, target, column, slot):
        copy = pltpu.make_async_copy(
            sums_ref.at[own_rows, part * PAIR : part * PAIR + PAIR],
            target.at[:, pl.ds(pl.multiple_of(column + me * PAIR, PAIR), PAIR)],
            keep_sems.at[slot],
        )
        copy.start()
        return copy

    def from_peers(target, column):
        return lambda sender: target.at[
            :, pl.ds(pl.multiple_of(column + sender * PAIR, PAIR), PAIR)
        ]

    def join(exchange, grads, piece, keep_slot, rest):
        block = grads.at[place.at["x"], place.at["y"]]
        mine = pl.ds(pl.multiple_of(rank * 16, 16), 16)
        exchange.push(
            lambda to: block.at[pl.ds(pl.multiple_of(to * 16, 16), 16), :], piece.at[mine, :]
        )
        keeps = [
            pltpu.make_async_copy(block.at[mine, :], piece.at[mine, :], keep_sems.at[keep_slot])
        ]
        if rest:
            keeps.append(
                pltpu.make_async_copy(
                    block.at[pl.ds(128, 128), :], piece.at[pl.ds(128, 128), :],
                    keep_sems.at[keep_slot + 1],
                )
            )
        for one in keeps:
            one.start()
        return keeps

    def joined(exchange, piece, keeps):
        for one in keeps:
            one.wait()
        exchange.receive(lambda to: piece.at[pl.ds(pl.multiple_of(to * 16, 16), 16), :])

    spreads = []

    def spread(piece, whole, base, slot):
        exchange = Exchange(send_sems, recv_sems, base)
        for distance in range(1, SEQ):
            exchange.push(piece, whole.at[me], lax.rem(me + distance, SEQ), False)
        keep = pltpu.make_async_copy(piece, whole.at[me], keep_sems.at[slot])
        keep.start()
        spreads.append((exchange, keep, whole))

    for one in kept:
        one.wait()
    keep_do2.wait()
    give_do2.receive(lambda sender: do2h_ref.at[aligned(sender, TOK), :])

    def after_cross(step, rows):
        for half in range(2):
            send_part(give_e2, 0, 2 * step + half, e2_ref, 0)

    attend_back(
        cqh_ref[...], memh_ref[:, 0:PAIR], memh_ref[:, PAIR : 2 * PAIR], do2h_ref, mix2_ref,
        inv2_ref, False, after_cross,
    )
    keeps = [keep_part(0, e2_ref, 0, 2)]
    sums_ref[:, PAIR : 2 * PAIR] = dkt_ref[...].T.astype(LOW)
    sums_ref[:, 2 * PAIR : 3 * PAIR] = dvt_ref[...].T.astype(LOW)
    for there in range(SEQ):
        send_part(give_k2, 1, there, dkv_ref, 0)
        send_part(give_v2, 2, there, dkv_ref, WIDTH)
    keeps += [keep_part(1, dkv_ref, 0, 3), keep_part(2, dkv_ref, WIDTH, 4)]
    exp1_load = load(exp1_hbm, exp_ref, 21)

    keeps[0].wait()
    later[0].wait()
    unit2, inverse2 = norm_unit(x1_ref[...])
    give_e2.receive(from_peers(e2_ref, 0))
    dn2 = dot_nt(e2_ref[...], ring_r[1024:2048, :])
    dx1 = acc_ref[...] + norm_back(dn2, unit2, inverse2, gain_ref[1:2, :])
    acc_ref[...] = dx1
    da_ref[...] = dx1.astype(LOW)
    later[1].wait()
    keep_do1 = push_heads(
        give_do1, do1_ref, lambda rows: ring_r[rows, :], da_ref[...], do1h_ref, 5
    )
    gather.third()
    share(give_be2, e2_ref, b_e2, PAIR)
    share(give_da, da_ref, b_da, PAIR)
    col_n3.finish()
    both_cores(a_n3)
    for one in gathered:
        one.wait()
    both_cores(a_cot)
    both_cores(a_mem)
    for whole in (a_n2, a_o1):
        for step in (-1, 0, 1):
            block_to_core(whole, step)
    vec_ref[1:2, :] = column_sum(dn2 * unit2)
    vec_ref[4:5, :] = column_sum(dn2)
    vec_ref[8:9, :] = column_sum(da_ref[...].astype(F32))
    vec_ref[9:10, :] = column_sum(e2_ref[...].astype(F32))
    keeps[1].wait()
    keeps[2].wait()
    give_k2.receive(from_peers(dkv_ref, 0))
    give_v2.receive(from_peers(dkv_ref, WIDTH))
    share(give_kv, dkv_ref, b_kv, 256)
    later[2].wait()
    gmem_ref[...] = dot_nt(dkv_ref[...], ring_e[...])
    vec_ref[10:11, :] = column_sum(dkv_ref[:, WIDTH : 2 * WIDTH].astype(F32))
    last = [
        load(qkv_hbm.at[:, 0 : 2 * WIDTH], ring_e, 22),
        load(qkv_hbm.at[:, 2 * WIDTH : 3 * WIDTH], ring_r.at[0:1024, :], 23),
    ]

    for index in (0, 1):
        to_core[index][1].wait_recv()
    give_act.receive(lambda to: act_in.at[aligned(to, TOK), :])
    give_dfe.receive(lambda to: dfe_in.at[aligned(to, TOK), :])
    lax.fori_loop(0, 8, fill_f, 0)
    fill_reduce()
    next(run_f)
    col_o2.second()
    col_n2.forward()
    col_o1.forward()

    for exchange in (give_e2, give_k2, give_v2):
        exchange.drain()
    for one in kept1:
        one.wait()
    exp1_load.wait()
    keep_do1.wait()
    give_do1.receive(lambda sender: do1h_ref.at[aligned(sender, TOK), :])

    def after_self(step, rows):
        sums_ref[rows, PAIR : 2 * PAIR] = dkt_ref[:, rows].T.astype(LOW)
        sums_ref[rows, 2 * PAIR : 3 * PAIR] = dvt_ref[:, rows].T.astype(LOW)
        for half in range(2):
            for part, exchange in enumerate((give_q1, give_k1, give_v1)):
                send_part(exchange, part, 2 * step + half, e1_ref, part * WIDTH)

    attend_back(
        heads_ref[:, 0:PAIR], heads_ref[:, PAIR : 2 * PAIR], heads_ref[:, 2 * PAIR : 3 * PAIR],
        do1h_ref, mix1_ref, inv1_ref, True, after_self,
    )
    keeps = [keep_part(part, e1_ref, part * WIDTH, 6 + part) for part in range(3)]
    next(run_f)


    gather.finish()
    for part in range(3):
        value = sums_ref[:, part * PAIR : part * PAIR + PAIR].T
        weight_ref[:, :, :, part * PAIR : part * PAIR + PAIR] = (
            dot(value, n1_all[...]).T.astype(LOW).reshape(DP // 2, 2, ROW // DP, PAIR)
        )
    both_sums = pltpu.make_async_remote_copy(
        src_ref=weight_ref.at[:, 1 - core],
        dst_ref=weight_in.at[0],
        send_sem=pair_send.at[6],
        recv_sem=pair_recv.at[6],
        device_id=place.other,
        device_id_type=MESH,
    )
    both_sums.start()
    pair = dp // 2

    def pair_copy(source, target, distance):
        there = lax.rem(pair + distance + 8, 8)
        return pltpu.make_async_remote_copy(
            src_ref=source.at[there],
            dst_ref=target.at[1, pair],
            send_sem=dp_send.at[distance],
            recv_sem=dp_recv.at[distance],
            device_id=(there * 2 + core, me),
            device_id_type=MESH,
        )

    def pair_receive(target, distance):
        sender = lax.rem(pair - distance + 8, 8)
        return pltpu.make_async_remote_copy(
            src_ref=target.at[1, sender],
            dst_ref=target.at[1, sender],
            send_sem=dp_send.at[distance],
            recv_sem=dp_recv.at[distance],
            device_id=(sender * 2 + core, me),
            device_id_type=MESH,
        )

    def dp_copy(source, target, distance, base):
        there = lax.rem(dp + distance, DP)
        return pltpu.make_async_remote_copy(
            src_ref=source.at[there],
            dst_ref=target.at[dp],
            send_sem=dp_send.at[base + distance],
            recv_sem=dp_recv.at[base + distance],
            device_id=(there, me),
            device_id_type=MESH,
        )

    def dp_receive(target, distance, base):
        sender = lax.rem(dp - distance + DP, DP)
        return pltpu.make_async_remote_copy(
            src_ref=target.at[sender],
            dst_ref=target.at[sender],
            send_sem=dp_send.at[base + distance],
            recv_sem=dp_recv.at[base + distance],
            device_id=(sender, me),
            device_id_type=MESH,
        )

    both_sums.wait()
    weight_sum[...] = (
        weight_ref[:, core].astype(F32) + weight_in[0].astype(F32)
    ).astype(LOW)
    for one in keeps:
        one.wait()
    give_q1.receive(from_peers(e1_ref, 0))
    give_k1.receive(from_peers(e1_ref, WIDTH))
    next(run_f)
    for step in (-1, 0, 1):
        block_to_core(a_o2, step)
    for column, whole in ((col_o2, a_o2), (col_n2, a_n2), (col_o1, a_o1)):
        column.far()
        block_to_core(whole, 2)
    for distance in range(1, 8):
        pair_copy(weight_sum, weight_in, distance).start()

    for one in last:
        one.wait()
    unit1, inverse1 = norm_unit(tok_ref[...].astype(F32))
    dn1 = dot_nt(e1_ref[:, 0 : 2 * WIDTH], ring_e[...])
    give_v1.receive(from_peers(e1_ref, 2 * WIDTH))
    dn1 = dn1 + dot_nt(e1_ref[:, 2 * WIDTH : 3 * WIDTH], ring_r[0:1024, :])
    gtok_ref[...] = acc_ref[...] + norm_back(dn1, unit1, inverse1, gain_ref[0:1, :])
    vec_ref[0:1, :] = column_sum(dn1 * unit1)
    vec_ref[3:4, :] = column_sum(dn1)
    vec_ref[6:7, :] = column_sum(e1_ref[:, 0:WIDTH].astype(F32))
    vec_ref[7:8, :] = column_sum(e1_ref[:, 2 * WIDTH : 3 * WIDTH].astype(F32))

    to_core[2][1].wait_recv()
    for _, arrival in blocks_to_core:
        arrival.wait_recv()
    for exchange, target in ((give_dc, b_dc), (give_be2, b_e2), (give_kv, b_kv), (give_da, b_da)):
        exchange.receive(lambda to, target=target: target.at[aligned(to, TOK), :])
    fill_c()
    next(run_c)

    vec_out[...] = jnp.zeros_like(vec_out)
    for owner in range(DP):
        vec_out[owner, 0:13, 0:64] = vec_ref[0:13, owner * 64 : owner * 64 + 64]
        for half in range(2):
            at = (owner // 8) * 256 + half * PAIR
            vec_out[owner, 13 + half : 14 + half, :] = expand_sums[owner % 8, :, at : at + PAIR]
    for distance in range(1, DP):
        dp_copy(vec_out, vec_in, distance, DP).start()

    next(run_f)
    keeps_f = join(join_f, grads_f, piece_f, 9, True)
    joined(join_f, piece_f, keeps_f)
    gather_f.first()
    next(run_c)
    gather_f.second()
    for distance in range(1, 8):
        pair_receive(weight_in, distance).wait_recv()
    total = weight_sum[pair].astype(F32)
    for distance in range(1, 8):
        total = total + weight_in[1, lax.rem(pair + distance, 8)].astype(F32)
    piece_q[...] = total.astype(LOW)
    next(run_c)
    keeps_c = join(join_c, grads_c, piece_c, 11, False)
    spread(piece_q, all_q, 70, 12)
    gather_f.third()
    for distance in range(1, DP):
        dp_receive(vec_in, distance, DP).wait_recv()
    total = vec_out[dp]
    for distance in range(1, DP):
        total = total + vec_in[lax.rem(dp + distance, DP)]
    piece_v[...] = total
    spread(piece_v, all_v, 86, 14)
    joined(join_c, piece_c, keeps_c)
    spread(piece_c, all_c, 94, 15)
    gather_f.finish()

    for exchange, keep, whole in spreads:
        keep.wait()
        exchange.receive(lambda sender, whole=whole: whole.at[sender])
        exchange.drain()
    for exchange in (give_do2, give_do1, give_q1, give_k1, give_v1):
        exchange.drain()
    for copy, _ in to_core + blocks_to_core:
        copy.wait_send()
    col_o2.sent_near()
    for exchange in (give_act, give_dfe, give_dc, give_be2, give_kv, give_da, join_f, join_c):
        exchange.drain()
    for distance in range(1, DP):
        dp_copy(vec_out, vec_in, distance, DP).wait_send()
    for distance in range(1, 8):
        pair_copy(weight_sum, weight_in, distance).wait_send()
    sum_f.drain()
    sum_c.drain()


def back_call(operands):
    dma = pltpu.SemaphoreType.DMA
    vmem = pltpu.VMEM
    token = vmem((TOK, WIDTH), LOW)
    token_wide = vmem((TOK, WIDTH), F32)
    heads = vmem((ROW, PAIR), LOW)
    inverse = vmem((ROW, PAIR), F32)
    eight = vmem((4, 2, TOK, WIDTH), LOW)
    column = vmem((ROW, PAIR), LOW)
    chunk = vmem((ROW, FF_CHUNK), LOW)
    chunks = vmem((7, TOK, FF_CHUNK), LOW)

    def sums(rows, lanes):
        return [
            vmem((4, 4, rows, lanes), LOW), vmem((3, 4, rows, lanes), LOW),
            vmem((3, rows, lanes), LOW),
        ]

    return pl.pallas_call(
        back_kernel,
        out_shape=(
            shaped((TOK, WIDTH)), shaped((TOK, WIDTH), F32), shaped((TOK, WIDTH), F32),
            shaped((SEQ, 256, LANES)), shaped((SEQ, 128, 384)),
            shaped((SEQ, 64, 3 * PAIR)), shaped((SEQ, 16, PAIR), F32),
        ),
        in_specs=[spec_vmem()] * 3 + [spec_any()] * 25,
        out_specs=(spec_vmem(),) * 4 + (spec_any(),) * 3,
        scratch_shapes=[
            vmem((ROW, WIDTH), LOW),
            vmem((WIDTH, 2 * WIDTH), LOW), vmem((2 * WIDTH, WIDTH), LOW), vmem((WIDTH, WIDTH), LOW),
            vmem((2, ROW, ROW), LOW), token_wide, token, token,
            vmem((ROW, 3 * PAIR), LOW), vmem((ROW, 2 * PAIR), LOW), heads, heads, heads, inverse,
            inverse,
            eight, eight, eight, eight, eight, eight, chunk, chunk, chunks, chunks,
            column, column, column, vmem((ROW, 256), LOW),
            token, token, token_wide, token_wide,
            vmem((FF // FF_CHUNK, 1, FF_CHUNK), F32), vmem((16, WIDTH), F32),
            token, token, heads, heads, vmem((ROW, 3 * PAIR), LOW), token,
            vmem((TOK, 2 * WIDTH), LOW), vmem((TOK, 3 * WIDTH), LOW),
            vmem((PAIR, ROW), F32), vmem((PAIR, ROW), F32),
        ]
        + sums(256, LANES) + sums(128, 384)
        + [
            vmem((256, LANES), LOW), vmem((128, 384), LOW),
            vmem((8, 2, 64, 3 * PAIR), LOW), vmem((2, 8, 64, 3 * PAIR), LOW),
            vmem((8, 64, 3 * PAIR), LOW),
            vmem((64, 3 * PAIR), LOW), vmem((DP, 16, PAIR), F32), vmem((DP, 16, PAIR), F32),
            vmem((16, PAIR), F32),
            dma((38,)), dma((16,)), dma((16,)), dma((19,)), dma((19,)), dma((102,)), dma((102,)),
            dma((32,)), dma((32,)), dma((48,)), dma((48,)), dma((64,)), dma((64,)), dma((16,)),
            dma((16,)),
        ],
        compiler_params=pltpu.CompilerParams(
            collective_id=3, has_side_effects=True, vmem_limit_bytes=63 * MIB
        ),
        cost_estimate=pl.CostEstimate(
            flops=2 * TOK * WIDTH * 27 * WIDTH, bytes_accessed=100 * MIB, transcendentals=0
        ),
        name="back",
    )(*operands)


def finish_kernel(
    f_hbm, c_hbm, q_hbm, vec_hbm, output_hbm, gtok_hbm, gmem_hbm,
    gqkv_ref, gout_ref, gque_ref, gckv_ref, gcro_ref, gexp_ref, gred_ref, ggain_ref, gbias_ref,
    gebias_ref, to_output, to_gtok, to_gmem,
    f_ref, c_ref, q_ref, vec_ref, sems,
):
    copies = [
        pltpu.make_async_copy(source, target, sems.at[index])
        for index, (source, target) in enumerate(
            (
                (f_hbm, f_ref), (c_hbm, c_ref), (q_hbm, q_ref), (vec_hbm, vec_ref),
                (output_hbm, to_output), (gtok_hbm, to_gtok), (gmem_hbm, to_gmem),
            )
        )
    ]
    for one in copies:
        one.start()
    for one in copies[:4]:
        one.wait()
    for seq in range(SEQ):
        y, xl = seq // 2, seq % 2
        rows = slice(16 * y, 16 * y + 16)
        for owner in range(8):
            own = slice(owner * 16, owner * 16 + 16)
            at = (owner + 8 * xl) * 256
            gexp_ref[rows, at : at + 256] = f_ref[seq, own, :].astype(F32)
            if xl == 0:
                for index, target in enumerate((gque_ref, gout_ref, gcro_ref)):
                    target[rows, owner * PAIR : owner * PAIR + PAIR] = c_ref[
                        seq, own, index * PAIR : index * PAIR + PAIR
                    ].astype(F32)
            else:
                gckv_ref[rows, owner * 256 : owner * 256 + 256] = c_ref[seq, own, 0:256].astype(F32)
        for sub in range(2):
            at = xl * 512 + sub * LANES
            gred_ref[64 * y : 64 * y + 64, at : at + LANES] = f_ref[
                seq, 128 + sub * 64 : 192 + sub * 64, :
            ].astype(F32)
        for part in range(3):
            at = part * WIDTH + seq * PAIR
            gqkv_ref[:, at : at + PAIR] = q_ref[seq, :, part * PAIR : (part + 1) * PAIR].astype(F32)
    total = vec_ref[0]
    for seq in range(1, SEQ):
        total = total + vec_ref[seq]
    ggain_ref[...] = total[0:3, 0:64]
    gbias_ref[...] = total[3:13, 0:64]
    gebias_ref[:, 0:PAIR] = total[13:14, :]
    gebias_ref[:, PAIR : 2 * PAIR] = total[14:15, :]
    for one in copies[4:]:
        one.wait()


def finish_call(operands):
    vmem = pltpu.VMEM
    return pl.pallas_call(
        finish_kernel,
        out_shape=(
            shaped((64, 3 * WIDTH), F32), shaped((64, WIDTH), F32), shaped((64, WIDTH), F32),
            shaped((64, 2 * WIDTH), F32), shaped((64, WIDTH), F32), shaped((64, FF), F32),
            shaped((256, WIDTH), F32), shaped((3, 64), F32), shaped((10, 64), F32),
            shaped((1, 256), F32), shaped((TOK, WIDTH)), shaped((TOK, WIDTH), F32),
            shaped((TOK, WIDTH), F32),
        ),
        in_specs=[spec_any()] * 7,
        out_specs=(spec_vmem(),) * 13,
        scratch_shapes=[
            vmem((SEQ, 256, LANES), LOW), vmem((SEQ, 128, 384), LOW), vmem((SEQ, 64, 3 * PAIR), LOW),
            vmem((SEQ, 16, PAIR), F32), pltpu.SemaphoreType.DMA((8,)),
        ],
        compiler_params=pltpu.CompilerParams(vmem_limit_bytes=63 * MIB),
        cost_estimate=pl.CostEstimate(flops=0, bytes_accessed=10 * MIB, transcendentals=0),
        name="finish",
    )(*operands)


def on_device(
    tokens, memory, cotangent, offsets, memory_ids, pair_map, self_qkv, self_out, cross_query,
    cross_kv, cross_out, expand_weight, expand_bias, reduce_weight, norm_gains, bias_rows,
):
    tok = tokens.reshape(TOK, WIDTH)
    mem = memory.reshape(TOK, WIDTH)
    cot = cotangent.reshape(TOK, WIDTH)
    (
        x1, _, _, o2, heads, mem_heads, cq, mix1, mix2, inv1, inv2, n1, exp1, exp2, cot4, mem4, n24, o14,
    ) = front_call(
        (tok, mem, cot, norm_gains, bias_rows, memory_ids, offsets, pair_map, self_qkv, cross_kv,
         self_out, cross_query)
    )
    output, gtok, gmem, all_f, all_c, all_q, all_v = back_call(
        (norm_gains, bias_rows, expand_bias.reshape(1, FF),
         o2, x1, cot, tok, n1, cot4, mem4, n24, o14, heads, mem_heads, cq, mix1, mix2, inv1, inv2,
         exp1, exp2, self_qkv, cross_kv, self_out, cross_query, cross_out, expand_weight,
         reduce_weight)
    )
    (
        gqkv, gout, gque, gckv, gcro, gexp, gred, ggain, gbias, gebias, output, gtok, gmem,
    ) = finish_call((all_f, all_c, all_q, all_v, output, gtok, gmem))
    return (
        output.reshape(1, TOK, WIDTH), gtok.reshape(1, TOK, WIDTH), gmem.reshape(1, TOK, WIDTH),
        gqkv, gout, gque, gckv, gcro, gexp, gebias.reshape(256), gred, ggain, gbias,
    )


def solution(mesh):
    row = P("dp", "seq", None)
    split = P("dp", None)
    in_specs = (row,) * 3 + (split,) * 3 + (P(),) * 10
    out_specs = (row,) * 3 + (split,) * 6 + (P("dp"), split, P(None, "dp"), P(None, "dp"))
    return jax.shard_map(
        on_device, mesh=mesh, in_specs=in_specs, out_specs=out_specs, check_vma=False
    )
```

```python
import functools
import math

import jax
import jax.numpy as jnp
from jax import lax
from jax.experimental import pallas as pl
from jax.experimental.pallas import tpu as pltpu
from jax.sharding import PartitionSpec as P

HEADS = 16
HEAD_DIM = 64
WIDTH = 1024
TOK = 128
ROW = 1024
FF = 4096
SEQ = 8
DP = 16
PAIR = 128
NEG_FILL = -1e30
EPS = 1e-05
SCALE = HEAD_DIM ** (-0.5)
LOW = jnp.bfloat16
F32 = jnp.float32
MESH = pl.DeviceIdType.MESH
MIB = 2**20


def dot(left, right):
    return lax.dot_general(left, right, (((1,), (0,)), ((), ())), preferred_element_type=F32)


def dot_nt(left, right):
    return lax.dot_general(left, right, (((1,), (1,)), ((), ())), preferred_element_type=F32)


def dot_tn(left, right):
    return lax.dot_general(left, right, (((0,), (0,)), ((), ())), preferred_element_type=F32)


def norm_unit(values):
    average = jnp.mean(values, -1, keepdims=True)
    centered = values - average
    inverse = lax.rsqrt(jnp.mean(centered * centered, -1, keepdims=True) + EPS)
    return centered * inverse, inverse


def norm_back(incoming, unit, inverse, gain_row):
    scaled = incoming * gain_row
    return inverse * (
        scaled
        - jnp.mean(scaled, -1, keepdims=True)
        - unit * jnp.mean(scaled * unit, -1, keepdims=True)
    )


def column_sum(values):
    return jnp.sum(values, 0, keepdims=True)


def spec_any():
    return pl.BlockSpec(memory_space=pl.ANY)


def spec_vmem():
    return pl.BlockSpec(memory_space=pltpu.VMEM)


def spec_smem():
    return pl.BlockSpec(memory_space=pltpu.SMEM)


def shaped(shape, kind=LOW):
    return jax.ShapeDtypeStruct(shape, kind)


def head_lanes(rows):
    return lax.broadcasted_iota(jnp.int32, (rows, PAIR), 1) < HEAD_DIM


def pick_head(values, lanes, head):
    zero = jnp.zeros_like(values)
    return jnp.where(lanes, values, zero) if head == 0 else jnp.where(lanes, zero, values)


def attend_tile(query, key_t, value, allowed, exp_ref, rows, width):
    lanes = head_lanes(query.shape[0])
    mixed, inverses = [], []
    for head in range(2):
        scores = dot(pick_head(query, lanes, head), key_t)
        scores = jnp.where(allowed, scores, NEG_FILL)
        top = jnp.max(scores, -1, keepdims=True)
        exponent = jnp.exp(scores - top)
        inverse = 1.0 / jnp.sum(exponent, -1, keepdims=True)
        low = exponent.astype(LOW)
        exp_ref[head, rows, 0:width] = low
        mixed.append(dot(low, value))
        inverses.append(inverse)
    inverse = jnp.where(lanes, inverses[0], inverses[1])
    return jnp.where(lanes, mixed[0], mixed[1]) * inverse, inverse


def self_allowed(offsets_ref, step, tile, width):
    places = lax.broadcasted_iota(jnp.int32, (tile, 1), 0) + step * tile
    begin = jnp.zeros((tile, 1), jnp.int32)
    for seg in range(1, 16):
        offset = offsets_ref[0, seg]
        begin = jnp.where(places >= offset, offset, begin)
    keys = lax.broadcasted_iota(jnp.int32, (tile, width), 1)
    return (keys <= places) & (keys >= begin)


def cross_allowed(ids, offsets_ref, pair_ref, step, tile):
    places = lax.broadcasted_iota(jnp.int32, (tile, 1), 0) + step * tile
    reads = jnp.zeros((tile, 1), jnp.int32) + pair_ref[0, 0]
    for seg in range(1, 16):
        reads = jnp.where(places >= offsets_ref[0, seg], pair_ref[0, seg], reads)
    return ids == reads


def aligned(index, unit):
    return pl.ds(pl.multiple_of(index * unit, unit), unit)


class Exchange:
    def __init__(self, send_sems, recv_sems, base):
        self.dp = lax.axis_index("dp")
        self.me = lax.axis_index("seq")
        self.send_sems, self.recv_sems, self.base = send_sems, recv_sems, base
        self.sent = []

    def copy(self, source, target, there, distance):
        return pltpu.make_async_remote_copy(
            src_ref=source,
            dst_ref=target,
            send_sem=self.send_sems.at[self.base + distance],
            recv_sem=self.recv_sems.at[self.base + distance],
            device_id=(self.dp, there),
            device_id_type=MESH,
        )

    def push(self, source, target, there, may_be_own):
        distance = lax.rem(there - self.me + SEQ, SEQ)
        if may_be_own:
            remote = there != self.me

            @pl.when(remote)
            def _():
                self.copy(source, target, there, distance).start()

        else:
            self.copy(source, target, there, distance).start()
        self.sent.append((source, target))

    def receive(self, place):
        for distance in range(1, SEQ):
            sender = lax.rem(self.me - distance + SEQ, SEQ)
            spot = place(sender)
            self.copy(spot, spot, sender, distance).wait_recv()

    def drain(self):
        source, target = self.sent[0]
        for distance in range(1, SEQ):
            there = lax.rem(self.me + distance, SEQ)
            self.copy(source, target, there, distance).wait_send()


def greet_row():
    dp = lax.axis_index("dp")
    me = lax.axis_index("seq")
    barrier = pltpu.get_barrier_semaphore()
    for distance in range(1, SEQ):
        pl.semaphore_signal(
            barrier, inc=1, device_id=(dp, lax.rem(me + distance, SEQ)), device_id_type=MESH
        )
    return barrier


class Gather:
    def __init__(self, block, spot, local_sem, send_sems, recv_sems, base):
        self.dp = lax.axis_index("dp")
        self.me = lax.axis_index("seq")
        self.y, self.xl = self.me // 2, lax.rem(self.me, 2)
        self.spot, self.send_sems, self.recv_sems, self.base = spot, send_sems, recv_sems, base
        self.own = pltpu.make_async_copy(block, spot(self.me), local_sem)
        self.block = block

    def part(self, y, xl):
        return self.spot(lax.rem(y + 8, 4) * 2 + xl)

    def copy(self, source, target, there, slot):
        return pltpu.make_async_remote_copy(
            src_ref=source,
            dst_ref=target,
            send_sem=self.send_sems.at[self.base + slot],
            recv_sem=self.recv_sems.at[self.base + slot],
            device_id=(self.dp, there),
            device_id_type=MESH,
        )

    def beside(self, step):
        return lax.rem(self.y + step + 4, 4) * 2 + self.xl

    def send(self, slot):
        y, xl = self.y, self.xl
        if slot == 0:
            return self.copy(self.block, self.part(y, xl), y * 2 + 1 - xl, 0)
        step = 1 if slot % 2 else -1
        if slot < 3:
            return self.copy(self.block, self.part(y, xl), self.beside(step), slot)
        spot = self.part(y, 1 - xl) if slot < 5 else self.part(y - step, xl if step == 1 else 1 - xl)
        return self.copy(spot, spot, self.beside(step), slot)

    def arrive(self, slot):
        y, xl = self.y, self.xl
        if slot == 0:
            spot = self.part(y, 1 - xl)
        else:
            step = 1 if slot % 2 else -1
            if slot < 5:
                spot = self.part(y - step, xl if slot < 3 else 1 - xl)
            else:
                spot = self.part(y + 2, xl if step == 1 else 1 - xl)
        self.copy(spot, spot, self.beside(1), slot).wait_recv()

    def first(self):
        self.own.start()
        for slot in range(3):
            self.send(slot).start()

    def second(self):
        self.arrive(0)
        for slot in (3, 4):
            self.send(slot).start()

    def third(self):
        self.arrive(1)
        self.send(5).start()
        self.arrive(4)
        self.send(6).start()

    def finish(self):
        for slot in (2, 3, 5, 6):
            self.arrive(slot)
        self.own.wait()
        for slot in range(7):
            self.send(slot).wait_send()


class Column:
    def __init__(self, block, spot, local_sem, send_sems, recv_sems, base):
        self.dp, self.me = lax.axis_index("dp"), lax.axis_index("seq")
        self.z = lax.rem(self.dp // 2, 4)
        self.block, self.spot, self.local_sem = block, spot, local_sem
        self.send_sems, self.recv_sems, self.base = send_sems, recv_sems, base

    def at(self, step):
        return self.spot(lax.rem(self.z + step + 4, 4))

    def copy(self, source, target, step, slot):
        there = self.dp + 2 * (lax.rem(self.z + step + 4, 4) - self.z)
        return pltpu.make_async_remote_copy(
            src_ref=source,
            dst_ref=target,
            send_sem=self.send_sems.at[self.base + slot],
            recv_sem=self.recv_sems.at[self.base + slot],
            device_id=(there, self.me),
            device_id_type=MESH,
        )

    def own(self):
        return pltpu.make_async_copy(self.block, self.at(0), self.local_sem)

    def half(self, step, slot):
        return self.at(step).at[pl.ds(0 if slot == 2 else TOK // 2, TOK // 2), :]

    def first(self):
        if self.local_sem is not None:
            self.own().start()
        self.copy(self.block, self.at(0), 1, 0).start()
        self.copy(self.block, self.at(0), -1, 1).start()

    def second(self):
        for slot, step in ((0, 1), (1, -1)):
            self.copy(self.block, self.at(-step), step, slot).wait_recv()
            piece = self.half(-step, slot + 2)
            self.copy(piece, piece, step, slot + 2).start()

    def near(self):
        for slot, step in ((0, 1), (1, -1)):
            self.copy(self.block, self.at(-step), step, slot).wait_recv()
            self.copy(self.block, self.at(0), step, slot).wait_send()
        self.own().wait()

    def sent_near(self):
        for slot, step in ((0, 1), (1, -1)):
            self.copy(self.block, self.at(0), step, slot).wait_send()

    def forward(self):
        for slot, step in ((0, 1), (1, -1)):
            piece = self.half(-step, slot + 2)
            self.copy(piece, piece, step, slot + 2).start()

    def far(self):
        for slot, step in ((0, 1), (1, -1)):
            piece = self.half(2, slot + 2)
            self.copy(piece, piece, step, slot + 2).wait_recv()
            piece = self.half(-step, slot + 2)
            self.copy(piece, piece, step, slot + 2).wait_send()

    def finish(self):
        self.far()
        for slot, step in ((0, 1), (1, -1)):
            self.copy(self.block, self.at(0), step, slot).wait_send()
        if self.local_sem is not None:
            self.own().wait()


def front_kernel(
    tok_ref, mem_ref, cot_ref, gain_ref, bias_ref, ids_ref, offsets_ref, pair_ref,
    qkv_hbm, ckv_hbm, out_hbm, query_hbm,
    o2_ref, mix2_ref, inv2_ref, x1_hbm, heads_hbm, memh_hbm, cqh_hbm, mix1_hbm, inv1_hbm, n1_hbm,
    exp1_hbm, exp2_hbm, cot_all, mem_all, n2_all, o1_all,
    x1_ref, n2_ref, o1_ref, heads_ref, memh_ref, cqh_ref, mix1_ref, inv1_ref, n1_ref,
    qkv_w, ckv_w, out_w, query_w, give_heads, give_mem, cq_ref, exp1_ref, exp2_ref,
    load_sems, keep_sems, exp_sems, send_sems, recv_sems,
):
    me = lax.axis_index("seq")
    y, xl = me // 2, lax.rem(me, 2)
    dp = lax.axis_index("dp")
    barrier = greet_row()
    for step in (1, 2, 3):
        z = lax.rem(dp // 2, 4)
        there = dp + 2 * (lax.rem(z + step, 4) - z)
        pl.semaphore_signal(barrier, inc=1, device_id=(there, me), device_id_type=MESH)
    order = [lax.rem(y + step, 4) for step in (1, 2, 3, 0)]
    loads = {}
    for step in range(4):
        for part in range(3):
            cols = pl.ds(pl.multiple_of(part * WIDTH + order[step] * 256, 256), 256)
            loads["qkv", step, part] = pltpu.make_async_copy(
                qkv_hbm.at[:, cols], qkv_w.at[:, cols], load_sems.at[step * 3 + part]
            )
    for step in range(4):
        for part in range(2):
            cols = pl.ds(pl.multiple_of(part * WIDTH + order[step] * 256, 256), 256)
            loads["ckv", step, part] = pltpu.make_async_copy(
                ckv_hbm.at[:, cols], ckv_w.at[:, cols], load_sems.at[12 + step * 2 + part]
            )
    loads["out"] = pltpu.make_async_copy(out_hbm, out_w, load_sems.at[20])
    loads["query"] = pltpu.make_async_copy(query_hbm, query_w, load_sems.at[21])
    for name, one in loads.items():
        if name[0] == "qkv":
            one.start()

    give_qkv, give_kv, back1, give_q, back2 = (
        Exchange(send_sems, recv_sems, 8 * index) for index in range(5)
    )
    own_rows = aligned(me, TOK)
    columns = [
        Column(
            block, lambda at, whole=whole: whole.at[at], keep_sems.at[7 + index],
            send_sems, recv_sems, 40 + 4 * index,
        )
        for index, (block, whole) in enumerate(
            ((cot_ref, cot_all), (mem_ref, mem_all), (o1_ref, o1_all), (n2_ref, n2_all))
        )
    ]

    unit, _ = norm_unit(tok_ref[...].astype(F32))
    n1 = (unit * gain_ref[0:1, :] + bias_ref[0:1, :]).astype(LOW)
    n1_ref[...] = n1
    stored = []

    def store(source, target):
        copy = pltpu.make_async_copy(source, target, keep_sems.at[11 + len(stored)])
        copy.start()
        stored.append(copy)

    store(n1_ref, n1_hbm)
    mem = mem_ref[...]
    for kind, count, source, give, heads, exchange in (
        ("qkv", 3, n1, give_heads, heads_ref, give_qkv),
        ("ckv", 2, mem, give_mem, memh_ref, give_kv),
    ):
        for step in range(4):
            at = order[step]
            own = aligned(at, 256)
            for part in range(count):
                loads[kind, step, part].wait()
                cols = pl.ds(pl.multiple_of(part * WIDTH + at * 256, 256), 256)
                if kind == "qkv":
                    value = dot(source, qkv_w[:, cols])
                    if part == 0:
                        value = (value + bias_ref[3:4, own]) * SCALE
                    elif part == 2:
                        value = value + bias_ref[4:5, own]
                else:
                    value = dot(source, ckv_w[:, cols])
                    if part == 1:
                        value = value + bias_ref[7:8, own]
                low = value.astype(LOW)
                give[2 * at, :, part * PAIR : part * PAIR + PAIR] = low[:, :PAIR]
                give[2 * at + 1, :, part * PAIR : part * PAIR + PAIR] = low[:, PAIR:]
            if kind == "qkv" and step == 0:
                for name, one in loads.items():
                    if name[0] != "qkv":
                        one.start()
                pl.semaphore_wait(barrier, SEQ - 1 + 3)
                columns[0].first()
                columns[1].first()
            there = heads.at[own_rows, :]
            if step < 3:
                exchange.push(give.at[2 * at], there, 2 * at, False)
                exchange.push(give.at[2 * at + 1], there, 2 * at + 1, False)
            else:
                partner = 2 * y + 1 - xl
                exchange.push(give.at[partner], there, partner, False)
                keep = pltpu.make_async_copy(
                    give.at[me], there, keep_sems.at[2 if kind == "qkv" else 3]
                )
                keep.start()
                loads[kind] = keep

    def attended(allowed_of, query_of, key_t, value_ref, value_at, mix_ref, inv_ref, exp_ref,
                 exp_hbm, exp_base, causal, back, target_ref, keep_sem):
        tile = 256
        for step in range(ROW // tile):
            rows = slice(step * tile, step * tile + tile)
            width = (step + 1) * tile if causal else ROW
            mixture, inverse = attend_tile(
                query_of(rows), key_t[:, 0:width], value_ref[0:width, value_at], allowed_of(step, width),
                exp_ref, rows, width,
            )
            mix_ref[rows, :] = mixture.astype(LOW)
            inv_ref[rows, :] = inverse
            for half in range(2):
                there = 2 * step + half
                back.push(
                    mix_ref.at[there * TOK : there * TOK + TOK, :],
                    target_ref.at[:, aligned(me, PAIR)], there, True,
                )
            for head in range(2):
                spot = (head, rows, slice(0, width))
                pltpu.make_async_copy(
                    exp_ref.at[spot], exp_hbm.at[spot], exp_sems.at[exp_base + step * 2 + head]
                ).start()
        keep = pltpu.make_async_copy(
            mix_ref.at[own_rows, :], target_ref.at[:, aligned(me, PAIR)], keep_sem
        )
        keep.start()
        return keep

    loads["qkv"].wait()
    give_qkv.receive(lambda sender: heads_ref.at[aligned(sender, TOK), :])
    store(heads_ref, heads_hbm)
    key_t = heads_ref[:, PAIR : 2 * PAIR].T
    keep1 = attended(
        lambda step, width: self_allowed(offsets_ref, step, 256, width),
        lambda rows: heads_ref[rows, 0:PAIR], key_t, heads_ref, slice(2 * PAIR, 3 * PAIR),
        mix1_ref, inv1_ref, exp1_ref, exp1_hbm, 0, True, back1, o1_ref, keep_sems.at[4],
    )
    columns[0].second()
    columns[1].second()
    store(mix1_ref, mix1_hbm)
    store(inv1_ref, inv1_hbm)
    keep1.wait()
    loads["out"].wait()
    back1.receive(lambda sender: o1_ref.at[:, aligned(sender, PAIR)])
    columns[2].first()
    x1 = tok_ref[...].astype(F32) + dot(o1_ref[...], out_w[...]) + bias_ref[5:6, :]
    x1_ref[...] = x1
    store(x1_ref, x1_hbm)
    unit, _ = norm_unit(x1)
    n2 = (unit * gain_ref[1:2, :] + bias_ref[1:2, :]).astype(LOW)
    n2_ref[...] = n2
    columns[3].first()
    loads["query"].wait()
    for step in range(4):
        at = order[step]
        own = aligned(at, 256)
        cq_ref[:, own] = ((dot(n2, query_w[:, own]) + bias_ref[6:7, own]) * SCALE).astype(LOW)
        for half in range(2):
            there = 2 * at + half if step < 3 else 2 * y + 1 - xl
            if step == 3 and half == 1:
                continue
            give_q.push(cq_ref.at[:, aligned(there, PAIR)], cqh_ref.at[own_rows, :], there, False)
    keep = pltpu.make_async_copy(cq_ref.at[:, aligned(me, PAIR)], cqh_ref.at[own_rows, :], keep_sems.at[5])
    keep.start()
    loads["ckv"].wait()
    give_kv.receive(lambda sender: memh_ref.at[aligned(sender, TOK), :])
    store(memh_ref, memh_hbm)
    key_t = memh_ref[:, 0:PAIR].T
    keep.wait()
    give_q.receive(lambda sender: cqh_ref.at[aligned(sender, TOK), :])
    store(cqh_ref, cqh_hbm)
    ids = ids_ref[...]
    keep2 = attended(
        lambda step, width: cross_allowed(ids, offsets_ref, pair_ref, step, 256),
        lambda rows: cqh_ref[rows, :], key_t, memh_ref, slice(PAIR, 2 * PAIR),
        mix2_ref, inv2_ref, exp2_ref, exp2_hbm, 8, False, back2, o2_ref, keep_sems.at[6],
    )
    keep2.wait()
    back2.receive(lambda sender: o2_ref.at[:, aligned(sender, PAIR)])
    for step in range(4):
        rows = slice(step * 256, step * 256 + 256)
        for head in range(2):
            spot = (head, rows, slice(0, step * 256 + 256))
            pltpu.make_async_copy(
                exp1_ref.at[spot], exp1_hbm.at[spot], exp_sems.at[step * 2 + head]
            ).wait()
            spot = (head, rows, slice(0, ROW))
            pltpu.make_async_copy(
                exp2_ref.at[spot], exp2_hbm.at[spot], exp_sems.at[8 + step * 2 + head]
            ).wait()
    for one in stored:
        one.wait()
    for exchange in (give_qkv, give_kv, back1, give_q, back2):
        exchange.drain()
    for column in columns[:2]:
        column.finish()
    for column in columns[2:]:
        column.near()


def front_call(operands):
    dma = pltpu.SemaphoreType.DMA
    vmem = pltpu.VMEM
    heads = shaped((ROW, PAIR))
    token = shaped((TOK, WIDTH))
    inverse = shaped((ROW, PAIR), F32)
    exps = shaped((2, ROW, ROW))
    four = shaped((4, TOK, WIDTH))
    return pl.pallas_call(
        front_kernel,
        out_shape=(
            token, heads, inverse, shaped((TOK, WIDTH), F32), shaped((ROW, 3 * PAIR)),
            shaped((ROW, 2 * PAIR)), heads, heads, inverse, token, exps, exps, four, four, four, four,
        ),
        in_specs=[spec_vmem()] * 6 + [spec_smem()] * 2 + [spec_any()] * 4,
        out_specs=(spec_vmem(),) * 3 + (spec_any(),) * 13,
        scratch_shapes=[
            vmem((TOK, WIDTH), F32), vmem((TOK, WIDTH), LOW), vmem((TOK, WIDTH), LOW),
            vmem((ROW, 3 * PAIR), LOW), vmem((ROW, 2 * PAIR), LOW), vmem((ROW, PAIR), LOW),
            vmem((ROW, PAIR), LOW), vmem((ROW, PAIR), F32), vmem((TOK, WIDTH), LOW),
            vmem((WIDTH, 3 * WIDTH), LOW), vmem((WIDTH, 2 * WIDTH), LOW), vmem((WIDTH, WIDTH), LOW),
            vmem((WIDTH, WIDTH), LOW), vmem((SEQ, TOK, 3 * PAIR), LOW), vmem((SEQ, TOK, 2 * PAIR), LOW),
            vmem((TOK, WIDTH), LOW), vmem((2, ROW, ROW), LOW), vmem((2, ROW, ROW), LOW),
            dma((22,)), dma((18,)), dma((16,)), dma((56,)), dma((56,)),
        ],
        compiler_params=pltpu.CompilerParams(
            collective_id=2, has_side_effects=True, vmem_limit_bytes=56 * MIB
        ),
        cost_estimate=pl.CostEstimate(
            flops=2 * TOK * WIDTH * 7 * WIDTH, bytes_accessed=60 * MIB, transcendentals=0
        ),
        name="front",
    )(*operands)


LANES = 256


def wrap(index):
    return lax.rem(index + 8, 4)


def device_of(core, x, y, z):
    return ((x // 2) * 8 + z * 2 + core, y * 2 + lax.rem(x, 2))


class Place:
    def __init__(self):
        self.dp = lax.axis_index("dp")
        self.seq = lax.axis_index("seq")
        self.core = lax.rem(self.dp, 2)
        self.y, self.xl = self.seq // 2, lax.rem(self.seq, 2)
        self.at = {
            "x": (self.dp // 8) * 2 + self.xl,
            "y": self.y,
            "z": lax.rem(self.dp // 2, 4),
        }
        self.z = self.at["z"]
        self.other = (self.dp + 1 - 2 * self.core, self.seq)
        self.rank = lax.rem(self.dp, 8)

    def member(self, distance):
        rank = lax.rem(self.rank + distance + 8, 8)
        return (self.dp - self.rank + rank, self.seq), rank

    def neighbour(self, axis, step):
        at = dict(self.at)
        at[axis] = wrap(at[axis] + step)
        return device_of(self.core, **at)


class Sum:
    def __init__(self, place, grads, lands, flows, send_sems, recv_sems, base):
        self.place, self.grads, self.lands, self.flows = place, grads, lands, flows
        self.send_sems, self.recv_sems, self.base = send_sems, recv_sems, base
        self.open_sends = []

    def view(self, order, stage, block, first, rows):
        index = {"x": slice(None), "y": slice(None)}
        for done in range(stage):
            index[order[done]] = self.place.at[order[done]]
        index[order[stage]] = block
        return (index["x"], index["y"], slice(first, first + rows), slice(None))

    def land(self, stage, slot, first, rows):
        return (slot,) + (slice(None),) * (1 - stage) + (slice(first, first + rows), slice(None))

    def spans(self, flow):
        order, first, low, high = self.flows[flow]
        return order, (first, low), (first + low, high)

    def copy(self, stage, flow, kind):
        order, low, high = self.spans(flow)
        axis = order[stage]
        step = (2, 2, 1, -1, 1, -1)[kind]
        way = (1, -1, 1, -1, 1, -1)[kind]
        first, rows = (low, high, high, low, low, high)[kind]
        slot = (0, 0, 1, 1, 2, 2)[kind]
        at = self.base + (stage * len(self.flows) + flow) * 6 + kind
        return pltpu.make_async_remote_copy(
            src_ref=self.grads.at[
                self.view(order, stage, wrap(self.place.at[axis] + step), first, rows)
            ],
            dst_ref=self.lands[stage].at[self.land(stage, slot, first, rows)],
            send_sem=self.send_sems.at[at],
            recv_sem=self.recv_sems.at[at],
            device_id=self.place.neighbour(axis, way),
            device_id_type=MESH,
        )

    def straight(self, stage, flow, distance):
        order, (first, low), (_, high) = self.spans(flow)
        axis, rows = order[stage], low + high
        at = self.base + (stage * len(self.flows) + flow) * 6 + distance
        return pltpu.make_async_remote_copy(
            src_ref=self.grads.at[
                self.view(order, stage, wrap(self.place.at[axis] + distance), first, rows)
            ],
            dst_ref=self.lands[stage].at[self.land(stage, distance - 1, first, rows)],
            send_sem=self.send_sems.at[at],
            recv_sem=self.recv_sems.at[at],
            device_id=self.place.neighbour(axis, distance),
            device_id_type=MESH,
        )

    def add(self, stage, flow, step, span, slots):
        order, _, _ = self.spans(flow)
        at = self.view(order, stage, wrap(self.place.at[order[stage]] + step), *span)
        total = self.grads[at].astype(F32)
        for slot in slots:
            total = total + self.lands[stage][self.land(stage, slot, *span)].astype(F32)
        self.grads[at] = total.astype(LOW)

    def start(self, copy):
        copy.start()
        self.open_sends.append(copy)

    def run(self):
        flows = range(len(self.flows))
        for kind in range(4):
            for flow in flows:
                self.start(self.copy(0, flow, kind))
        yield
        for flow in flows:
            _, low, high = self.spans(flow)
            self.copy(0, flow, 0).wait_recv()
            self.add(0, flow, 1, low, (0,))
            self.start(self.copy(0, flow, 4))
            self.copy(0, flow, 1).wait_recv()
            self.add(0, flow, -1, high, (0,))
            self.start(self.copy(0, flow, 5))
        yield
        for flow in flows:
            _, low, high = self.spans(flow)
            for kind in (2, 3, 4, 5):
                self.copy(0, flow, kind).wait_recv()
            self.add(0, flow, 0, low, (1, 2))
            self.add(0, flow, 0, high, (1, 2))
            for distance in (1, 2, 3):
                self.start(self.straight(1, flow, distance))
        yield
        for flow in flows:
            _, low, high = self.spans(flow)
            for distance in (1, 2, 3):
                self.straight(1, flow, distance).wait_recv()
            self.add(1, flow, 0, (low[0], low[1] + high[1]), (0, 1, 2))
        yield

    def run_straight(self):
        flows = range(len(self.flows))
        for stage in range(2):
            for flow in flows:
                for distance in (1, 2, 3):
                    self.start(self.straight(stage, flow, distance))
            yield
            for flow in flows:
                _, low, high = self.spans(flow)
                for distance in (1, 2, 3):
                    self.straight(stage, flow, distance).wait_recv()
                self.add(stage, flow, 0, (low[0], low[1] + high[1]), (0, 1, 2))
        yield

    def drain(self):
        for copy in self.open_sends:
            copy.wait_send()
        self.open_sends = []


FF_CHUNK = 512
HALF_CHUNKS = FF // FF_CHUNK // 2
FLOWS_F = (("xy", 0, 64, 64), ("yx", 128, 64, 64))
FLOWS_C = (("xy", 0, 32, 32), ("yx", 64, 32, 32))


class Eight:
    def __init__(self, place, send_sems, recv_sems, base):
        self.place, self.send_sems, self.recv_sems = place, send_sems, recv_sems
        self.base, self.last = base, None

    def copy(self, source, target, distance):
        device, _ = self.place.member(distance)
        return pltpu.make_async_remote_copy(
            src_ref=source,
            dst_ref=target,
            send_sem=self.send_sems.at[self.base + distance],
            recv_sem=self.recv_sems.at[self.base + distance],
            device_id=device,
            device_id_type=MESH,
        )

    def push(self, source_of, target):
        for distance in range(1, 8):
            _, rank = self.place.member(distance)
            self.last = (source_of(rank), target)
            self.copy(source_of(rank), target, distance).start()

    def receive(self, place_of):
        for distance in range(1, 8):
            _, rank = self.place.member(-distance)
            spot = place_of(rank)
            self.copy(spot, spot, distance).wait_recv()

    def drain(self):
        for distance in range(1, 8):
            self.copy(*self.last, distance).wait_send()


def back_kernel(
    gain_ref, bias_ref, ebias_ref,
    o2_hbm, x1_hbm, cot_hbm, tok_hbm, n1_hbm, cot4_hbm, mem4_hbm, n24_hbm, o14_hbm,
    heads_hbm, memh_hbm, cqh_hbm, mix1_hbm, mix2_hbm, inv1_hbm, inv2_hbm, exp1_hbm, exp2_hbm,
    qkv_hbm, ckv_hbm, out_hbm, query_hbm, cross_hbm, expand_hbm, reduce_hbm,
    output_ref, gtok_ref, gmem_ref, all_f, all_c, all_q, all_v,
    n1_all, ring_e, ring_r, cross_w, exp_ref, x1_ref, cot_ref, tok_ref,
    heads_ref, memh_ref, cqh_ref, mix1_ref, mix2_ref, inv1_ref, inv2_ref,
    a_n3, a_cot, a_o2, a_n2, a_o1, a_mem, act_in, dfe_in, act_out, dfe_out,
    b_dc, b_e2, b_da, b_kv,
    dc_ref, da_ref, acc_ref, dn_ref, expand_sums, vec_ref,
    do2_ref, do1_ref, do2h_ref, do1h_ref, sums_ref, e2_ref, dkv_ref, e1_ref, dkt_ref, dvt_ref,
    grads_f, land_f1, land_f2, grads_c, land_c1, land_c2,
    piece_f, piece_c, weight_ref, weight_in, weight_sum, piece_q, vec_out, vec_in, piece_v,
    load_sems, ring_sems, keep_sems, pair_send, pair_recv, send_sems, recv_sems,
    dp_send, dp_recv, sum_send, sum_recv, eight_send, eight_recv, column_send, column_recv,
):
    place = Place()
    core, y, xl, me, dp = place.core, place.y, place.xl, place.seq, place.dp
    partner = 2 * y + 1 - xl
    own_rows = aligned(me, TOK)
    order = [lax.rem(y + step, 4) for step in (1, 2, 3, 0)]

    barrier = greet_row()
    for distance in range(1, DP):
        pl.semaphore_signal(
            barrier, inc=1, device_id=(lax.rem(dp + distance, DP), me), device_id_type=MESH
        )
    outer = place.neighbour("x", 2 * xl - 1)
    pl.semaphore_signal(barrier, inc=1, device_id=outer, device_id_type=MESH)

    def load(source, target, sem):
        copy = pltpu.make_async_copy(source, target, load_sems.at[sem])
        copy.start()
        return copy

    z, rank = place.z, place.rank
    rank_rows = aligned(rank, TOK)

    def chunk_of(step):
        return lax.rem(rank + 1 + step, 8)

    def ring_copies(step, slot):
        copies = []
        for block in range(2):
            span = aligned(chunk_of(step) + 8 * block, 256)
            to = pl.ds(pl.multiple_of(slot * FF_CHUNK + block * 256, 256), 256)
            at = slot * 4 + block * 2
            copies += [
                pltpu.make_async_copy(expand_hbm.at[:, span], ring_e.at[:, to], ring_sems.at[at]),
                pltpu.make_async_copy(
                    reduce_hbm.at[span, :], ring_r.at[to, :], ring_sems.at[at + 1]
                ),
            ]
        return copies

    loads = [
        load(o2_hbm, a_o2.at[z, core], 0), load(cross_hbm, cross_w, 1), load(x1_hbm, x1_ref, 2),
        load(cot_hbm, cot_ref, 3)
    ]
    gather = Gather(
        n1_hbm, lambda at: n1_all.at[aligned(at, TOK), :], keep_sems.at[0], send_sems, recv_sems, 64
    )
    gather_f = Gather(
        piece_f, lambda at: all_f.at[at], keep_sems.at[13], send_sems, recv_sems, 79
    )
    col_n3, col_o2, col_n2, col_o1 = (
        Column(
            block, lambda at, whole=whole: whole.at[at, core], None,
            column_send, column_recv, 4 * index,
        )
        for index, (block, whole) in enumerate(
            (
                (a_n3.at[z, core], a_n3), (o2_hbm, a_o2), (a_n2.at[z, core], a_n2),
                (a_o1.at[z, core], a_o1),
            )
        )
    )
    to_core = []

    def both_cores(whole):
        slot = len(to_core)
        copy = pltpu.make_async_remote_copy(
            src_ref=whole.at[:, core],
            dst_ref=whole.at[:, core],
            send_sem=pair_send.at[slot],
            recv_sem=pair_recv.at[slot],
            device_id=place.other,
            device_id_type=MESH,
        )
        copy.start()
        arrival = pltpu.make_async_remote_copy(
            src_ref=whole.at[:, 1 - core],
            dst_ref=whole.at[:, 1 - core],
            send_sem=pair_send.at[slot],
            recv_sem=pair_recv.at[slot],
            device_id=place.other,
            device_id_type=MESH,
        )
        to_core.append((copy, arrival))

    blocks_to_core = []

    def block_to_core(whole, step):
        slot = 7 + len(blocks_to_core)
        at = lax.rem(z + step + 4, 4)

        def copy(half):
            return pltpu.make_async_remote_copy(
                src_ref=whole.at[at, half],
                dst_ref=whole.at[at, half],
                send_sem=pair_send.at[slot],
                recv_sem=pair_recv.at[slot],
                device_id=place.other,
                device_id_type=MESH,
            )

        copy(core).start()
        blocks_to_core.append((copy(core), copy(1 - core)))

    give_act, give_dfe, give_dc, give_be2, give_kv, give_da, join_f, join_c = (
        Eight(place, eight_send, eight_recv, 8 * index) for index in range(8)
    )

    for one in loads[:3]:
        one.wait()
    for step in range(4):
        for one in ring_copies(step, step):
            one.start()
    x2 = x1_ref[...] + dot(a_o2[z, core], cross_w[...]) + bias_ref[8:9, :]
    unit3, inverse3 = norm_unit(x2)
    a_n3[z, core] = (unit3 * gain_ref[2:3, :] + bias_ref[2:3, :]).astype(LOW)
    acc_ref[...] = x2 + bias_ref[9:10, :]
    dn_ref[...] = jnp.zeros_like(dn_ref)
    loads[3].wait()
    pl.semaphore_wait(barrier, SEQ - 1 + DP - 1 + 1)
    gather.first()
    col_n3.first()
    root = math.sqrt(2.0 / math.pi)

    def feed(step, slot, own):
        for one in ring_copies(step, slot):
            one.wait()
        chunk = chunk_of(step)
        span = aligned(slot, FF_CHUNK)
        offset = jnp.concatenate(
            [ebias_ref[:, aligned(chunk + 8 * block, 256)] for block in range(2)], 1
        )
        hidden = dot(a_n3[z, core], ring_e[:, span]) + offset
        square = hidden * hidden
        curve = jnp.tanh(root * hidden * (1.0 + 0.044715 * square))
        share = 0.5 * (1.0 + curve)
        act = (hidden * share).astype(LOW)
        slope = share + 0.5 * hidden * (1.0 - curve * curve) * (
            root * (1.0 + 3.0 * 0.044715 * square)
        )
        acc_ref[...] += dot(act, ring_r[span, :])
        grad_act = dot_nt(cot_ref[...], ring_r[span, :])
        grad_hidden = (slope * grad_act).astype(LOW)
        if own:
            act_in[rank_rows, :] = act
            dfe_in[rank_rows, :] = grad_hidden
        else:
            act_out[step] = act
            dfe_out[step] = grad_hidden
            give_act.copy(act_out.at[step], act_in.at[rank_rows, :], step + 1).start()
            give_dfe.copy(dfe_out.at[step], dfe_in.at[rank_rows, :], step + 1).start()
        expand_sums[chunk] = column_sum(grad_hidden.astype(F32))
        dn_ref[...] += dot_nt(grad_hidden, ring_e[:, span])

    gathered = [
        (source.at[at], whole.at[at, core])
        for source, whole, steps in (
            (cot4_hbm, a_cot, (0, 1, 2, 3)), (mem4_hbm, a_mem, (0, 1, 2, 3)),
            (n24_hbm, a_n2, (-1, 0, 1)), (o14_hbm, a_o1, (-1, 0, 1)),
        )
        for at in [lax.rem(z + step + 4, 4) for step in steps]
    ]
    gathered = [
        pltpu.make_async_copy(source, target, load_sems.at[24 + index])
        for index, (source, target) in enumerate(gathered)
    ]

    def feed_step(step, carry):
        feed(step, lax.rem(step, 4), False)

        @pl.when(step < 4)
        def _():
            for one in ring_copies(step + 4, step):
                one.start()

        @pl.when(step == 2)
        def _():
            gather.second()

        @pl.when(step == 4)
        def _():
            col_n3.second()

        return carry

    lax.fori_loop(0, 7, feed_step, 0)
    feed(7, 3, True)
    give_act.last = (act_out.at[0], act_in.at[rank_rows, :])
    give_dfe.last = (dfe_out.at[0], dfe_in.at[rank_rows, :])
    col_o2.first()
    for one in gathered:
        one.start()
    kept = [
        load(memh_hbm, memh_ref, 9), load(cqh_hbm, cqh_ref, 10), load(mix2_hbm, mix2_ref, 11),
        load(inv2_hbm, inv2_ref, 12), load(exp2_hbm, exp_ref, 13),
    ]
    later = [
        load(query_hbm, ring_r.at[1024:2048, :], 14), load(out_hbm, ring_r.at[0:1024, :], 15),
        load(ckv_hbm, ring_e, 16),
    ]
    kept1 = [
        load(heads_hbm, heads_ref, 17), load(mix1_hbm, mix1_ref, 18), load(inv1_hbm, inv1_ref, 19),
        load(tok_hbm, tok_ref, 20),
    ]
    output_ref[...] = acc_ref[...].astype(LOW)
    dn3 = dn_ref[...]
    grad = cot_ref[...].astype(F32)
    dx2 = grad + norm_back(dn3, unit3, inverse3, gain_ref[2:3, :])
    acc_ref[...] = dx2
    dc_ref[...] = dx2.astype(LOW)

    give_do2, give_e2, give_k2, give_v2, give_do1, give_q1, give_k1, give_v1 = (
        Exchange(send_sems, recv_sems, 8 * index) for index in range(8)
    )

    def push_heads(exchange, low_ref, weight_of, values, target, keep_slot):
        for step in range(4):
            at = order[step]
            low_ref[:, aligned(at, 256)] = dot_nt(values, weight_of(aligned(at, 256))).astype(LOW)
            if step < 3:
                for half in range(2):
                    there = 2 * at + half
                    exchange.push(
                        low_ref.at[:, aligned(there, PAIR)], target.at[own_rows, :], there, False
                    )
            else:
                exchange.push(
                    low_ref.at[:, aligned(partner, PAIR)], target.at[own_rows, :], partner, False
                )
        keep = pltpu.make_async_copy(
            low_ref.at[:, aligned(me, PAIR)], target.at[own_rows, :], keep_sems.at[keep_slot]
        )
        keep.start()
        return keep

    keep_do2 = push_heads(
        give_do2, do2_ref, lambda rows: cross_w[rows, :], dc_ref[...], do2h_ref, 1
    )

    def share(exchange, source, target, width):
        exchange.push(lambda to: source.at[:, aligned(to, width)], target.at[rank_rows, :])
        target[rank_rows, :] = source[:, aligned(rank, width)]

    share(give_dc, dc_ref, b_dc, PAIR)
    vec_ref[2:3, :] = column_sum(dn3 * unit3)
    vec_ref[5:6, :] = column_sum(dn3)
    vec_ref[11:12, :] = column_sum(dc_ref[...].astype(F32))
    vec_ref[12:13, :] = column_sum(grad)

    def left_of(whole, group):
        return whole[:, :, :, aligned(group, 128)].reshape(ROW, 128)

    def rows_of(group, block):
        to = lax.rem(group, 4) * 2 + block
        return pl.ds(pl.multiple_of(to * 16, 16), 16)

    def fill_f(group, carry):
        result = dot_tn(left_of(a_n3, group), dfe_in[...]).astype(LOW)
        for block in range(2):
            for yy in range(4):
                at = (block * 4 + yy) * 16
                for col in range(2):
                    grads_f[(group // 4) * 2 + col, yy, rows_of(group, block), :] = result[
                        at : at + 16, col * LANES : col * LANES + LANES
                    ]
        return carry

    def fill_reduce():
        for xh in range(2):
            result = dot_tn(
                act_in[:, xh * 256 : xh * 256 + 256], a_cot[...].reshape(ROW, WIDTH)
            ).astype(LOW)
            for yy in range(4):
                for col in range(2):
                    for sub in range(2):
                        at = (col * 2 + sub) * LANES
                        grads_f[xh * 2 + col, yy, 128 + sub * 64 : 192 + sub * 64, :] = result[
                            yy * 64 : yy * 64 + 64, at : at + LANES
                        ]

    def fill_c():
        parts = ((a_n2, b_e2, 0, 0, PAIR), (a_o1, b_da, 0, PAIR, PAIR), (a_o2, b_dc, 0, 2 * PAIR, PAIR),
                 (a_mem, b_kv, 1, 0, 256))
        for whole, right, x_at, lane, width in parts:
            result = dot_tn(right[...], whole[...].reshape(ROW, WIDTH)).T.astype(LOW)
            for xh in range(2):
                for to in range(8):
                    for yy in range(4):
                        at = xh * 512 + to * 64 + yy * 16
                        grads_c[
                            xh * 2 + x_at, yy, to * 16 : to * 16 + 16, lane : lane + width
                        ] = result[at : at + 16, :]
        for xh in range(2):
            grads_c[xh * 2 + 1, :, :, 256:384] = jnp.zeros((4, 128, PAIR), LOW)

    sum_f = Sum(place, grads_f, (land_f1, land_f2), FLOWS_F, sum_send, sum_recv, 0)
    sum_c = Sum(place, grads_c, (land_c1, land_c2), FLOWS_C, sum_send, sum_recv, 24)
    run_f, run_c = sum_f.run(), sum_c.run_straight()

    def attend_back(query, key_rows, value_rows, grad_ref, mix_ref, inv_ref, causal, after_tile):
        tile = 256
        scaled = (grad_ref[...].astype(F32) * inv_ref[...]).astype(LOW)
        lanes = head_lanes(ROW)
        product = scaled.astype(F32) * mix_ref[...].astype(F32)
        inner = [jnp.sum(pick_head(product, lanes, head), -1, keepdims=True) for head in range(2)]
        value_t = value_rows.T
        query_t = query.T
        scaled_t = scaled.T
        dkt_ref[...] = jnp.zeros_like(dkt_ref)
        dvt_ref[...] = jnp.zeros_like(dvt_ref)
        tile_lanes = head_lanes(tile)
        steps = range(ROW // tile)
        for step in reversed(steps) if causal else steps:
            rows = slice(step * tile, step * tile + tile)
            width = (step + 1) * tile if causal else ROW
            parts = []
            for head in range(2):
                own = slice(head * HEAD_DIM, head * HEAD_DIM + HEAD_DIM)
                exponent = exp_ref[head, rows, 0:width]
                grad_p = dot(pick_head(scaled[rows, :], tile_lanes, head), value_t[:, 0:width])
                grad_s = (exponent.astype(F32) * (grad_p - inner[head][rows, :])).astype(LOW)
                parts.append(dot(grad_s, key_rows[0:width, :]))
                dkt_ref[own, 0:width] += dot(query_t[own, rows], grad_s)
                dvt_ref[own, 0:width] += dot(scaled_t[own, rows], exponent)
            grad_q = jnp.where(tile_lanes, parts[0], parts[1]).astype(LOW) * SCALE
            sums_ref[rows, 0:PAIR] = grad_q.astype(LOW)
            after_tile(step, rows)

    def send_part(exchange, part, there, target, column):
        exchange.push(
            sums_ref.at[there * TOK : there * TOK + TOK, part * PAIR : part * PAIR + PAIR],
            target.at[:, pl.ds(pl.multiple_of(column + me * PAIR, PAIR), PAIR)], there, True,
        )

    def keep_part(part, target, column, slot):
        copy = pltpu.make_async_copy(
            sums_ref.at[own_rows, part * PAIR : part * PAIR + PAIR],
            target.at[:, pl.ds(pl.multiple_of(column + me * PAIR, PAIR), PAIR)],
            keep_sems.at[slot],
        )
        copy.start()
        return copy

    def from_peers(target, column):
        return lambda sender: target.at[
            :, pl.ds(pl.multiple_of(column + sender * PAIR, PAIR), PAIR)
        ]

    def join(exchange, grads, piece, keep_slot, rest):
        block = grads.at[place.at["x"], place.at["y"]]
        mine = pl.ds(pl.multiple_of(rank * 16, 16), 16)
        exchange.push(
            lambda to: block.at[pl.ds(pl.multiple_of(to * 16, 16), 16), :], piece.at[mine, :]
        )
        keeps = [
            pltpu.make_async_copy(block.at[mine, :], piece.at[mine, :], keep_sems.at[keep_slot])
        ]
        if rest:
            keeps.append(
                pltpu.make_async_copy(
                    block.at[pl.ds(128, 128), :], piece.at[pl.ds(128, 128), :],
                    keep_sems.at[keep_slot + 1],
                )
            )
        for one in keeps:
            one.start()
        return keeps

    def joined(exchange, piece, keeps):
        for one in keeps:
            one.wait()
        exchange.receive(lambda to: piece.at[pl.ds(pl.multiple_of(to * 16, 16), 16), :])

    spreads = []

    def spread(piece, whole, base, slot):
        exchange = Exchange(send_sems, recv_sems, base)
        for distance in range(1, SEQ):
            exchange.push(piece, whole.at[me], lax.rem(me + distance, SEQ), False)
        keep = pltpu.make_async_copy(piece, whole.at[me], keep_sems.at[slot])
        keep.start()
        spreads.append((exchange, keep, whole))

    for one in kept:
        one.wait()
    keep_do2.wait()
    give_do2.receive(lambda sender: do2h_ref.at[aligned(sender, TOK), :])

    def after_cross(step, rows):
        for half in range(2):
            send_part(give_e2, 0, 2 * step + half, e2_ref, 0)

    attend_back(
        cqh_ref[...], memh_ref[:, 0:PAIR], memh_ref[:, PAIR : 2 * PAIR], do2h_ref, mix2_ref,
        inv2_ref, False, after_cross,
    )
    keeps = [keep_part(0, e2_ref, 0, 2)]
    sums_ref[:, PAIR : 2 * PAIR] = dkt_ref[...].T.astype(LOW)
    sums_ref[:, 2 * PAIR : 3 * PAIR] = dvt_ref[...].T.astype(LOW)
    for there in range(SEQ):
        send_part(give_k2, 1, there, dkv_ref, 0)
        send_part(give_v2, 2, there, dkv_ref, WIDTH)
    keeps += [keep_part(1, dkv_ref, 0, 3), keep_part(2, dkv_ref, WIDTH, 4)]
    exp1_load = load(exp1_hbm, exp_ref, 21)

    keeps[0].wait()
    later[0].wait()
    unit2, inverse2 = norm_unit(x1_ref[...])
    give_e2.receive(from_peers(e2_ref, 0))
    dn2 = dot_nt(e2_ref[...], ring_r[1024:2048, :])
    dx1 = acc_ref[...] + norm_back(dn2, unit2, inverse2, gain_ref[1:2, :])
    acc_ref[...] = dx1
    da_ref[...] = dx1.astype(LOW)
    later[1].wait()
    keep_do1 = push_heads(
        give_do1, do1_ref, lambda rows: ring_r[rows, :], da_ref[...], do1h_ref, 5
    )
    gather.third()
    share(give_be2, e2_ref, b_e2, PAIR)
    share(give_da, da_ref, b_da, PAIR)
    col_n3.finish()
    both_cores(a_n3)
    for one in gathered:
        one.wait()
    both_cores(a_cot)
    both_cores(a_mem)
    for whole in (a_n2, a_o1):
        for step in (-1, 0, 1):
            block_to_core(whole, step)
    vec_ref[1:2, :] = column_sum(dn2 * unit2)
    vec_ref[4:5, :] = column_sum(dn2)
    vec_ref[8:9, :] = column_sum(da_ref[...].astype(F32))
    vec_ref[9:10, :] = column_sum(e2_ref[...].astype(F32))
    keeps[1].wait()
    keeps[2].wait()
    give_k2.receive(from_peers(dkv_ref, 0))
    give_v2.receive(from_peers(dkv_ref, WIDTH))
    share(give_kv, dkv_ref, b_kv, 256)
    later[2].wait()
    gmem_ref[...] = dot_nt(dkv_ref[...], ring_e[...])
    vec_ref[10:11, :] = column_sum(dkv_ref[:, WIDTH : 2 * WIDTH].astype(F32))
    last = [
        load(qkv_hbm.at[:, 0 : 2 * WIDTH], ring_e, 22),
        load(qkv_hbm.at[:, 2 * WIDTH : 3 * WIDTH], ring_r.at[0:1024, :], 23),
    ]

    for index in (0, 1):
        to_core[index][1].wait_recv()
    give_act.receive(lambda to: act_in.at[aligned(to, TOK), :])
    give_dfe.receive(lambda to: dfe_in.at[aligned(to, TOK), :])
    lax.fori_loop(0, 8, fill_f, 0)
    fill_reduce()
    next(run_f)
    col_o2.second()
    col_n2.forward()
    col_o1.forward()

    for exchange in (give_e2, give_k2, give_v2):
        exchange.drain()
    for one in kept1:
        one.wait()
    exp1_load.wait()
    keep_do1.wait()
    give_do1.receive(lambda sender: do1h_ref.at[aligned(sender, TOK), :])

    def after_self(step, rows):
        sums_ref[rows, PAIR : 2 * PAIR] = dkt_ref[:, rows].T.astype(LOW)
        sums_ref[rows, 2 * PAIR : 3 * PAIR] = dvt_ref[:, rows].T.astype(LOW)
        for half in range(2):
            for part, exchange in enumerate((give_q1, give_k1, give_v1)):
                send_part(exchange, part, 2 * step + half, e1_ref, part * WIDTH)

    attend_back(
        heads_ref[:, 0:PAIR], heads_ref[:, PAIR : 2 * PAIR], heads_ref[:, 2 * PAIR : 3 * PAIR],
        do1h_ref, mix1_ref, inv1_ref, True, after_self,
    )
    keeps = [keep_part(part, e1_ref, part * WIDTH, 6 + part) for part in range(3)]
    next(run_f)


    gather.finish()
    for part in range(3):
        value = sums_ref[:, part * PAIR : part * PAIR + PAIR].T
        weight_ref[:, :, :, part * PAIR : part * PAIR + PAIR] = (
            dot(value, n1_all[...]).T.astype(LOW).reshape(DP // 2, 2, ROW // DP, PAIR)
        )
    both_sums = pltpu.make_async_remote_copy(
        src_ref=weight_ref.at[:, 1 - core],
        dst_ref=weight_in.at[0],
        send_sem=pair_send.at[6],
        recv_sem=pair_recv.at[6],
        device_id=place.other,
        device_id_type=MESH,
    )
    both_sums.start()
    pair = dp // 2

    def pair_copy(source, target, distance):
        there = lax.rem(pair + distance + 8, 8)
        return pltpu.make_async_remote_copy(
            src_ref=source.at[there],
            dst_ref=target.at[1, pair],
            send_sem=dp_send.at[distance],
            recv_sem=dp_recv.at[distance],
            device_id=(there * 2 + core, me),
            device_id_type=MESH,
        )

    def pair_receive(target, distance):
        sender = lax.rem(pair - distance + 8, 8)
        return pltpu.make_async_remote_copy(
            src_ref=target.at[1, sender],
            dst_ref=target.at[1, sender],
            send_sem=dp_send.at[distance],
            recv_sem=dp_recv.at[distance],
            device_id=(sender * 2 + core, me),
            device_id_type=MESH,
        )

    def dp_copy(source, target, distance, base):
        there = lax.rem(dp + distance, DP)
        return pltpu.make_async_remote_copy(
            src_ref=source.at[there],
            dst_ref=target.at[dp],
            send_sem=dp_send.at[base + distance],
            recv_sem=dp_recv.at[base + distance],
            device_id=(there, me),
            device_id_type=MESH,
        )

    def dp_receive(target, distance, base):
        sender = lax.rem(dp - distance + DP, DP)
        return pltpu.make_async_remote_copy(
            src_ref=target.at[sender],
            dst_ref=target.at[sender],
            send_sem=dp_send.at[base + distance],
            recv_sem=dp_recv.at[base + distance],
            device_id=(sender, me),
            device_id_type=MESH,
        )

    both_sums.wait()
    weight_sum[...] = (
        weight_ref[:, core].astype(F32) + weight_in[0].astype(F32)
    ).astype(LOW)
    for one in keeps:
        one.wait()
    give_q1.receive(from_peers(e1_ref, 0))
    give_k1.receive(from_peers(e1_ref, WIDTH))
    next(run_f)
    for step in (-1, 0, 1):
        block_to_core(a_o2, step)
    for column, whole in ((col_o2, a_o2), (col_n2, a_n2), (col_o1, a_o1)):
        column.far()
        block_to_core(whole, 2)
    for distance in range(1, 8):
        pair_copy(weight_sum, weight_in, distance).start()

    for one in last:
        one.wait()
    unit1, inverse1 = norm_unit(tok_ref[...].astype(F32))
    dn1 = dot_nt(e1_ref[:, 0 : 2 * WIDTH], ring_e[...])
    give_v1.receive(from_peers(e1_ref, 2 * WIDTH))
    dn1 = dn1 + dot_nt(e1_ref[:, 2 * WIDTH : 3 * WIDTH], ring_r[0:1024, :])
    gtok_ref[...] = acc_ref[...] + norm_back(dn1, unit1, inverse1, gain_ref[0:1, :])
    vec_ref[0:1, :] = column_sum(dn1 * unit1)
    vec_ref[3:4, :] = column_sum(dn1)
    vec_ref[6:7, :] = column_sum(e1_ref[:, 0:WIDTH].astype(F32))
    vec_ref[7:8, :] = column_sum(e1_ref[:, 2 * WIDTH : 3 * WIDTH].astype(F32))

    to_core[2][1].wait_recv()
    for _, arrival in blocks_to_core:
        arrival.wait_recv()
    for exchange, target in ((give_dc, b_dc), (give_be2, b_e2), (give_kv, b_kv), (give_da, b_da)):
        exchange.receive(lambda to, target=target: target.at[aligned(to, TOK), :])
    fill_c()
    next(run_c)

    vec_out[...] = jnp.zeros_like(vec_out)
    for owner in range(DP):
        vec_out[owner, 0:13, 0:64] = vec_ref[0:13, owner * 64 : owner * 64 + 64]
        for half in range(2):
            at = (owner // 8) * 256 + half * PAIR
            vec_out[owner, 13 + half : 14 + half, :] = expand_sums[owner % 8, :, at : at + PAIR]
    for distance in range(1, DP):
        dp_copy(vec_out, vec_in, distance, DP).start()

    next(run_f)
    keeps_f = join(join_f, grads_f, piece_f, 9, True)
    joined(join_f, piece_f, keeps_f)
    gather_f.first()
    next(run_c)
    gather_f.second()
    for distance in range(1, 8):
        pair_receive(weight_in, distance).wait_recv()
    total = weight_sum[pair].astype(F32)
    for distance in range(1, 8):
        total = total + weight_in[1, lax.rem(pair + distance, 8)].astype(F32)
    piece_q[...] = total.astype(LOW)
    next(run_c)
    keeps_c = join(join_c, grads_c, piece_c, 11, False)
    spread(piece_q, all_q, 70, 12)
    gather_f.third()
    for distance in range(1, DP):
        dp_receive(vec_in, distance, DP).wait_recv()
    total = vec_out[dp]
    for distance in range(1, DP):
        total = total + vec_in[lax.rem(dp + distance, DP)]
    piece_v[...] = total
    spread(piece_v, all_v, 86, 14)
    joined(join_c, piece_c, keeps_c)
    spread(piece_c, all_c, 94, 15)
    gather_f.finish()

    for exchange, keep, whole in spreads:
        keep.wait()
        exchange.receive(lambda sender, whole=whole: whole.at[sender])
        exchange.drain()
    for exchange in (give_do2, give_do1, give_q1, give_k1, give_v1):
        exchange.drain()
    for copy, _ in to_core + blocks_to_core:
        copy.wait_send()
    col_o2.sent_near()
    for exchange in (give_act, give_dfe, give_dc, give_be2, give_kv, give_da, join_f, join_c):
        exchange.drain()
    for distance in range(1, DP):
        dp_copy(vec_out, vec_in, distance, DP).wait_send()
    for distance in range(1, 8):
        pair_copy(weight_sum, weight_in, distance).wait_send()
    sum_f.drain()
    sum_c.drain()


def back_call(operands):
    dma = pltpu.SemaphoreType.DMA
    vmem = pltpu.VMEM
    token = vmem((TOK, WIDTH), LOW)
    token_wide = vmem((TOK, WIDTH), F32)
    heads = vmem((ROW, PAIR), LOW)
    inverse = vmem((ROW, PAIR), F32)
    eight = vmem((4, 2, TOK, WIDTH), LOW)
    column = vmem((ROW, PAIR), LOW)
    chunk = vmem((ROW, FF_CHUNK), LOW)
    chunks = vmem((7, TOK, FF_CHUNK), LOW)

    def sums(rows, lanes):
        return [
            vmem((4, 4, rows, lanes), LOW), vmem((3, 4, rows, lanes), LOW),
            vmem((3, rows, lanes), LOW),
        ]

    return pl.pallas_call(
        back_kernel,
        out_shape=(
            shaped((TOK, WIDTH)), shaped((TOK, WIDTH), F32), shaped((TOK, WIDTH), F32),
            shaped((SEQ, 256, LANES)), shaped((SEQ, 128, 384)),
            shaped((SEQ, 64, 3 * PAIR)), shaped((SEQ, 16, PAIR), F32),
        ),
        in_specs=[spec_vmem()] * 3 + [spec_any()] * 25,
        out_specs=(spec_vmem(),) * 4 + (spec_any(),) * 3,
        scratch_shapes=[
            vmem((ROW, WIDTH), LOW),
            vmem((WIDTH, 2 * WIDTH), LOW), vmem((2 * WIDTH, WIDTH), LOW), vmem((WIDTH, WIDTH), LOW),
            vmem((2, ROW, ROW), LOW), token_wide, token, token,
            vmem((ROW, 3 * PAIR), LOW), vmem((ROW, 2 * PAIR), LOW), heads, heads, heads, inverse,
            inverse,
            eight, eight, eight, eight, eight, eight, chunk, chunk, chunks, chunks,
            column, column, column, vmem((ROW, 256), LOW),
            token, token, token_wide, token_wide,
            vmem((FF // FF_CHUNK, 1, FF_CHUNK), F32), vmem((16, WIDTH), F32),
            token, token, heads, heads, vmem((ROW, 3 * PAIR), LOW), token,
            vmem((TOK, 2 * WIDTH), LOW), vmem((TOK, 3 * WIDTH), LOW),
            vmem((PAIR, ROW), F32), vmem((PAIR, ROW), F32),
        ]
        + sums(256, LANES) + sums(128, 384)
        + [
            vmem((256, LANES), LOW), vmem((128, 384), LOW),
            vmem((8, 2, 64, 3 * PAIR), LOW), vmem((2, 8, 64, 3 * PAIR), LOW),
            vmem((8, 64, 3 * PAIR), LOW),
            vmem((64, 3 * PAIR), LOW), vmem((DP, 16, PAIR), F32), vmem((DP, 16, PAIR), F32),
            vmem((16, PAIR), F32),
            dma((38,)), dma((16,)), dma((16,)), dma((19,)), dma((19,)), dma((102,)), dma((102,)),
            dma((32,)), dma((32,)), dma((48,)), dma((48,)), dma((64,)), dma((64,)), dma((16,)),
            dma((16,)),
        ],
        compiler_params=pltpu.CompilerParams(
            collective_id=3, has_side_effects=True, vmem_limit_bytes=63 * MIB
        ),
        cost_estimate=pl.CostEstimate(
            flops=2 * TOK * WIDTH * 27 * WIDTH, bytes_accessed=100 * MIB, transcendentals=0
        ),
        name="back",
    )(*operands)


def finish_kernel(
    f_hbm, c_hbm, q_hbm, vec_hbm, output_hbm, gtok_hbm, gmem_hbm,
    gqkv_ref, gout_ref, gque_ref, gckv_ref, gcro_ref, gexp_ref, gred_ref, ggain_ref, gbias_ref,
    gebias_ref, to_output, to_gtok, to_gmem,
    f_ref, c_ref, q_ref, vec_ref, sems,
):
    copies = [
        pltpu.make_async_copy(source, target, sems.at[index])
        for index, (source, target) in enumerate(
            (
                (f_hbm, f_ref), (c_hbm, c_ref), (q_hbm, q_ref), (vec_hbm, vec_ref),
                (output_hbm, to_output), (gtok_hbm, to_gtok), (gmem_hbm, to_gmem),
            )
        )
    ]
    for one in copies:
        one.start()
    for one in copies[:4]:
        one.wait()
    for seq in range(SEQ):
        y, xl = seq // 2, seq % 2
        rows = slice(16 * y, 16 * y + 16)
        for owner in range(8):
            own = slice(owner * 16, owner * 16 + 16)
            at = (owner + 8 * xl) * 256
            gexp_ref[rows, at : at + 256] = f_ref[seq, own, :].astype(F32)
            if xl == 0:
                for index, target in enumerate((gque_ref, gout_ref, gcro_ref)):
                    target[rows, owner * PAIR : owner * PAIR + PAIR] = c_ref[
                        seq, own, index * PAIR : index * PAIR + PAIR
                    ].astype(F32)
            else:
                gckv_ref[rows, owner * 256 : owner * 256 + 256] = c_ref[seq, own, 0:256].astype(F32)
        for sub in range(2):
            at = xl * 512 + sub * LANES
            gred_ref[64 * y : 64 * y + 64, at : at + LANES] = f_ref[
                seq, 128 + sub * 64 : 192 + sub * 64, :
            ].astype(F32)
        for part in range(3):
            at = part * WIDTH + seq * PAIR
            gqkv_ref[:, at : at + PAIR] = q_ref[seq, :, part * PAIR : (part + 1) * PAIR].astype(F32)
    total = vec_ref[0]
    for seq in range(1, SEQ):
        total = total + vec_ref[seq]
    ggain_ref[...] = total[0:3, 0:64]
    gbias_ref[...] = total[3:13, 0:64]
    gebias_ref[:, 0:PAIR] = total[13:14, :]
    gebias_ref[:, PAIR : 2 * PAIR] = total[14:15, :]
    for one in copies[4:]:
        one.wait()


def finish_call(operands):
    vmem = pltpu.VMEM
    return pl.pallas_call(
        finish_kernel,
        out_shape=(
            shaped((64, 3 * WIDTH), F32), shaped((64, WIDTH), F32), shaped((64, WIDTH), F32),
            shaped((64, 2 * WIDTH), F32), shaped((64, WIDTH), F32), shaped((64, FF), F32),
            shaped((256, WIDTH), F32), shaped((3, 64), F32), shaped((10, 64), F32),
            shaped((1, 256), F32), shaped((TOK, WIDTH)), shaped((TOK, WIDTH), F32),
            shaped((TOK, WIDTH), F32),
        ),
        in_specs=[spec_any()] * 7,
        out_specs=(spec_vmem(),) * 13,
        scratch_shapes=[
            vmem((SEQ, 256, LANES), LOW), vmem((SEQ, 128, 384), LOW), vmem((SEQ, 64, 3 * PAIR), LOW),
            vmem((SEQ, 16, PAIR), F32), pltpu.SemaphoreType.DMA((8,)),
        ],
        compiler_params=pltpu.CompilerParams(vmem_limit_bytes=63 * MIB),
        cost_estimate=pl.CostEstimate(flops=0, bytes_accessed=10 * MIB, transcendentals=0),
        name="finish",
    )(*operands)


def on_device(
    tokens, memory, cotangent, offsets, memory_ids, pair_map, self_qkv, self_out, cross_query,
    cross_kv, cross_out, expand_weight, expand_bias, reduce_weight, norm_gains, bias_rows,
):
    tok = tokens.reshape(TOK, WIDTH)
    mem = memory.reshape(TOK, WIDTH)
    cot = cotangent.reshape(TOK, WIDTH)
    (
        o2, mix2, inv2, x1, heads, mem_heads, cq, mix1, inv1, n1, exp1, exp2, cot4, mem4, n24, o14,
    ) = front_call(
        (tok, mem, cot, norm_gains, bias_rows, memory_ids, offsets, pair_map, self_qkv, cross_kv,
         self_out, cross_query)
    )
    output, gtok, gmem, all_f, all_c, all_q, all_v = back_call(
        (norm_gains, bias_rows, expand_bias.reshape(1, FF),
         o2, x1, cot, tok, n1, cot4, mem4, n24, o14, heads, mem_heads, cq, mix1, mix2, inv1, inv2,
         exp1, exp2, self_qkv, cross_kv, self_out, cross_query, cross_out, expand_weight,
         reduce_weight)
    )
    (
        gqkv, gout, gque, gckv, gcro, gexp, gred, ggain, gbias, gebias, output, gtok, gmem,
    ) = finish_call((all_f, all_c, all_q, all_v, output, gtok, gmem))
    return (
        output.reshape(1, TOK, WIDTH), gtok.reshape(1, TOK, WIDTH), gmem.reshape(1, TOK, WIDTH),
        gqkv, gout, gque, gckv, gcro, gexp, gebias.reshape(256), gred, ggain, gbias,
    )


def solution(mesh):
    row = P("dp", "seq", None)
    split = P("dp", None)
    in_specs = (row,) * 3 + (split,) * 3 + (P(),) * 10
    out_specs = (row,) * 3 + (split,) * 6 + (P("dp"), split, P(None, "dp"), P(None, "dp"))
    return jax.shard_map(
        on_device, mesh=mesh, in_specs=in_specs, out_specs=out_specs, check_vma=False
    )
```
